128 devices in a mesh: band: 8 (over z, core), sector: 16 (over y, x).
Axes of the slice: x: 4, y: 4, z: 4, core: 2. Of those that a mesh axis runs over, the one named last changes fastest.
Arguments:
- field: float32 [2, 640, 2, 2560], P(None, 'band', None, 'sector'), may hold values from -6 to 6
- depart: int32 [2, 640, 80], P(None, 'band', 'sector'), may hold values from -2 to 2
- interp_weight: bfloat16 [2, 640, 80, 64, 32], P(None, 'band', 'sector'), may hold values from -0.75 to 0.75
- legendre: float32 [640, 640, 1281], P('sector', 'band'), may hold values from -0.25 to 0.25
- damping: float32 [2], replicated, may hold values from 0.3 to 30
Outputs:
- new_field: float32 [2, 640, 2, 2560], P(None, 'band', None, 'sector')
The draws below stay inside these ranges and needn't reach their ends.
All inputs are finite; a program needn't handle non-finite values.
Results may differ from the reference program's by a relative error of at most 0.0003.
Values sent between devices are 32-bit elements; how exact they have to be, the bound alone decides.
A program may use at most 192 MiB of HBM per device.

```python
import math
import jax
import jax.numpy as jnp
from jax import lax

NLON = 2560
M = 1280
TILE = 32
LEV = 2
NH = 640
MPAIR = 640


def set_ends(values, rng, least, high):
    place = [jax.random.randint(jax.random.fold_in(rng, axis), (), 0, length) for axis, length in enumerate(values.shape)]
    widest = values.shape.index(max(values.shape))
    next_to = place[:widest] + [(place[widest] + 1) % values.shape[widest]] + place[widest + 1:]
    return values.at[tuple(place)].set(least).at[tuple(next_to)].set(high)


def steps_of(key, shape, cuts, smallest, largest):
    level = 1.0
    for dim, parts in cuts:
        steps = jax.random.uniform(jax.random.fold_in(jax.random.fold_in(key, 6), dim), (parts,), jnp.float32, smallest / len(cuts), largest / len(cuts))
        level = level * jnp.repeat(jnp.exp(steps), shape[dim] // parts).reshape((-1,) + (1,) * (len(shape) - 1 - dim))
    return level


def normal_values(rng, dims, scale, most, cuts=(), kind=jnp.bfloat16):
    level = steps_of(rng, dims, cuts, -0.22, 0.18) if cuts else 1.0
    entries = jax.random.normal(rng, dims, jnp.float32) * scale * level
    return jnp.minimum(jnp.maximum(entries, -most), most).astype(kind)


def setup_inputs(seed: int = 0) -> dict:
    streams_of = jax.random.split(jax.random.key(seed), 6)
    field = normal_values(streams_of[0], (2, NH, LEV, NLON), 1.0, 6.0, ((1, 8), (3, 16)), jnp.float32)
    depart = set_ends(jax.random.randint(streams_of[1], (2, NH, NLON // TILE), -2, 3), jax.random.fold_in(streams_of[1], 1), -2, 2).astype(jnp.int32)
    interp_weight = normal_values(streams_of[2], (2, NH, NLON // TILE, 2 * TILE, TILE), (2 * TILE) ** -0.5, 0.75, ((1, 8), (2, 16)))
    legendre = normal_values(streams_of[3], (MPAIR, NH, M + 1), NH ** -0.5, 0.25, ((0, 16), (1, 8)), jnp.float32)
    damping = jnp.clip(jnp.exp(jax.random.uniform(streams_of[4], (LEV,), jnp.float32, math.log(0.3), math.log(30.0))), 0.3, 30.0)
    return {"field": field, "depart": depart, "interp_weight": interp_weight, "legendre": legendre, "damping": damping}


HIGHEST = lax.Precision.HIGHEST


def pair_masks(pair_index, m_count, row_count):
    column = jnp.arange(row_count, dtype=jnp.int32)[None, :]
    limit = (m_count - pair_index)[:, None]
    leading = column < limit
    lag_value = jnp.where(leading, column, column - limit)
    odd_rows = (lag_value % 2) == 1
    degree = jnp.where(leading, pair_index[:, None] + column, column - 1)
    return leading, odd_rows, degree


def analyse(wave, legendre, leading, odd_rows):
    stacked = jnp.stack([wave[0] + wave[1], wave[0] - wave[1]])
    product = jnp.einsum('svcpl,plk->svcpk', stacked, legendre, precision=HIGHEST)
    chosen = jnp.where(odd_rows, product[1], product[0])
    return jnp.where(leading, chosen[:, 0:2], chosen[:, 2:4])


def solve_modes(spectrum, damping_levels, degree, m_count):
    ratio = (degree * (degree + 1)).astype(jnp.float32) / float(m_count * m_count)
    return spectrum / (1.0 + damping_levels[:, None, None, None] * ratio[None, None])


def synthesise(spectrum, legendre, leading, odd_rows):
    lower = jnp.where(leading, spectrum, 0.0)
    upper = jnp.where(leading, 0.0, spectrum)
    northern = jnp.concatenate([lower, upper], axis=1)
    southern = jnp.where(odd_rows, -northern, northern)
    stacked = jnp.stack([northern, southern])
    return jnp.einsum('hvcpk,plk->hvcpl', stacked, legendre, precision=HIGHEST)


def reference(field, depart, interp_weight, legendre, damping):
    hemis, lat_count, level_count, lon_count = field.shape
    tile_width = interp_weight.shape[-1]
    tile_count = lon_count // tile_width
    pieces = field.reshape(hemis, lat_count, level_count, tile_count, tile_width)
    lead_tile = (jnp.arange(tile_count, dtype=jnp.int32)[None, None, :] + depart) % tile_count
    next_tile = (lead_tile + 1) % tile_count
    full_shape = (hemis, lat_count, level_count, tile_count, tile_width)
    lead_part = jnp.take_along_axis(pieces, jnp.broadcast_to(lead_tile[:, :, None, :, None], full_shape), axis=3)
    next_part = jnp.take_along_axis(pieces, jnp.broadcast_to(next_tile[:, :, None, :, None], full_shape), axis=3)
    window = jnp.concatenate([lead_part, next_part], axis=4)
    advected = jnp.einsum('hlvtj,hltji->hlvti', window, interp_weight.astype(jnp.float32), precision=HIGHEST)
    advected = advected.reshape(hemis, lat_count, level_count, lon_count)
    row_count = legendre.shape[2]
    m_count = row_count - 1
    pair_total = m_count // 2
    spectral = jnp.fft.rfft(advected, axis=-1) / lon_count
    lower_waves = spectral[..., :pair_total]
    upper_waves = spectral[..., pair_total:m_count][..., ::-1]
    stacked = jnp.stack([jnp.real(lower_waves), jnp.imag(lower_waves), jnp.real(upper_waves), jnp.imag(upper_waves)], axis=3)
    wave = jnp.transpose(stacked, (0, 2, 3, 4, 1)).astype(jnp.float32)
    pair_index = jnp.arange(pair_total, dtype=jnp.int32)
    leading, odd_rows, degree = pair_masks(pair_index, m_count, row_count)
    spectrum = analyse(wave, legendre, leading, odd_rows)
    solved = solve_modes(spectrum, damping, degree, m_count)
    synthesis = synthesise(solved, legendre, leading, odd_rows)
    lower_coef = synthesis[:, :, 0] + 1j * synthesis[:, :, 1]
    upper_coef = synthesis[:, :, 2] + 1j * synthesis[:, :, 3]
    padding = jnp.zeros((hemis, level_count, lon_count // 2 + 1 - m_count, lat_count), lower_coef.dtype)
    coefficients = jnp.concatenate([lower_coef, upper_coef[:, :, ::-1], padding], axis=2)
    coefficients = jnp.transpose(coefficients, (0, 3, 1, 2))
    return jnp.fft.irfft(coefficients, n=lon_count, axis=-1) * lon_count
```

```python
import math

import jax
import jax.numpy as jnp
import ml_dtypes
import numpy as np
from jax import lax
from jax.experimental import pallas as pl
from jax.experimental.pallas import tpu as pltpu
from jax.sharding import PartitionSpec as P

F32 = jnp.float32
BF16 = jnp.bfloat16
LON = 2560
WAVES = 1280
ROWS = WAVES + 1
TILE = 32
LANES = 128
LAT = 80
BLOCK = 40
SHARE = 5
TILES = 5


def halves(table):
    high = table.astype(ml_dtypes.bfloat16)
    low = (table - high.astype(np.float64)).astype(ml_dtypes.bfloat16)
    return high, low


def tables():
    cls = np.arange(4)[:, None, None]
    d = np.arange(16)[None, :, None]
    j = np.arange(10)[None, None, :]
    lower = BLOCK * d + 4 * j + cls
    upper = WAVES - 4 - BLOCK * d - 4 * j + cls
    m = np.stack([lower, upper], axis=2)
    xi = np.arange(640)
    angle = 2.0 * math.pi / LON * ((m[..., None] * xi) % LON)
    cos, sin = np.cos(angle), np.sin(angle)
    sign = np.where(np.arange(4) == 3, -1.0, 1.0)[:, None, None, None, None]
    real = np.concatenate([cos, sin * sign], axis=-1)
    imag = np.concatenate([-sin, cos * sign], axis=-1)
    forward = np.stack([real, imag], axis=4).reshape(4, 640, 1280) / LON
    scale = np.where(m == 0, 1.0, 2.0)[..., None]
    cos, sin = cos * scale, sin * scale
    real = np.stack([cos, -sin], axis=4).reshape(4, 640, 640)
    imag = np.stack([sin, cos], axis=4).reshape(4, 640, 640)
    both = np.stack([real, imag], axis=1)
    both = both.reshape(4, 2, 640, 4, 160).transpose(0, 3, 1, 4, 2)
    inverse = both.reshape(4, 1280, 640)
    return forward, inverse


def split(value):
    high = value.astype(BF16)
    low = (value - high.astype(F32)).astype(BF16)
    return high, low


def dot(a, b):
    return jnp.dot(a, b, preferred_element_type=F32)


def dot_t(a, b):
    return lax.dot_general(a, b, (((1,), (1,)), ((), ())), preferred_element_type=F32)


def remote(src, dst, send, recv, device):
    return pltpu.make_async_remote_copy(
        src_ref=src,
        dst_ref=dst,
        send_sem=send,
        recv_sem=recv,
        device_id=device,
        device_id_type=pl.DeviceIdType.MESH,
    )


def kernel(
    field,
    depart,
    weight,
    legendre,
    damping,
    fwd_high,
    fwd_low,
    inv_high,
    inv_low,
    out,
    ext,
    wbuf,
    win,
    adv,
    r1,
    s2,
    r2,
    zc,
    fh,
    fl,
    ih,
    il,
    s3,
    r3,
    eo,
    lf,
    lb,
    legf,
    legh,
    legl,
    pbuf,
    cbuf,
    sbuf,
    tbuf,
    gbuf,
    syn,
    s4,
    r4,
    yc,
    s5,
    r5,
    o6,
    local_sem,
    w_sem,
    leg_sem,
    tab_sem,
    halo_s,
    halo_r,
    e1_s,
    e1_r,
    e2_s,
    e2_r,
    e3_s,
    e3_r,
    c1_s,
    c1_r,
    c2_s,
    c2_r,
    gz_s,
    gz_r,
    gp_s,
    gp_r,
    e4_s,
    e4_r,
    e5_s,
    e5_r,
    e6_s,
    e6_r,
):
    band = lax.axis_index("band")
    sec = lax.axis_index("sector")
    y, x = sec // 4, sec % 4
    z, core = band // 2, band % 2
    odd = x % 2 == 1

    own = pltpu.make_async_copy(field, ext.at[:, :, pl.ds(64, 160), :], local_sem)
    own.start()

    def w_copy(h, t):
        return pltpu.make_async_copy(weight.at[h, t], wbuf.at[h, t], w_sem.at[h, t])

    @pl.loop(0, TILES)
    def _(t):
        for h in range(2):
            w_copy(h, t).start()

    loads = [
        pltpu.make_async_copy(src.at[x], dst, tab_sem.at[i])
        for i, (src, dst) in enumerate(
            [(fwd_high, fh), (fwd_low, fl), (inv_high, ih), (inv_low, il)]
        )
    ]
    loads[0].start()
    loads[1].start()

    def leg_copy(q):
        rows = pl.ds(q * SHARE, SHARE)
        return pltpu.make_async_copy(legendre.at[rows], legf.at[rows], leg_sem.at[q])

    @pl.loop(0, 8)
    def _(q):
        leg_copy(q).start()

    loads[2].start()
    loads[3].start()

    barrier = pltpu.get_barrier_semaphore()

    def greet(device):
        pl.semaphore_signal(barrier, inc=1, device_id=device, device_id_type=pl.DeviceIdType.MESH)

    for k in range(1, 16):
        greet((band, (sec + k) % 16))
    for k in range(1, 4):
        greet((((z + k) % 4) * 2 + core, sec))
    greet((z * 2 + 1 - core, sec))
    pl.semaphore_wait(barrier, 19)

    right, left = (sec + 1) % 16, (sec + 15) % 16
    to_right = remote(
        field.at[:, :, pl.ds(96, 64), :],
        ext.at[:, :, pl.ds(0, 64), :],
        halo_s.at[0],
        halo_r.at[0],
        (band, right),
    )
    to_left = remote(
        field.at[:, :, pl.ds(0, 96), :],
        ext.at[:, :, pl.ds(224, 96), :],
        halo_s.at[1],
        halo_r.at[1],
        (band, left),
    )
    to_right.start()
    to_left.start()
    adv[...] = jnp.zeros_like(adv)

    @pl.when(jnp.logical_not(odd))
    def _():
        r2[1] = jnp.zeros_like(r2[1])

    own.wait()
    to_right.wait_recv()
    to_left.wait_recv()

    def e1(t, k):
        to = (y + k) % 4
        return remote(
            adv.at[to, t], r1.at[y, t], e1_s.at[t, k], e1_r.at[t, y], (band, to * 4 + x)
        )

    def e1_arrives(t, k):
        source = (y + k) % 4
        remote(
            adv.at[source, t],
            r1.at[source, t],
            e1_s.at[t, k],
            e1_r.at[t, source],
            (band, source * 4 + x),
        ).wait_recv()

    def e2(t, k, part):
        to = (x + k) % 4
        src = s2.at[3, t] if part else s2.at[to - 2 * (to // 3), t]
        return remote(
            src,
            r2.at[part, x, t],
            e2_s.at[part, t, k],
            e2_r.at[part, t, x],
            (band, y * 4 + to),
        )

    def e2_arrives(t, k, part):
        source = (x + k) % 4
        remote(
            s2.at[0, t],
            r2.at[part, source, t],
            e2_s.at[part, t, k],
            e2_r.at[part, t, source],
            (band, y * 4 + source),
        ).wait_recv()

    def advect(t):
        for h in range(2):
            w_copy(h, t).wait()
            dep = depart[t, h : h + 1, :]
            for v in range(2):
                window = ext[h, v, pl.ds(pl.multiple_of(t * TILE, TILE), 64), 0:LAT]
                for offset in range(-1, 3):
                    start = pl.multiple_of((t + offset + 2) * TILE, TILE)
                    candidate = ext[h, v, pl.ds(start, 64), 0:LAT]
                    window = jnp.where(dep == offset, candidate, window)
                win[v] = window
            total = [jnp.zeros((TILE, LAT), F32) for _ in range(2)]
            for j in range(64):
                w = wbuf[h, t, j].astype(F32)
                for v in range(2):
                    total[v] = total[v] + win[v, j : j + 1, :] * w
            for v in range(2):
                adv[h * 2 + v, t, :, 0:LAT] = total[v]
        for k in range(1, 4):
            e1(t, k).start()
        r1[y, t] = adv[y, t]

    def radix(t):
        for k in range(1, 4):
            e1_arrives(t, k)
        a, b, c, d = r1[0, t], r1[1, t], r1[2, t], r1[3, t]
        s2[0, t] = (a + c) + (b + d)
        s2[1, t] = a - c
        s2[2, t] = (a + c) - (b + d)
        s2[3, t] = d - b
        for k in range(1, 4):
            e2(t, k, 0).start()

            @pl.when((x + k) % 2 == 1)
            def _():
                e2(t, k, 1).start()

        r2[0, x, t] = s2[x - 2 * (x // 3), t]

        @pl.when(odd)
        def _():
            r2[1, x, t] = s2[3, t]

    @pl.loop(0, TILES + 1)
    def _(t):
        @pl.when(t < TILES)
        def _():
            advect(t)

        @pl.when(t > 0)
        def _():
            radix(t - 1)

    @pl.loop(0, TILES)
    def _(t):
        for k in range(1, 4):
            e2_arrives(t, k, 0)

            @pl.when(odd)
            def _():
                e2_arrives(t, k, 1)

    @pl.loop(0, 8)
    def _(i):
        part, source = i // 4, i % 4
        for t in range(TILES):
            high, low = split(r2[part, source, t])
            start = pl.multiple_of(i * 160 + t * TILE, TILE)
            zc[pl.ds(start, TILE), 0:LANES] = high
            zc[pl.ds(start, TILE), LANES : 2 * LANES] = low

    loads[0].wait()
    loads[1].wait()

    def e3(d):
        return remote(s3.at[d], r3.at[sec], e3_s.at[d], e3_r.at[sec], (band, d))

    @pl.loop(0, 4)
    def _(g):
        group = (g + sec // 4) % 4
        rows = pl.ds(pl.multiple_of(group * 160, 160), 160)
        both = dot(fh[rows, :], zc[...])
        value = both[:, 0:LANES] + both[:, LANES:] + dot(fl[rows, :], zc[:, 0:LANES])
        for q in range(4):
            d = group * 4 + q
            s3[d] = value[q * BLOCK : (q + 1) * BLOCK]

            @pl.when(d != sec)
            def _():
                e3(d).start()

            @pl.when(d == sec)
            def _():
                r3[d] = value[q * BLOCK : (q + 1) * BLOCK]

    @pl.loop(0, 8)
    def _(q):
        leg_copy(q).wait()

        @pl.loop(0, SHARE * TILES)
        def _(i):
            p = q * SHARE + i // 5
            rows = pl.ds(pl.multiple_of((i % 5) * 16, 16), 16)
            high, low = split(legf[p, rows, :])
            legh[p, rows, :] = high
            legl[p, rows, :] = low

    @pl.loop(1, 16)
    def _(k):
        source = (sec + k) % 16
        remote(
            s3.at[source], r3.at[source], e3_s.at[source], e3_r.at[source], (band, source)
        ).wait_recv()

    for v in range(2):
        for c in range(4):
            north, south = r3[v * 4 + c], r3[8 + v * 4 + c]
            eo[0, v, c] = north + south
            eo[1, v, c] = north - south
    for p in range(BLOCK):
        j, c = p // 4, p % 4
        for s in range(2):
            for v in range(2):
                row = s * 8 + v * 2
                lf[p, row : row + 2, :] = eo[s, v, c, 2 * j : 2 * j + 2, :]
                lf[p, row + 4 : row + 6, :] = eo[s, v, 3 - c, 20 + 2 * j : 22 + 2 * j, :]

    @pl.loop(0, BLOCK)
    def _(p):
        high, low = split(lf[p])
        lb[p, 0:16, :] = high
        lb[p, 16:32, :] = low

    column = lax.broadcasted_iota(jnp.int32, (8, ROWS), 1)

    def masks(p):
        limit = WAVES - (sec * BLOCK + p)
        leading = column < limit
        lag = jnp.where(leading, column, column - limit)
        return leading, (lag & 1) == 1

    def analyse(share, i):
        p = share * SHARE + i
        lhs = lb[p, :, 0:LAT]
        both = dot(lhs, legh[p])
        total = both[0:16] + both[16:32] + dot(lhs[0:16], legl[p])
        leading, odd_rows = masks(p)
        chosen = jnp.where(odd_rows, total[8:16], total[0:8])
        return jnp.where(leading[0:4], chosen[0:4], chosen[4:8])

    partner = (z * 2 + 1 - core, sec)

    def c1(to):
        return remote(pbuf.at[to], cbuf.at[to], c1_s.at[to], c1_r.at[to], partner)

    @pl.loop(0, 4)
    def _(k):
        to = (z + 1 + k) % 4

        @pl.loop(0, SHARE)
        def _(i):
            pbuf[to, i] = analyse(to * 2 + 1 - core, i)

        c1(to).start()

    def c2(to):
        return remote(sbuf.at[to], tbuf.at[z], c2_s.at[to], c2_r.at[z], (to * 2 + core, sec))

    @pl.loop(0, 4)
    def _(k):
        to = (z + 1 + k) % 4

        @pl.loop(0, SHARE)
        def _(i):
            sbuf[to, i] = analyse(to * 2 + core, i)

        c1(to).wait_recv()

        @pl.loop(0, SHARE)
        def _(i):
            sbuf[to, i] = sbuf[to, i] + cbuf[to, i]

        @pl.when(to != z)
        def _():
            c2(to).start()

    for k in range(1, 4):
        source = (z + k) % 4
        remote(
            sbuf.at[source],
            tbuf.at[source],
            c2_s.at[source],
            c2_r.at[source],
            (source * 2 + core, sec),
        ).wait_recv()

    tbuf[z] = sbuf[z]
    first_level = lax.broadcasted_iota(jnp.int32, (4, ROWS), 0) < 2
    level = jnp.where(first_level, damping[0], damping[1])

    @pl.loop(0, SHARE)
    def _(i):
        p = sec * BLOCK + band * SHARE + i
        column4 = column[0:4]
        degree = jnp.where(column4 < WAVES - p, p + column4, column4 - 1)
        ratio = (degree * (degree + 1)).astype(F32) / float(WAVES * WAVES)
        total = (tbuf[0, i] + tbuf[1, i]) + (tbuf[2, i] + tbuf[3, i])
        gbuf[band, i] = total / (1.0 + level * ratio)

    def gz(k):
        to = (z + k) % 4
        return remote(
            gbuf.at[band], gbuf.at[band], gz_s.at[k], gz_r.at[z], (to * 2 + core, sec)
        )

    def gz_arrives(source):
        share = source * 2 + core
        remote(
            gbuf.at[share], gbuf.at[share], gz_s.at[0], gz_r.at[source], (share, sec)
        ).wait_recv()

    def gp(source):
        share = source * 2 + core
        return remote(gbuf.at[share], gbuf.at[share], gp_s.at[source], gp_r.at[source], partner)

    def gp_arrives(source):
        share = source * 2 + 1 - core
        remote(
            gbuf.at[share], gbuf.at[share], gp_s.at[source], gp_r.at[source], partner
        ).wait_recv()

    for k in range(1, 4):
        gz(k).start()
    gp(z).start()

    def synthesise(share):
        @pl.loop(0, SHARE)
        def _(i):
            p = share * SHARE + i
            spec = gbuf[share, i]
            leading, odd_rows = masks(p)
            north = jnp.concatenate([spec, spec], axis=0)
            upper = lax.broadcasted_iota(jnp.int32, (8, ROWS), 0) >= 4
            north = jnp.where(leading != upper, north, 0.0)
            south = jnp.where(odd_rows, -north, north)
            high, low = split(jnp.concatenate([north, south], axis=0))
            both = dot_t(jnp.concatenate([high, low], axis=0), legh[p])
            syn[p, :, 0:LAT] = both[0:16] + both[16:32] + dot_t(high, legl[p])

    synthesise(band)
    gp_arrives(z)
    synthesise(z * 2 + 1 - core)

    @pl.loop(1, 4)
    def _(k):
        source = (z + k) % 4
        gz_arrives(source)
        gp(source).start()
        synthesise(source * 2 + core)

    @pl.loop(1, 4)
    def _(k):
        source = (z + k) % 4
        gp_arrives(source)
        synthesise(source * 2 + 1 - core)

    for p in range(BLOCK):
        j, c = p // 4, p % 4
        for h in range(2):
            for v in range(2):
                row = h * 8 + v * 2
                block = (h * 2 + v) * 4
                s4[block + c, 2 * j : 2 * j + 2, :] = syn[p, row : row + 2, :]
                s4[block + 3 - c, 20 + 2 * j : 22 + 2 * j, :] = syn[p, row + 4 : row + 6, :]

    def e4(k):
        to = (sec + k) % 16
        return remote(s4.at[to], r4.at[sec], e4_s.at[k], e4_r.at[sec], (band, to))

    @pl.loop(1, 16)
    def _(k):
        e4(k).start()

    r4[sec] = s4[sec]
    loads[2].wait()
    loads[3].wait()

    @pl.loop(1, 16)
    def _(k):
        source = (sec + k) % 16
        remote(
            s4.at[source], r4.at[source], e4_s.at[k], e4_r.at[source], (band, source)
        ).wait_recv()

    @pl.loop(0, 8)
    def _(i):
        pair = jnp.concatenate([r4[2 * i], r4[2 * i + 1]], axis=0)
        high, low = split(pair)
        start = pl.multiple_of(i * 80, 80)
        yc[pl.ds(start, 80), 0:LANES] = high
        yc[pl.ds(start, 80), LANES : 2 * LANES] = low

    def e5(k, part):
        to = (x + k) % 4
        return remote(
            s5.at[part, to],
            r5.at[part, x],
            e5_s.at[part, k],
            e5_r.at[part, x],
            (band, y * 4 + to),
        )

    def e5_arrives(k, part):
        source = (x + k) % 4
        remote(
            s5.at[part, source],
            r5.at[part, source],
            e5_s.at[part, k],
            e5_r.at[part, source],
            (band, y * 4 + source),
        ).wait_recv()

    @pl.loop(0, 4)
    def _(g):
        k = (g + 1) % 4
        to = (x + k) % 4

        def part_of(part):
            rows = pl.ds(pl.multiple_of((to * 2 + part) * 160, 160), 160)
            both = dot(ih[rows, :], yc[...])
            value = both[:, 0:LANES] + both[:, LANES:] + dot(il[rows, :], yc[:, 0:LANES])
            s5[part, to] = value

            @pl.when(k != 0)
            def _():
                e5(k, part).start()

            @pl.when(k == 0)
            def _():
                r5[part, to] = value

        part_of(0)

        @pl.when(odd)
        def _():
            part_of(1)

    for k in range(1, 4):
        e5_arrives(k, 0)

        @pl.when((x + k) % 2 == 1)
        def _():
            e5_arrives(k, 1)

    def e6(t, k):
        to = (y + k) % 4
        return remote(
            o6.at[to, t], out.at[y, t], e6_s.at[t, k], e6_r.at[t, y], (band, to * 4 + x)
        )

    @pl.loop(0, TILES)
    def _(t):
        rows = pl.ds(pl.multiple_of(t * TILE, TILE), TILE)
        a, c = r5[0, 0, rows, :], r5[0, 2, rows, :]
        b = r5[0, 1, rows, :] + r5[0, 3, rows, :]
        d = r5[1, 3, rows, :] - r5[1, 1, rows, :]
        o6[0, t] = (a + c) + b
        o6[1, t] = (a - c) + d
        o6[2, t] = (a + c) - b
        o6[3, t] = (a - c) - d
        for k in range(1, 4):
            e6(t, k).start()
        out[y, t] = o6[y, t]

    @pl.loop(0, TILES)
    def _(t):
        for k in range(1, 4):
            source = (y + k) % 4
            remote(
                o6.at[source, t],
                out.at[source, t],
                e6_s.at[t, k],
                e6_r.at[t, source],
                (band, source * 4 + x),
            ).wait_recv()

    to_right.wait_send()
    to_left.wait_send()

    @pl.loop(0, TILES)
    def _(t):
        for k in range(1, 4):
            e1(t, k).wait_send()
            e2(t, k, 0).wait_send()

            @pl.when((x + k) % 2 == 1)
            def _():
                e2(t, k, 1).wait_send()

            e6(t, k).wait_send()

    @pl.loop(1, 16)
    def _(k):
        e3((sec + k) % 16).wait_send()
        e4(k).wait_send()

    for k in range(4):
        c1((z + k) % 4).wait_send()
        gp(k).wait_send()
    for k in range(1, 4):
        c2((z + k) % 4).wait_send()
        gz(k).wait_send()
        e5(k, 0).wait_send()

        @pl.when(odd)
        def _():
            e5(k, 1).wait_send()


def local(field, depart, interp_weight, legendre, damping):
    moved = jnp.pad(jnp.transpose(field, (0, 2, 3, 1)), ((0, 0),) * 3 + ((0, LANES - LAT),))
    forward, inverse = tables()
    constants = [jnp.asarray(t) for t in (*halves(forward), *halves(inverse))]
    vmem = pl.BlockSpec(memory_space=pltpu.VMEM)
    hbm = pl.BlockSpec(memory_space=pl.ANY)
    scratch = [
        pltpu.VMEM((2, 2, 320, LANES), F32),
        pltpu.VMEM((2, 5, 64, TILE, LAT), BF16),
        pltpu.VMEM((2, 64, LAT), F32),
        pltpu.VMEM((4, 5, TILE, LANES), F32),
        pltpu.VMEM((4, 5, TILE, LANES), F32),
        pltpu.VMEM((4, 5, TILE, LANES), F32),
        pltpu.VMEM((2, 4, 5, TILE, LANES), F32),
        pltpu.VMEM((1280, 2 * LANES), BF16),
        pltpu.VMEM((640, 1280), BF16),
        pltpu.VMEM((640, 1280), BF16),
        pltpu.VMEM((1280, 640), BF16),
        pltpu.VMEM((1280, 640), BF16),
        pltpu.VMEM((16, BLOCK, LANES), F32),
        pltpu.VMEM((16, BLOCK, LANES), F32),
        pltpu.VMEM((2, 2, 4, BLOCK, LANES), F32),
        pltpu.VMEM((BLOCK, 16, LANES), F32),
        pltpu.VMEM((BLOCK, 32, LANES), BF16),
        pltpu.VMEM((BLOCK, LAT, ROWS), F32),
        pltpu.VMEM((BLOCK, LAT, ROWS), BF16),
        pltpu.VMEM((BLOCK, LAT, ROWS), BF16),
        pltpu.VMEM((4, SHARE, 4, ROWS), F32),
        pltpu.VMEM((4, SHARE, 4, ROWS), F32),
        pltpu.VMEM((4, SHARE, 4, ROWS), F32),
        pltpu.VMEM((4, SHARE, 4, ROWS), F32),
        pltpu.VMEM((8, SHARE, 4, ROWS), F32),
        pltpu.VMEM((BLOCK, 16, LANES), F32),
        pltpu.VMEM((16, BLOCK, LANES), F32),
        pltpu.VMEM((16, BLOCK, LANES), F32),
        pltpu.VMEM((640, 2 * LANES), BF16),
        pltpu.VMEM((2, 4, 160, LANES), F32),
        pltpu.VMEM((2, 4, 160, LANES), F32),
        pltpu.VMEM((4, 5, TILE, LANES), F32),
    ]
    dma = pltpu.SemaphoreType.DMA
    scratch += [
        dma,
        dma((2, 5)),
        dma((8,)),
        dma((4,)),
        dma((2,)),
        dma((2,)),
        dma((5, 4)),
        dma((5, 4)),
        dma((2, 5, 4)),
        dma((2, 5, 4)),
        dma((16,)),
        dma((16,)),
        dma((4,)),
        dma((4,)),
        dma((4,)),
        dma((4,)),
        dma((4,)),
        dma((4,)),
        dma((4,)),
        dma((4,)),
        dma((16,)),
        dma((16,)),
        dma((2, 4)),
        dma((2, 4)),
        dma((5, 4)),
        dma((5, 4)),
    ]
    grid = pl.pallas_call(
        kernel,
        out_shape=jax.ShapeDtypeStruct((4, 5, TILE, LANES), F32),
        in_specs=[vmem, vmem, hbm, hbm, pl.BlockSpec(memory_space=pltpu.SMEM)] + [hbm] * 4,
        out_specs=vmem,
        scratch_shapes=scratch,
        compiler_params=pltpu.CompilerParams(
            collective_id=0, has_side_effects=True, vmem_limit_bytes=62 * 1024 * 1024
        ),
    )(
        moved,
        jnp.transpose(depart, (2, 0, 1)),
        jnp.transpose(interp_weight, (0, 2, 3, 4, 1)),
        legendre,
        damping,
        *constants,
    )
    grid = grid.reshape(2, 2, 160, LANES)[..., 0:LAT]
    return jnp.transpose(grid, (0, 3, 1, 2))


def solution(mesh):
    placed = (
        P(None, "band", None, "sector"),
        P(None, "band", "sector"),
        P(None, "band", "sector", None, None),
        P("sector", "band", None),
        P(),
    )
    return jax.shard_map(
        local, mesh=mesh, in_specs=placed, out_specs=P(None, "band", None, "sector"), check_vma=False
    )
```

```python
import math

import jax
import jax.numpy as jnp
import ml_dtypes
import numpy as np
from jax import lax
from jax.experimental import pallas as pl
from jax.experimental.pallas import tpu as pltpu
from jax.sharding import PartitionSpec as P

F32 = jnp.float32
BF16 = jnp.bfloat16
LON = 2560
WAVES = 1280
ROWS = WAVES + 1
WIDE = WAVES + 128
TILE = 32
LANES = 128
LAT = 80
BLOCK = 40
SHARE = 5
TILES = 5


def halves(table):
    high = table.astype(ml_dtypes.bfloat16)
    low = (table - high.astype(np.float64)).astype(ml_dtypes.bfloat16)
    return high, low


def tables():
    cls = np.arange(4)[:, None, None]
    d = np.arange(16)[None, :, None]
    j = np.arange(10)[None, None, :]
    lower = BLOCK * d + 4 * j + cls
    upper = WAVES - 4 - BLOCK * d - 4 * j + cls
    m = np.stack([lower, upper], axis=2)
    xi = np.arange(640)
    angle = 2.0 * math.pi / LON * ((m[..., None] * xi) % LON)
    cos, sin = np.cos(angle), np.sin(angle)
    sign = np.where(np.arange(4) == 3, -1.0, 1.0)[:, None, None, None, None]
    real = np.concatenate([cos, sin * sign], axis=-1)
    imag = np.concatenate([-sin, cos * sign], axis=-1)
    forward = np.stack([real, imag], axis=4).reshape(4, 640, 1280) / LON
    scale = np.where(m == 0, 1.0, 2.0)[..., None]
    cos, sin = cos * scale, sin * scale
    real = np.stack([cos, -sin], axis=4).reshape(4, 640, 640)
    imag = np.stack([sin, cos], axis=4).reshape(4, 640, 640)
    both = np.stack([real, imag], axis=1)
    both = both.reshape(4, 2, 640, 4, 160).transpose(0, 3, 1, 4, 2)
    inverse = both.reshape(4, 1280, 640)
    return forward, inverse


def split(value):
    high = value.astype(BF16)
    low = (value - high.astype(F32)).astype(BF16)
    return high, low


def dot(a, b):
    return jnp.dot(a, b, preferred_element_type=F32)


def dot_t(a, b):
    return lax.dot_general(a, b, (((1,), (1,)), ((), ())), preferred_element_type=F32)


def remote(src, dst, send, recv, device):
    return pltpu.make_async_remote_copy(
        src_ref=src,
        dst_ref=dst,
        send_sem=send,
        recv_sem=recv,
        device_id=device,
        device_id_type=pl.DeviceIdType.MESH,
    )


def kernel(
    field,
    depart,
    weight,
    legendre,
    damping,
    fwd_high,
    fwd_low,
    inv_high,
    inv_low,
    out,
    ext,
    wbuf,
    win,
    adv,
    r1,
    s2,
    r2,
    zc,
    fh,
    fl,
    ih,
    il,
    s3,
    r3,
    eo,
    lf,
    lb,
    legf,
    legh,
    legl,
    pbuf,
    cbuf,
    sbuf,
    rbuf,
    tbuf,
    gbuf,
    syn,
    s4,
    r4,
    yc,
    s5,
    r5,
    o6,
    local_sem,
    w_sem,
    leg_sem,
    tab_sem,
    halo_s,
    halo_r,
    e1_s,
    e1_r,
    e2_s,
    e2_r,
    e3_s,
    e3_r,
    c1_s,
    c1_r,
    c2_s,
    c2_r,
    gz_s,
    gz_r,
    gp_s,
    gp_r,
    e4_s,
    e4_r,
    e5_s,
    e5_r,
    e6_s,
    e6_r,
):
    band = lax.axis_index("band")
    sec = lax.axis_index("sector")
    y, x = sec // 4, sec % 4
    z, core = band // 2, band % 2
    odd = x % 2 == 1

    own = pltpu.make_async_copy(field, ext.at[:, :, pl.ds(64, 160), :], local_sem)
    own.start()

    def w_copy(h, t):
        return pltpu.make_async_copy(weight.at[h, t], wbuf.at[h, t], w_sem.at[h, t])

    @pl.loop(0, TILES)
    def _(t):
        for h in range(2):
            w_copy(h, t).start()

    loads = [
        pltpu.make_async_copy(src.at[x], dst, tab_sem.at[i])
        for i, (src, dst) in enumerate(
            [(fwd_high, fh), (fwd_low, fl), (inv_high, ih), (inv_low, il)]
        )
    ]
    loads[0].start()
    loads[1].start()

    def leg_copy(q):
        rows = pl.ds(q * SHARE, SHARE)
        return pltpu.make_async_copy(legendre.at[rows], legf.at[rows], leg_sem.at[q])

    barrier = pltpu.get_barrier_semaphore()

    def greet(device):
        pl.semaphore_signal(barrier, inc=1, device_id=device, device_id_type=pl.DeviceIdType.MESH)

    for k in range(1, 16):
        greet((band, (sec + k) % 16))
    for k in range(1, 4):
        greet((((z + k) % 4) * 2 + core, sec))
    greet((z * 2 + 1 - core, sec))
    pl.semaphore_wait(barrier, 19)

    right, left = (sec + 1) % 16, (sec + 15) % 16
    to_right = remote(
        field.at[:, :, pl.ds(96, 64), :],
        ext.at[:, :, pl.ds(0, 64), :],
        halo_s.at[0],
        halo_r.at[0],
        (band, right),
    )
    to_left = remote(
        field.at[:, :, pl.ds(0, 96), :],
        ext.at[:, :, pl.ds(224, 96), :],
        halo_s.at[1],
        halo_r.at[1],
        (band, left),
    )
    to_right.start()
    to_left.start()
    adv[...] = jnp.zeros_like(adv)

    @pl.when(jnp.logical_not(odd))
    def _():
        r2[1] = jnp.zeros_like(r2[1])

    own.wait()
    to_right.wait_recv()
    to_left.wait_recv()

    @pl.loop(0, 8)
    def _(q):
        leg_copy(q).start(priority=1)


    def e1(t, k):
        to = (y + k) % 4
        return remote(
            adv.at[to, t], r1.at[y, t], e1_s.at[t, k], e1_r.at[t, y], (band, to * 4 + x)
        )

    def e1_arrives(t, k):
        source = (y + k) % 4
        remote(
            adv.at[source, t],
            r1.at[source, t],
            e1_s.at[t, k],
            e1_r.at[t, source],
            (band, source * 4 + x),
        ).wait_recv()

    def e2(t, k, part):
        to = (x + k) % 4
        src = s2.at[3, t] if part else s2.at[to - 2 * (to // 3), t]
        return remote(
            src,
            r2.at[part, x, t],
            e2_s.at[part, t, k],
            e2_r.at[part, t, x],
            (band, y * 4 + to),
        )

    def e2_arrives(t, k, part):
        source = (x + k) % 4
        remote(
            s2.at[0, t],
            r2.at[part, source, t],
            e2_s.at[part, t, k],
            e2_r.at[part, t, source],
            (band, y * 4 + source),
        ).wait_recv()

    def advect(t):
        for h in range(2):
            w_copy(h, t).wait()
            dep = depart[t, h : h + 1, :]
            for v in range(2):
                window = ext[h, v, pl.ds(pl.multiple_of(t * TILE, TILE), 64), 0:LAT]
                for offset in range(-1, 3):
                    start = pl.multiple_of((t + offset + 2) * TILE, TILE)
                    candidate = ext[h, v, pl.ds(start, 64), 0:LAT]
                    window = jnp.where(dep == offset, candidate, window)
                win[v] = window
            total = [jnp.zeros((TILE, LAT), F32) for _ in range(2)]
            for j in range(64):
                w = wbuf[h, t, j].astype(F32)
                for v in range(2):
                    total[v] = total[v] + win[v, j : j + 1, :] * w
            for v in range(2):
                adv[h * 2 + v, t, :, 0:LAT] = total[v]
        for k in range(1, 4):
            e1(t, k).start()
        r1[y, t] = adv[y, t]

    def radix(t):
        for k in range(1, 4):
            e1_arrives(t, k)
        a, b, c, d = r1[0, t], r1[1, t], r1[2, t], r1[3, t]
        s2[0, t] = (a + c) + (b + d)
        s2[1, t] = a - c
        s2[2, t] = (a + c) - (b + d)
        s2[3, t] = d - b
        for k in range(1, 4):
            e2(t, k, 0).start()

            @pl.when((x + k) % 2 == 1)
            def _():
                e2(t, k, 1).start()

        r2[0, x, t] = s2[x - 2 * (x // 3), t]

        @pl.when(odd)
        def _():
            r2[1, x, t] = s2[3, t]

    pl.loop(0, TILES)(advect)
    pl.loop(0, TILES)(radix)

    @pl.loop(0, TILES)
    def _(t):
        for k in range(1, 4):
            e2_arrives(t, k, 0)

            @pl.when(odd)
            def _():
                e2_arrives(t, k, 1)

    @pl.loop(0, 8)
    def _(i):
        part, source = i // 4, i % 4
        for t in range(TILES):
            high, low = split(r2[part, source, t])
            start = pl.multiple_of(i * 160 + t * TILE, TILE)
            zc[pl.ds(start, TILE), 0:LANES] = high
            zc[pl.ds(start, TILE), LANES : 2 * LANES] = low

    loads[0].wait()
    loads[1].wait()

    def e3(d):
        return remote(s3.at[d], r3.at[sec], e3_s.at[d], e3_r.at[sec], (band, d))

    @pl.loop(0, 4)
    def _(g):
        group = (g + sec // 4) % 4
        rows = pl.ds(pl.multiple_of(group * 160, 160), 160)
        both = dot(fh[rows, :], zc[...])
        value = both[:, 0:LANES] + both[:, LANES:] + dot(fl[rows, :], zc[:, 0:LANES])
        for q in range(4):
            d = group * 4 + q
            s3[d] = value[q * BLOCK : (q + 1) * BLOCK]

            @pl.when(d != sec)
            def _():
                e3(d).start()

            @pl.when(d == sec)
            def _():
                r3[d] = value[q * BLOCK : (q + 1) * BLOCK]

    loads[2].start()
    loads[3].start()

    @pl.loop(0, 8)
    def _(q):
        leg_copy(q).wait()

        @pl.loop(0, SHARE * TILES)
        def _(i):
            p = q * SHARE + i // 5
            rows = pl.ds(pl.multiple_of((i % 5) * 16, 16), 16)
            high, low = split(legf[p, rows, :])
            legh[p, rows, :] = high
            legl[p, rows, :] = low

    @pl.loop(1, 16)
    def _(k):
        source = (sec + k) % 16
        remote(
            s3.at[source], r3.at[source], e3_s.at[source], e3_r.at[source], (band, source)
        ).wait_recv()

    for v in range(2):
        for c in range(4):
            north, south = r3[v * 4 + c], r3[8 + v * 4 + c]
            eo[0, v, c] = north + south
            eo[1, v, c] = north - south
    for p in range(BLOCK):
        j, c = p // 4, p % 4
        for s in range(2):
            for v in range(2):
                row = s * 8 + v * 2
                lf[p, row : row + 2, :] = eo[s, v, c, 2 * j : 2 * j + 2, :]
                lf[p, row + 4 : row + 6, :] = eo[s, v, 3 - c, 20 + 2 * j : 22 + 2 * j, :]

    @pl.loop(0, BLOCK)
    def _(p):
        high, low = split(lf[p])
        lb[p, 0:16, :] = high
        lb[p, 16:32, :] = low

    column = lax.broadcasted_iota(jnp.int32, (8, ROWS), 1)

    def masks(p):
        limit = WAVES - (sec * BLOCK + p)
        leading = column < limit
        lag = jnp.where(leading, column, column - limit)
        return leading, (lag & 1) == 1

    def analyse(share):
        results = []
        for i in range(SHARE):
            p = share * SHARE + i
            lhs = lb[p, :, 0:LAT]
            both = dot(lhs, legh[p])
            total = both[0:16] + both[16:32] + dot(lhs[0:16], legl[p])
            leading, odd_rows = masks(p)
            chosen = jnp.where(odd_rows, total[8:16], total[0:8])
            results.append(jnp.where(leading[0:4], chosen[0:4], chosen[4:8]))
        return results

    partner = (z * 2 + 1 - core, sec)
    ahead, behind, across = (z + 1) % 4, (z + 3) % 4, (z + 2) % 4
    up, down = (ahead * 2 + core, sec), (behind * 2 + core, sec)

    def c1(k):
        return remote(pbuf.at[k], cbuf.at[k], c1_s.at[k], c1_r.at[k], partner)

    def share_at(k, which):
        return ((z + 2 + 3 * k + 3 * (k // 2) + 2 * (k // 3)) % 4) * 2 + which

    @pl.loop(0, 4)
    def _(k):
        for i, value in enumerate(analyse(share_at(k, 1 - core))):
            pbuf[k, i, :, 0:ROWS] = value
        c1(k).start()

    first, last = pl.ds(0, 3), pl.ds(3, 2)
    half_up = remote(sbuf.at[0, first], rbuf.at[first], c2_s.at[0], c2_r.at[0], up)
    half_down = remote(sbuf.at[0, last], rbuf.at[last], c2_s.at[1], c2_r.at[1], down)
    early_up = remote(sbuf.at[1, last], tbuf.at[0, last], c2_s.at[2], c2_r.at[2], up)
    early_down = remote(sbuf.at[2, first], tbuf.at[1, first], c2_s.at[3], c2_r.at[3], down)
    late_up = remote(sbuf.at[1, first], tbuf.at[0, first], c2_s.at[4], c2_r.at[4], up)
    late_down = remote(sbuf.at[2, last], tbuf.at[1, last], c2_s.at[5], c2_r.at[5], down)

    @pl.loop(0, 4)
    def _(k):
        values = analyse(share_at(k, core))
        for i, value in enumerate(values):
            sbuf[k, i, :, 0:ROWS] = value
        c1(k).wait_recv()
        for i in range(SHARE):
            sbuf[k, i] = sbuf[k, i] + cbuf[k, i]

        @pl.when(k == 0)
        def _():
            half_up.start()
            half_down.start()

        @pl.when(k == 1)
        def _():
            early_up.start()

        @pl.when(k == 2)
        def _():
            early_down.start()
            half_up.wait_recv()
            for i in range(3):
                sbuf[1, i] = sbuf[1, i] + rbuf[i]
            late_up.start()
            half_down.wait_recv()
            for i in range(3, SHARE):
                sbuf[2, i] = sbuf[2, i] + rbuf[i]
            late_down.start()

    for copy in (early_up, early_down, late_up, late_down):
        copy.wait_recv()
    first_level = lax.broadcasted_iota(jnp.int32, (4, ROWS), 0) < 2
    level = jnp.where(first_level, damping[0], damping[1])

    @pl.loop(0, SHARE)
    def _(i):
        p = sec * BLOCK + band * SHARE + i
        column4 = column[0:4]
        degree = jnp.where(column4 < WAVES - p, p + column4, column4 - 1)
        ratio = (degree * (degree + 1)).astype(F32) / float(WAVES * WAVES)
        total = (tbuf[0, i] + tbuf[1, i]) + sbuf[3, i]
        gbuf[band, i, :, 0:ROWS] = total[:, 0:ROWS] / (1.0 + level * ratio)

    def gathered(share, rows, sem, to, send, recv):
        ref = gbuf.at[share, rows]
        return remote(ref, ref, send.at[sem], recv.at[sem], to)

    every = pl.ds(0, SHARE)

    def gz(sem, share, rows, to):
        return gathered(share, rows, sem, to, gz_s, gz_r)

    def gp(sem, share, rows):
        return gathered(share, rows, sem, partner, gp_s, gp_r)

    other = 1 - core
    sends = [
        gz(0, band, first, up),
        gz(1, band, last, down),
        gz(2, behind * 2 + core, first, up),
        gz(3, ahead * 2 + core, last, down),
        gz(4, band, last, up),
        gz(5, band, first, down),
        gp(0, band, every),
        gp(1, behind * 2 + core, every),
        gp(2, ahead * 2 + core, every),
        gp(3, across * 2 + core, first),
        gp(4, across * 2 + core, last),
    ]
    arrivals = [
        gz(0, behind * 2 + core, first, up),
        gz(1, ahead * 2 + core, last, down),
        gz(2, across * 2 + core, first, up),
        gz(3, across * 2 + core, last, down),
        gz(4, behind * 2 + core, last, up),
        gz(5, ahead * 2 + core, first, down),
        gp(0, z * 2 + other, every),
        gp(1, behind * 2 + other, every),
        gp(2, ahead * 2 + other, every),
        gp(3, across * 2 + other, first),
        gp(4, across * 2 + other, last),
    ]
    for k in (0, 1, 4, 5, 6):
        sends[k].start()
    upper = lax.broadcasted_iota(jnp.int32, (8, ROWS), 0) >= 4

    def synthesise(share):
        for i in range(SHARE):
            p = share * SHARE + i
            spec = gbuf[share, i, :, 0:ROWS]
            leading, odd_rows = masks(p)
            north = jnp.concatenate([spec, spec], axis=0)
            north = jnp.where(leading != upper, north, 0.0)
            south = jnp.where(odd_rows, -north, north)
            high, low = split(jnp.concatenate([north, south], axis=0))
            both = dot_t(jnp.concatenate([high, low], axis=0), legh[p])
            syn[p, :, 0:LAT] = both[0:16] + both[16:32] + dot_t(high, legl[p])

    def step_share(k):
        late, turn = (k + 6) // 8, (k + 1) % 3
        chip = (z + late * (3 + 2 * turn + 3 * (turn // 2))) % 4
        swap = (k + 3) // 8 + (1 - late) * k
        return chip * 2 + core + swap * (1 - 2 * core)

    @pl.loop(0, 8)
    def _(k):
        @pl.when(k == 1)
        def _():
            arrivals[6].wait_recv()

        @pl.when(k == 2)
        def _():
            for n in (0, 1):
                arrivals[n].wait_recv()
                sends[n + 2].start()
            for n in (4, 5):
                arrivals[n].wait_recv()
                sends[n + 3].start()

        @pl.when(k == 4)
        def _():
            for n in (2, 3):
                arrivals[n].wait_recv()
                sends[n + 7].start()

        @pl.when(k == 5)
        def _():
            arrivals[7].wait_recv()

        @pl.when(k == 6)
        def _():
            arrivals[8].wait_recv()

        @pl.when(k == 7)
        def _():
            arrivals[9].wait_recv()
            arrivals[10].wait_recv()

        synthesise(step_share(k))

    for p in range(BLOCK):
        j, c = p // 4, p % 4
        for h in range(2):
            for v in range(2):
                row = h * 8 + v * 2
                block = (h * 2 + v) * 4
                s4[block + c, 2 * j : 2 * j + 2, :] = syn[p, row : row + 2, :]
                s4[block + 3 - c, 20 + 2 * j : 22 + 2 * j, :] = syn[p, row + 4 : row + 6, :]

    def e4(k):
        to = (sec + k) % 16
        return remote(s4.at[to], r4.at[sec], e4_s.at[k], e4_r.at[sec], (band, to))

    @pl.loop(1, 16)
    def _(k):
        e4(k).start()

    r4[sec] = s4[sec]
    loads[2].wait()
    loads[3].wait()

    @pl.loop(1, 16)
    def _(k):
        source = (sec + k) % 16
        remote(
            s4.at[source], r4.at[source], e4_s.at[k], e4_r.at[source], (band, source)
        ).wait_recv()

    @pl.loop(0, 8)
    def _(i):
        pair = jnp.concatenate([r4[2 * i], r4[2 * i + 1]], axis=0)
        high, low = split(pair)
        start = pl.multiple_of(i * 80, 80)
        yc[pl.ds(start, 80), 0:LANES] = high
        yc[pl.ds(start, 80), LANES : 2 * LANES] = low

    def e5(k, part):
        to = (x + k) % 4
        return remote(
            s5.at[part, to],
            r5.at[part, x],
            e5_s.at[part, k],
            e5_r.at[part, x],
            (band, y * 4 + to),
        )

    def e5_arrives(k, part):
        source = (x + k) % 4
        remote(
            s5.at[part, source],
            r5.at[part, source],
            e5_s.at[part, k],
            e5_r.at[part, source],
            (band, y * 4 + source),
        ).wait_recv()

    @pl.loop(0, 4)
    def _(g):
        k = (g + 1) % 4
        to = (x + k) % 4

        def part_of(part):
            rows = pl.ds(pl.multiple_of((to * 2 + part) * 160, 160), 160)
            both = dot(ih[rows, :], yc[...])
            value = both[:, 0:LANES] + both[:, LANES:] + dot(il[rows, :], yc[:, 0:LANES])
            s5[part, to] = value

            @pl.when(k != 0)
            def _():
                e5(k, part).start()

            @pl.when(k == 0)
            def _():
                r5[part, to] = value

        part_of(0)

        @pl.when(odd)
        def _():
            part_of(1)

    for k in range(1, 4):
        e5_arrives(k, 0)

        @pl.when((x + k) % 2 == 1)
        def _():
            e5_arrives(k, 1)

    def e6(t, k):
        to = (y + k) % 4
        return remote(
            o6.at[to, t], out.at[y, t], e6_s.at[t, k], e6_r.at[t, y], (band, to * 4 + x)
        )

    @pl.loop(0, TILES)
    def _(t):
        rows = pl.ds(pl.multiple_of(t * TILE, TILE), TILE)
        a, c = r5[0, 0, rows, :], r5[0, 2, rows, :]
        b = r5[0, 1, rows, :] + r5[0, 3, rows, :]
        d = r5[1, 3, rows, :] - r5[1, 1, rows, :]
        o6[0, t] = (a + c) + b
        o6[1, t] = (a - c) + d
        o6[2, t] = (a + c) - b
        o6[3, t] = (a - c) - d
        for k in range(1, 4):
            e6(t, k).start()
        out[y, t] = o6[y, t]

    @pl.loop(0, TILES)
    def _(t):
        for k in range(1, 4):
            source = (y + k) % 4
            remote(
                o6.at[source, t],
                out.at[source, t],
                e6_s.at[t, k],
                e6_r.at[t, source],
                (band, source * 4 + x),
            ).wait_recv()

    to_right.wait_send()
    to_left.wait_send()

    @pl.loop(0, TILES)
    def _(t):
        for k in range(1, 4):
            e1(t, k).wait_send()
            e2(t, k, 0).wait_send()

            @pl.when((x + k) % 2 == 1)
            def _():
                e2(t, k, 1).wait_send()

            e6(t, k).wait_send()

    @pl.loop(1, 16)
    def _(k):
        e3((sec + k) % 16).wait_send()
        e4(k).wait_send()

    for k in range(4):
        c1(k).wait_send()
    for copy in (half_up, half_down, early_up, early_down, late_up, late_down, *sends):
        copy.wait_send()
    for k in range(1, 4):
        e5(k, 0).wait_send()

        @pl.when(odd)
        def _():
            e5(k, 1).wait_send()


def local(field, depart, interp_weight, legendre, damping):
    moved = jnp.pad(jnp.transpose(field, (0, 2, 3, 1)), ((0, 0),) * 3 + ((0, LANES - LAT),))
    forward, inverse = tables()
    constants = [jnp.asarray(t) for t in (*halves(forward), *halves(inverse))]
    vmem = pl.BlockSpec(memory_space=pltpu.VMEM)
    hbm = pl.BlockSpec(memory_space=pl.ANY)
    scratch = [
        pltpu.VMEM((2, 2, 320, LANES), F32),
        pltpu.VMEM((2, 5, 64, TILE, LAT), BF16),
        pltpu.VMEM((2, 64, LAT), F32),
        pltpu.VMEM((4, 5, TILE, LANES), F32),
        pltpu.VMEM((4, 5, TILE, LANES), F32),
        pltpu.VMEM((4, 5, TILE, LANES), F32),
        pltpu.VMEM((2, 4, 5, TILE, LANES), F32),
        pltpu.VMEM((1280, 2 * LANES), BF16),
        pltpu.VMEM((640, 1280), BF16),
        pltpu.VMEM((640, 1280), BF16),
        pltpu.VMEM((1280, 640), BF16),
        pltpu.VMEM((1280, 640), BF16),
        pltpu.VMEM((16, BLOCK, LANES), F32),
        pltpu.VMEM((16, BLOCK, LANES), F32),
        pltpu.VMEM((2, 2, 4, BLOCK, LANES), F32),
        pltpu.VMEM((BLOCK, 16, LANES), F32),
        pltpu.VMEM((BLOCK, 32, LANES), BF16),
        pltpu.VMEM((BLOCK, LAT, ROWS), F32),
        pltpu.VMEM((BLOCK, LAT, ROWS), BF16),
        pltpu.VMEM((BLOCK, LAT, ROWS), BF16),
        pltpu.VMEM((4, SHARE, 4, WIDE), F32),
        pltpu.VMEM((4, SHARE, 4, WIDE), F32),
        pltpu.VMEM((4, SHARE, 4, WIDE), F32),
        pltpu.VMEM((SHARE, 4, WIDE), F32),
        pltpu.VMEM((2, SHARE, 4, WIDE), F32),
        pltpu.VMEM((8, SHARE, 4, WIDE), F32),
        pltpu.VMEM((BLOCK, 16, LANES), F32),
        pltpu.VMEM((16, BLOCK, LANES), F32),
        pltpu.VMEM((16, BLOCK, LANES), F32),
        pltpu.VMEM((640, 2 * LANES), BF16),
        pltpu.VMEM((2, 4, 160, LANES), F32),
        pltpu.VMEM((2, 4, 160, LANES), F32),
        pltpu.VMEM((4, 5, TILE, LANES), F32),
    ]
    dma = pltpu.SemaphoreType.DMA
    scratch += [
        dma,
        dma((2, 5)),
        dma((8,)),
        dma((4,)),
        dma((2,)),
        dma((2,)),
        dma((5, 4)),
        dma((5, 4)),
        dma((2, 5, 4)),
        dma((2, 5, 4)),
        dma((16,)),
        dma((16,)),
        dma((4,)),
        dma((4,)),
        dma((6,)),
        dma((6,)),
        dma((6,)),
        dma((6,)),
        dma((5,)),
        dma((5,)),
        dma((16,)),
        dma((16,)),
        dma((2, 4)),
        dma((2, 4)),
        dma((5, 4)),
        dma((5, 4)),
    ]
    grid = pl.pallas_call(
        kernel,
        out_shape=jax.ShapeDtypeStruct((4, 5, TILE, LANES), F32),
        in_specs=[vmem, vmem, hbm, hbm, pl.BlockSpec(memory_space=pltpu.SMEM)] + [hbm] * 4,
        out_specs=vmem,
        scratch_shapes=scratch,
        compiler_params=pltpu.CompilerParams(
            collective_id=0, has_side_effects=True, vmem_limit_bytes=62 * 1024 * 1024
        ),
    )(
        moved,
        jnp.transpose(depart, (2, 0, 1)),
        jnp.transpose(interp_weight, (0, 2, 3, 4, 1)),
        legendre,
        damping,
        *constants,
    )
    grid = grid.reshape(2, 2, 160, LANES)[..., 0:LAT]
    return jnp.transpose(grid, (0, 3, 1, 2))


def solution(mesh):
    placed = (
        P(None, "band", None, "sector"),
        P(None, "band", "sector"),
        P(None, "band", "sector", None, None),
        P("sector", "band", None),
        P(),
    )
    return jax.shard_map(
        local, mesh=mesh, in_specs=placed, out_specs=P(None, "band", None, "sector"), check_vma=False
    )
```

```python
import math

import jax
import jax.numpy as jnp
import ml_dtypes
import numpy as np
from jax import lax
from jax.experimental import pallas as pl
from jax.experimental.pallas import tpu as pltpu
from jax.sharding import PartitionSpec as P

F32 = jnp.float32
BF16 = jnp.bfloat16
LON = 2560
WAVES = 1280
ROWS = WAVES + 1
WIDE = WAVES + 128
TILE = 32
LANES = 128
LAT = 80
BLOCK = 40
SHARE = 5
TILES = 5
PACK = 24


def halves(table):
    high = table.astype(ml_dtypes.bfloat16)
    low = (table - high.astype(np.float64)).astype(ml_dtypes.bfloat16)
    return high, low


def tables():
    cls = np.arange(4)[:, None, None]
    d = np.arange(16)[None, :, None]
    j = np.arange(10)[None, None, :]
    lower = BLOCK * d + 4 * j + cls
    upper = WAVES - 4 - BLOCK * d - 4 * j + cls
    m = np.stack([lower, upper], axis=2)
    xi = np.arange(640)
    angle = 2.0 * math.pi / LON * ((m[..., None] * xi) % LON)
    cos, sin = np.cos(angle), np.sin(angle)
    sign = np.where(np.arange(4) == 3, -1.0, 1.0)[:, None, None, None, None]
    real = np.concatenate([cos, sin * sign], axis=-1)
    imag = np.concatenate([-sin, cos * sign], axis=-1)
    forward = np.stack([real, imag], axis=4).reshape(4, 640, 1280) / LON
    scale = np.where(m == 0, 1.0, 2.0)[..., None]
    cos, sin = cos * scale, sin * scale
    real = np.stack([cos, -sin], axis=4).reshape(4, 640, 640)
    imag = np.stack([sin, cos], axis=4).reshape(4, 640, 640)
    both = np.stack([real, imag], axis=1)
    both = both.reshape(4, 2, 640, 4, 160).transpose(0, 3, 1, 4, 2)
    inverse = both.reshape(4, 1280, 640)
    return forward, inverse


def split(value):
    high = value.astype(BF16)
    low = (value - high.astype(F32)).astype(BF16)
    return high, low


def dot(a, b):
    return jnp.dot(a, b, preferred_element_type=F32)


def dot_t(a, b):
    return lax.dot_general(a, b, (((1,), (1,)), ((), ())), preferred_element_type=F32)


def moves(count, base):
    found, slot, used = [], 0, 0
    for group in range(base, count):
        lane = 0
        while lane < LAT:
            n = min(LAT - lane, LANES - LAT - used)
            found.append((group, lane, n, slot, LAT + used))
            lane, used = lane + n, used + n
            if used == LANES - LAT:
                slot, used = slot + 1, 0
    return found


def between(start, n):
    lane = lax.broadcasted_iota(jnp.int32, (8, LANES), 1)
    return (lane >= start) & (lane < start + n)


def packed(value, base):
    groups = [value[8 * g : 8 * g + 8] for g in range(value.shape[0] // 8)]
    kept = groups[:base]
    for group, lane, n, slot, to in moves(len(groups), base):
        moved = pltpu.roll(groups[group], to - lane, 1)
        kept[slot] = jnp.where(between(to, n), moved, kept[slot])
    return jnp.concatenate(kept, axis=0)


def unpacked(value, count):
    base = value.shape[0] // 8
    groups = [value[8 * g : 8 * g + 8] for g in range(base)]
    groups += [jnp.zeros((8, LANES), F32)] * (count - base)
    for group, lane, n, slot, to in moves(count, base):
        moved = pltpu.roll(groups[slot], LANES + lane - to, 1)
        groups[group] = jnp.where(between(lane, n), moved, groups[group])
    return jnp.concatenate(groups, axis=0)


def remote(src, dst, send, recv, device):
    return pltpu.make_async_remote_copy(
        src_ref=src,
        dst_ref=dst,
        send_sem=send,
        recv_sem=recv,
        device_id=device,
        device_id_type=pl.DeviceIdType.MESH,
    )


def kernel(
    field,
    depart,
    weight,
    legendre,
    damping,
    fwd_high,
    fwd_low,
    inv_high,
    inv_low,
    out,
    ext,
    hs_right,
    hs_left,
    hr_right,
    hr_left,
    wbuf,
    win,
    adv,
    sent,
    r1,
    s2,
    r2,
    zc,
    fh,
    fl,
    ih,
    il,
    s3,
    r3,
    eo,
    lf,
    lb,
    legf,
    legh,
    legl,
    pbuf,
    cbuf,
    sbuf,
    rbuf,
    tbuf,
    gbuf,
    syn,
    s4,
    s4p,
    r4,
    yc,
    s5,
    r5,
    o6,
    r6,
    w_sem,
    leg_sem,
    tab_sem,
    halo_s,
    halo_r,
    e1_s,
    e1_r,
    e2_s,
    e2_r,
    e3_s,
    e3_r,
    c1_s,
    c1_r,
    c2_s,
    c2_r,
    gz_s,
    gz_r,
    gp_s,
    gp_r,
    e4_s,
    e4_r,
    e5_s,
    e5_r,
    e6_s,
    e6_r,
):
    band = lax.axis_index("band")
    sec = lax.axis_index("sector")
    y, x = sec // 4, sec % 4
    z, core = band // 2, band % 2
    odd = x % 2 == 1

    def w_copy(h, t):
        return pltpu.make_async_copy(weight.at[h, t], wbuf.at[h, t], w_sem.at[h, t])

    @pl.loop(0, TILES)
    def _(t):
        for h in range(2):
            w_copy(h, t).start()

    loads = [
        pltpu.make_async_copy(src.at[x], dst, tab_sem.at[i])
        for i, (src, dst) in enumerate(
            [(fwd_high, fh), (fwd_low, fl), (inv_high, ih), (inv_low, il)]
        )
    ]
    loads[0].start()
    loads[1].start()

    def leg_copy(q):
        rows = pl.ds(q * SHARE, SHARE)
        return pltpu.make_async_copy(legendre.at[rows], legf.at[rows], leg_sem.at[q])

    barrier = pltpu.get_barrier_semaphore()

    def greet(device):
        pl.semaphore_signal(barrier, inc=1, device_id=device, device_id_type=pl.DeviceIdType.MESH)

    for k in range(1, 16):
        greet((band, (sec + k) % 16))
    for k in range(1, 4):
        greet((((z + k) % 4) * 2 + core, sec))
    greet((z * 2 + 1 - core, sec))

    for h in range(2):
        for v in range(2):
            ext[h, v, 64:224, 0:LAT] = field[h, v]
            hs_right[h * 2 + v] = packed(ext[h, v, 160:224, :], 5)
            hs_left[h * 2 + v] = packed(ext[h, v, 64:160, :], 8)

    pl.semaphore_wait(barrier, 19)
    right, left = (sec + 1) % 16, (sec + 15) % 16
    to_right = remote(hs_right, hr_right, halo_s.at[0], halo_r.at[0], (band, right))
    to_left = remote(hs_left, hr_left, halo_s.at[1], halo_r.at[1], (band, left))
    to_right.start()
    to_left.start()
    adv[...] = jnp.zeros_like(adv)

    @pl.when(jnp.logical_not(odd))
    def _():
        r2[1] = jnp.zeros_like(r2[1])

    to_right.wait_recv()
    to_left.wait_recv()
    for h in range(2):
        for v in range(2):
            ext[h, v, 0:64, :] = unpacked(hr_right[h * 2 + v], 8)
            ext[h, v, 224:320, :] = unpacked(hr_left[h * 2 + v], 12)

    @pl.loop(0, 8)
    def _(q):
        leg_copy(q).start(priority=1)


    def e1(t, k):
        to = (y + k) % 4
        return remote(
            sent.at[to, t], r1.at[y, t], e1_s.at[t, k], e1_r.at[t, y], (band, to * 4 + x)
        )

    def e1_arrives(t, k):
        source = (y + k) % 4
        remote(
            sent.at[source, t],
            r1.at[source, t],
            e1_s.at[t, k],
            e1_r.at[t, source],
            (band, source * 4 + x),
        ).wait_recv()

    def e2(t, k, part):
        to = (x + k) % 4
        src = s2.at[3, t] if part else s2.at[to - 2 * (to // 3), t]
        return remote(
            src,
            r2.at[part, x, t],
            e2_s.at[part, t, k],
            e2_r.at[part, t, x],
            (band, y * 4 + to),
        )

    def e2_arrives(t, k, part):
        source = (x + k) % 4
        remote(
            s2.at[0, t],
            r2.at[part, source, t],
            e2_s.at[part, t, k],
            e2_r.at[part, t, source],
            (band, y * 4 + source),
        ).wait_recv()

    def advect(t):
        for h in range(2):
            w_copy(h, t).wait()
            dep = depart[t, h : h + 1, :]
            for v in range(2):
                window = ext[h, v, pl.ds(pl.multiple_of(t * TILE, TILE), 64), 0:LAT]
                for offset in range(-1, 3):
                    start = pl.multiple_of((t + offset + 2) * TILE, TILE)
                    candidate = ext[h, v, pl.ds(start, 64), 0:LAT]
                    window = jnp.where(dep == offset, candidate, window)
                win[v] = window
            total = [jnp.zeros((TILE, LAT), F32) for _ in range(2)]
            for j in range(64):
                w = wbuf[h, t, j].astype(F32)
                for v in range(2):
                    total[v] = total[v] + win[v, j : j + 1, :] * w
            for v in range(2):
                adv[h * 2 + v, :, 0:LAT] = total[v]
                sent[h * 2 + v, t] = packed(adv[h * 2 + v], 3)
        for k in range(1, 4):
            e1(t, k).start()
        r1[y, t] = sent[y, t]

    def radix(t):
        for k in range(1, 4):
            e1_arrives(t, k)
        a, b, c, d = r1[0, t], r1[1, t], r1[2, t], r1[3, t]
        s2[0, t] = (a + c) + (b + d)
        s2[1, t] = a - c
        s2[2, t] = (a + c) - (b + d)
        s2[3, t] = d - b
        for k in range(1, 4):
            e2(t, k, 0).start()

            @pl.when((x + k) % 2 == 1)
            def _():
                e2(t, k, 1).start()

        r2[0, x, t] = s2[x - 2 * (x // 3), t]

        @pl.when(odd)
        def _():
            r2[1, x, t] = s2[3, t]

    pl.loop(0, TILES)(advect)
    pl.loop(0, TILES)(radix)

    @pl.loop(0, TILES)
    def _(t):
        for k in range(1, 4):
            e2_arrives(t, k, 0)

            @pl.when(odd)
            def _():
                e2_arrives(t, k, 1)

    @pl.loop(0, 8)
    def _(i):
        part, source = i // 4, i % 4
        for t in range(TILES):
            high, low = split(unpacked(r2[part, source, t], 4))
            start = pl.multiple_of(i * 160 + t * TILE, TILE)
            zc[pl.ds(start, TILE), 0:LANES] = high
            zc[pl.ds(start, TILE), LANES : 2 * LANES] = low

    loads[0].wait()
    loads[1].wait()

    def e3(d):
        return remote(s3.at[d], r3.at[sec], e3_s.at[d], e3_r.at[sec], (band, d))

    @pl.loop(0, 4)
    def _(g):
        group = (g + sec // 4) % 4
        rows = pl.ds(pl.multiple_of(group * 160, 160), 160)
        both = dot(fh[rows, :], zc[...])
        value = both[:, 0:LANES] + both[:, LANES:] + dot(fl[rows, :], zc[:, 0:LANES])
        for q in range(4):
            d = group * 4 + q
            s3[d] = packed(value[q * BLOCK : (q + 1) * BLOCK], 4)

            @pl.when(d != sec)
            def _():
                e3(d).start()

            @pl.when(d == sec)
            def _():
                r3[d] = s3[d]

    loads[2].start()
    loads[3].start()

    @pl.loop(0, 8)
    def _(q):
        leg_copy(q).wait()

        @pl.loop(0, SHARE * TILES)
        def _(i):
            p = q * SHARE + i // 5
            rows = pl.ds(pl.multiple_of((i % 5) * 16, 16), 16)
            high, low = split(legf[p, rows, :])
            legh[p, rows, :] = high
            legl[p, rows, :] = low

    @pl.loop(1, 16)
    def _(k):
        source = (sec + k) % 16
        remote(
            s3.at[source], r3.at[source], e3_s.at[source], e3_r.at[source], (band, source)
        ).wait_recv()

    for v in range(2):
        for c in range(4):
            north, south = r3[v * 4 + c], r3[8 + v * 4 + c]
            eo[0, v, c] = unpacked(north + south, 5)
            eo[1, v, c] = unpacked(north - south, 5)
    for p in range(BLOCK):
        j, c = p // 4, p % 4
        for s in range(2):
            for v in range(2):
                row = s * 8 + v * 2
                lf[p, row : row + 2, :] = eo[s, v, c, 2 * j : 2 * j + 2, :]
                lf[p, row + 4 : row + 6, :] = eo[s, v, 3 - c, 20 + 2 * j : 22 + 2 * j, :]

    @pl.loop(0, BLOCK)
    def _(p):
        high, low = split(lf[p])
        lb[p, 0:16, :] = high
        lb[p, 16:32, :] = low

    column = lax.broadcasted_iota(jnp.int32, (8, ROWS), 1)

    def masks(p):
        limit = WAVES - (sec * BLOCK + p)
        leading = column < limit
        lag = jnp.where(leading, column, column - limit)
        return leading, (lag & 1) == 1

    def analyse(share):
        results = []
        for i in range(SHARE):
            p = share * SHARE + i
            lhs = lb[p, :, 0:LAT]
            both = dot(lhs, legh[p])
            total = both[0:16] + both[16:32] + dot(lhs[0:16], legl[p])
            leading, odd_rows = masks(p)
            chosen = jnp.where(odd_rows, total[8:16], total[0:8])
            results.append(jnp.where(leading[0:4], chosen[0:4], chosen[4:8]))
        return results

    partner = (z * 2 + 1 - core, sec)
    ahead, behind, across = (z + 1) % 4, (z + 3) % 4, (z + 2) % 4
    up, down = (ahead * 2 + core, sec), (behind * 2 + core, sec)

    def c1(k):
        return remote(pbuf.at[k], cbuf.at[k], c1_s.at[k], c1_r.at[k], partner)

    def share_at(k, which):
        return ((z + 2 + 3 * k + 3 * (k // 2) + 2 * (k // 3)) % 4) * 2 + which

    @pl.loop(0, 4)
    def _(k):
        for i, value in enumerate(analyse(share_at(k, 1 - core))):
            pbuf[k, i, :, 0:ROWS] = value
        c1(k).start()

    first, last = pl.ds(0, 3), pl.ds(3, 2)
    half_up = remote(sbuf.at[0, first], rbuf.at[first], c2_s.at[0], c2_r.at[0], up)
    half_down = remote(sbuf.at[0, last], rbuf.at[last], c2_s.at[1], c2_r.at[1], down)
    early_up = remote(sbuf.at[1, last], tbuf.at[0, last], c2_s.at[2], c2_r.at[2], up)
    early_down = remote(sbuf.at[2, first], tbuf.at[1, first], c2_s.at[3], c2_r.at[3], down)
    late_up = remote(sbuf.at[1, first], tbuf.at[0, first], c2_s.at[4], c2_r.at[4], up)
    late_down = remote(sbuf.at[2, last], tbuf.at[1, last], c2_s.at[5], c2_r.at[5], down)

    @pl.loop(0, 4)
    def _(k):
        values = analyse(share_at(k, core))
        for i, value in enumerate(values):
            sbuf[k, i, :, 0:ROWS] = value
        c1(k).wait_recv()
        for i in range(SHARE):
            sbuf[k, i] = sbuf[k, i] + cbuf[k, i]

        @pl.when(k == 0)
        def _():
            half_up.start()
            half_down.start()

        @pl.when(k == 1)
        def _():
            early_up.start()

        @pl.when(k == 2)
        def _():
            early_down.start()
            half_up.wait_recv()
            for i in range(3):
                sbuf[1, i] = sbuf[1, i] + rbuf[i]
            late_up.start()
            half_down.wait_recv()
            for i in range(3, SHARE):
                sbuf[2, i] = sbuf[2, i] + rbuf[i]
            late_down.start()

    for copy in (early_up, early_down, late_up, late_down):
        copy.wait_recv()
    first_level = lax.broadcasted_iota(jnp.int32, (4, ROWS), 0) < 2
    level = jnp.where(first_level, damping[0], damping[1])

    @pl.loop(0, SHARE)
    def _(i):
        p = sec * BLOCK + band * SHARE + i
        column4 = column[0:4]
        degree = jnp.where(column4 < WAVES - p, p + column4, column4 - 1)
        ratio = (degree * (degree + 1)).astype(F32) / float(WAVES * WAVES)
        total = (tbuf[0, i] + tbuf[1, i]) + sbuf[3, i]
        gbuf[band, i, :, 0:ROWS] = total[:, 0:ROWS] / (1.0 + level * ratio)

    def gathered(share, rows, sem, to, send, recv):
        ref = gbuf.at[share, rows]
        return remote(ref, ref, send.at[sem], recv.at[sem], to)

    every = pl.ds(0, SHARE)

    def gz(sem, share, rows, to):
        return gathered(share, rows, sem, to, gz_s, gz_r)

    def gp(sem, share, rows):
        return gathered(share, rows, sem, partner, gp_s, gp_r)

    other = 1 - core
    sends = [
        gz(0, band, first, up),
        gz(1, band, last, down),
        gz(2, behind * 2 + core, first, up),
        gz(3, ahead * 2 + core, last, down),
        gz(4, band, last, up),
        gz(5, band, first, down),
        gp(0, band, every),
        gp(1, behind * 2 + core, every),
        gp(2, ahead * 2 + core, every),
        gp(3, across * 2 + core, first),
        gp(4, across * 2 + core, last),
    ]
    arrivals = [
        gz(0, behind * 2 + core, first, up),
        gz(1, ahead * 2 + core, last, down),
        gz(2, across * 2 + core, first, up),
        gz(3, across * 2 + core, last, down),
        gz(4, behind * 2 + core, last, up),
        gz(5, ahead * 2 + core, first, down),
        gp(0, z * 2 + other, every),
        gp(1, behind * 2 + other, every),
        gp(2, ahead * 2 + other, every),
        gp(3, across * 2 + other, first),
        gp(4, across * 2 + other, last),
    ]
    for k in (0, 1, 4, 5, 6):
        sends[k].start()
    upper = lax.broadcasted_iota(jnp.int32, (8, ROWS), 0) >= 4

    def synthesise(share):
        for i in range(SHARE):
            p = share * SHARE + i
            spec = gbuf[share, i, :, 0:ROWS]
            leading, odd_rows = masks(p)
            north = jnp.concatenate([spec, spec], axis=0)
            north = jnp.where(leading != upper, north, 0.0)
            south = jnp.where(odd_rows, -north, north)
            high, low = split(jnp.concatenate([north, south], axis=0))
            both = dot_t(jnp.concatenate([high, low], axis=0), legh[p])
            syn[p, :, 0:LAT] = both[0:16] + both[16:32] + dot_t(high, legl[p])

    def step_share(k):
        late, turn = (k + 6) // 8, (k + 1) % 3
        chip = (z + late * (3 + 2 * turn + 3 * (turn // 2))) % 4
        swap = (k + 3) // 8 + (1 - late) * k
        return chip * 2 + core + swap * (1 - 2 * core)

    @pl.loop(0, 8)
    def _(k):
        @pl.when(k == 1)
        def _():
            arrivals[6].wait_recv()

        @pl.when(k == 2)
        def _():
            for n in (0, 1):
                arrivals[n].wait_recv()
                sends[n + 2].start()
            for n in (4, 5):
                arrivals[n].wait_recv()
                sends[n + 3].start()

        @pl.when(k == 4)
        def _():
            for n in (2, 3):
                arrivals[n].wait_recv()
                sends[n + 7].start()

        @pl.when(k == 5)
        def _():
            arrivals[7].wait_recv()

        @pl.when(k == 6)
        def _():
            arrivals[8].wait_recv()

        @pl.when(k == 7)
        def _():
            arrivals[9].wait_recv()
            arrivals[10].wait_recv()

        synthesise(step_share(k))

    for p in range(BLOCK):
        j, c = p // 4, p % 4
        for h in range(2):
            for v in range(2):
                row = h * 8 + v * 2
                block = (h * 2 + v) * 4
                s4[block + c, 2 * j : 2 * j + 2, :] = syn[p, row : row + 2, :]
                s4[block + 3 - c, 20 + 2 * j : 22 + 2 * j, :] = syn[p, row + 4 : row + 6, :]

    def e4(k):
        to = (sec + k) % 16
        return remote(s4p.at[to], r4.at[sec], e4_s.at[k], e4_r.at[sec], (band, to))

    @pl.loop(1, 16)
    def _(k):
        to = (sec + k) % 16
        s4p[to] = packed(s4[to], 4)
        e4(k).start()

    r4[sec] = packed(s4[sec], 4)
    loads[2].wait()
    loads[3].wait()

    @pl.loop(1, 16)
    def _(k):
        source = (sec + k) % 16
        remote(
            s4p.at[source], r4.at[source], e4_s.at[k], e4_r.at[source], (band, source)
        ).wait_recv()

    @pl.loop(0, 8)
    def _(i):
        pair = jnp.concatenate([unpacked(r4[2 * i], 5), unpacked(r4[2 * i + 1], 5)], axis=0)
        high, low = split(pair)
        start = pl.multiple_of(i * 80, 80)
        yc[pl.ds(start, 80), 0:LANES] = high
        yc[pl.ds(start, 80), LANES : 2 * LANES] = low

    def e5(k, part, half):
        to = (x + k) % 4
        return remote(
            s5.at[part, to, half],
            r5.at[part, x, half],
            e5_s.at[part, half, k],
            e5_r.at[part, half, x],
            (band, y * 4 + to),
        )

    def e5_arrives(k, part, half):
        source = (x + k) % 4
        remote(
            s5.at[part, source, half],
            r5.at[part, source, half],
            e5_s.at[part, half, k],
            e5_r.at[part, half, source],
            (band, y * 4 + source),
        ).wait_recv()

    @pl.loop(0, 8)
    def _(g):
        half, k = g // 4, (g + 1) % 4
        to = (x + k) % 4

        def part_of(part):
            rows = pl.ds(pl.multiple_of((to * 2 + part) * 160 + half * 80, 80), 80)
            both = dot(ih[rows, :], yc[...])
            value = both[:, 0:LANES] + both[:, LANES:] + dot(il[rows, :], yc[:, 0:LANES])
            s5[part, to, half] = packed(value, 7)

            @pl.when(k != 0)
            def _():
                e5(k, part, half).start()

            @pl.when(k == 0)
            def _():
                r5[part, to, half] = s5[part, to, half]

        part_of(0)

        @pl.when(odd)
        def _():
            part_of(1)

    def e6(half, k):
        to = (y + k) % 4
        return remote(
            o6.at[to, half], r6.at[y, half], e6_s.at[half, k], e6_r.at[half, y], (band, to * 4 + x)
        )

    @pl.loop(0, 2)
    def _(half):
        for k in range(1, 4):
            e5_arrives(k, 0, half)

            @pl.when((x + k) % 2 == 1)
            def _():
                e5_arrives(k, 1, half)

        a, c = r5[0, 0, half], r5[0, 2, half]
        b = r5[0, 1, half] + r5[0, 3, half]
        d = r5[1, 3, half] - r5[1, 1, half]
        o6[0, half] = (a + c) + b
        o6[1, half] = (a - c) + d
        o6[2, half] = (a + c) - b
        o6[3, half] = (a - c) - d
        for k in range(1, 4):
            e6(half, k).start()
        out[y, half] = unpacked(o6[y, half], 10)

    @pl.loop(0, 2)
    def _(half):
        for k in range(1, 4):
            source = (y + k) % 4
            remote(
                o6.at[source, half],
                r6.at[source, half],
                e6_s.at[half, k],
                e6_r.at[half, source],
                (band, source * 4 + x),
            ).wait_recv()
            out[source, half] = unpacked(r6[source, half], 10)

    to_right.wait_send()
    to_left.wait_send()

    @pl.loop(0, TILES)
    def _(t):
        for k in range(1, 4):
            e1(t, k).wait_send()
            e2(t, k, 0).wait_send()

            @pl.when((x + k) % 2 == 1)
            def _():
                e2(t, k, 1).wait_send()

    @pl.loop(1, 16)
    def _(k):
        e3((sec + k) % 16).wait_send()
        e4(k).wait_send()

    for k in range(4):
        c1(k).wait_send()
    for copy in (half_up, half_down, early_up, early_down, late_up, late_down, *sends):
        copy.wait_send()
    for k in range(1, 4):
        for half in range(2):
            e5(k, 0, half).wait_send()

            @pl.when(odd)
            def _():
                e5(k, 1, half).wait_send()

            e6(half, k).wait_send()


def local(field, depart, interp_weight, legendre, damping):
    forward, inverse = tables()
    constants = [jnp.asarray(t) for t in (*halves(forward), *halves(inverse))]
    vmem = pl.BlockSpec(memory_space=pltpu.VMEM)
    hbm = pl.BlockSpec(memory_space=pl.ANY)
    scratch = [
        pltpu.VMEM((2, 2, 320, LANES), F32),
        pltpu.VMEM((4, 40, LANES), F32),
        pltpu.VMEM((4, 64, LANES), F32),
        pltpu.VMEM((4, 40, LANES), F32),
        pltpu.VMEM((4, 64, LANES), F32),
        pltpu.VMEM((2, 5, 64, TILE, LAT), BF16),
        pltpu.VMEM((2, 64, LAT), F32),
        pltpu.VMEM((4, TILE, LANES), F32),
        pltpu.VMEM((4, 5, PACK, LANES), F32),
        pltpu.VMEM((4, 5, PACK, LANES), F32),
        pltpu.VMEM((4, 5, PACK, LANES), F32),
        pltpu.VMEM((2, 4, 5, PACK, LANES), F32),
        pltpu.VMEM((1280, 2 * LANES), BF16),
        pltpu.VMEM((640, 1280), BF16),
        pltpu.VMEM((640, 1280), BF16),
        pltpu.VMEM((1280, 640), BF16),
        pltpu.VMEM((1280, 640), BF16),
        pltpu.VMEM((16, 32, LANES), F32),
        pltpu.VMEM((16, 32, LANES), F32),
        pltpu.VMEM((2, 2, 4, BLOCK, LANES), F32),
        pltpu.VMEM((BLOCK, 16, LANES), F32),
        pltpu.VMEM((BLOCK, 32, LANES), BF16),
        pltpu.VMEM((BLOCK, LAT, ROWS), F32),
        pltpu.VMEM((BLOCK, LAT, ROWS), BF16),
        pltpu.VMEM((BLOCK, LAT, ROWS), BF16),
        pltpu.VMEM((4, SHARE, 4, WIDE), F32),
        pltpu.VMEM((4, SHARE, 4, WIDE), F32),
        pltpu.VMEM((4, SHARE, 4, WIDE), F32),
        pltpu.VMEM((SHARE, 4, WIDE), F32),
        pltpu.VMEM((2, SHARE, 4, WIDE), F32),
        pltpu.VMEM((8, SHARE, 4, WIDE), F32),
        pltpu.VMEM((BLOCK, 16, LANES), F32),
        pltpu.VMEM((16, BLOCK, LANES), F32),
        pltpu.VMEM((16, 32, LANES), F32),
        pltpu.VMEM((16, 32, LANES), F32),
        pltpu.VMEM((640, 2 * LANES), BF16),
        pltpu.VMEM((2, 4, 2, 56, LANES), F32),
        pltpu.VMEM((2, 4, 2, 56, LANES), F32),
        pltpu.VMEM((4, 2, 56, LANES), F32),
        pltpu.VMEM((4, 2, 56, LANES), F32),
    ]
    dma = pltpu.SemaphoreType.DMA
    scratch += [
        dma((2, 5)),
        dma((8,)),
        dma((4,)),
        dma((2,)),
        dma((2,)),
        dma((5, 4)),
        dma((5, 4)),
        dma((2, 5, 4)),
        dma((2, 5, 4)),
        dma((16,)),
        dma((16,)),
        dma((4,)),
        dma((4,)),
        dma((6,)),
        dma((6,)),
        dma((6,)),
        dma((6,)),
        dma((5,)),
        dma((5,)),
        dma((16,)),
        dma((16,)),
        dma((2, 2, 4)),
        dma((2, 2, 4)),
        dma((2, 4)),
        dma((2, 4)),
    ]
    grid = pl.pallas_call(
        kernel,
        out_shape=jax.ShapeDtypeStruct((4, 2, 80, LANES), F32),
        in_specs=[vmem, vmem, hbm, hbm, pl.BlockSpec(memory_space=pltpu.SMEM)] + [hbm] * 4,
        out_specs=vmem,
        scratch_shapes=scratch,
        compiler_params=pltpu.CompilerParams(
            collective_id=0, has_side_effects=True, vmem_limit_bytes=62 * 1024 * 1024
        ),
    )(
        jnp.transpose(field, (0, 2, 3, 1)),
        jnp.transpose(depart, (2, 0, 1)),
        jnp.transpose(interp_weight, (0, 2, 3, 4, 1)),
        legendre,
        damping,
        *constants,
    )
    grid = grid.reshape(2, 2, 160, LANES)[..., 0:LAT]
    return jnp.transpose(grid, (0, 3, 1, 2))


def solution(mesh):
    placed = (
        P(None, "band", None, "sector"),
        P(None, "band", "sector"),
        P(None, "band", "sector", None, None),
        P("sector", "band", None),
        P(),
    )
    return jax.shard_map(
        local, mesh=mesh, in_specs=placed, out_specs=P(None, "band", None, "sector"), check_vma=False
    )
```

```python
import math

import jax
import jax.numpy as jnp
import ml_dtypes
import numpy as np
from jax import lax
from jax.experimental import pallas as pl
from jax.experimental.pallas import tpu as pltpu
from jax.sharding import PartitionSpec as P

F32 = jnp.float32
BF16 = jnp.bfloat16
LON = 2560
WAVES = 1280
ROWS = WAVES + 1
WIDE = WAVES + 128
TILE = 32
LANES = 128
LAT = 80
BLOCK = 40
SHARE = 5
TILES = 5
PACK = 24


def halves(table):
    high = table.astype(ml_dtypes.bfloat16)
    low = (table - high.astype(np.float64)).astype(ml_dtypes.bfloat16)
    return high, low


def tables():
    cls = np.arange(4)[:, None, None]
    d = np.arange(16)[None, :, None]
    j = np.arange(10)[None, None, :]
    lower = BLOCK * d + 4 * j + cls
    upper = WAVES - 4 - BLOCK * d - 4 * j + cls
    m = np.stack([lower, upper], axis=2)
    xi = np.arange(640)
    angle = 2.0 * math.pi / LON * ((m[..., None] * xi) % LON)
    cos, sin = np.cos(angle), np.sin(angle)
    sign = np.where(np.arange(4) == 3, -1.0, 1.0)[:, None, None, None, None]
    real = np.concatenate([cos, sin * sign], axis=-1)
    imag = np.concatenate([-sin, cos * sign], axis=-1)
    forward = np.stack([real, imag], axis=4).reshape(4, 640, 1280) / LON
    scale = np.where(m == 0, 1.0, 2.0)[..., None]
    cos, sin = cos * scale, sin * scale
    real = np.stack([cos, -sin], axis=4).reshape(4, 640, 640)
    imag = np.stack([sin, cos], axis=4).reshape(4, 640, 640)
    both = np.stack([real, imag], axis=1)
    both = both.reshape(4, 2, 640, 4, 160).transpose(0, 3, 1, 4, 2)
    inverse = both.reshape(4, 1280, 640)
    return forward, inverse


def split(value):
    high = value.astype(BF16)
    low = (value - high.astype(F32)).astype(BF16)
    return high, low


def dot(a, b):
    return jnp.dot(a, b, preferred_element_type=F32)


def dot_t(a, b):
    return lax.dot_general(a, b, (((1,), (1,)), ((), ())), preferred_element_type=F32)


def moves(count, base):
    found, slot, used = [], 0, 0
    for group in range(base, count):
        lane = 0
        while lane < LAT:
            n = min(LAT - lane, LANES - LAT - used)
            found.append((group, lane, n, slot, LAT + used))
            lane, used = lane + n, used + n
            if used == LANES - LAT:
                slot, used = slot + 1, 0
    return found


def between(start, n):
    lane = lax.broadcasted_iota(jnp.int32, (8, LANES), 1)
    return (lane >= start) & (lane < start + n)


def packed(value, base):
    groups = [value[8 * g : 8 * g + 8] for g in range(value.shape[0] // 8)]
    kept = groups[:base]
    for group, lane, n, slot, to in moves(len(groups), base):
        moved = pltpu.roll(groups[group], to - lane, 1)
        kept[slot] = jnp.where(between(to, n), moved, kept[slot])
    return jnp.concatenate(kept, axis=0)


def unpacked(value, count):
    base = value.shape[0] // 8
    groups = [value[8 * g : 8 * g + 8] for g in range(base)]
    groups += [jnp.zeros((8, LANES), F32)] * (count - base)
    for group, lane, n, slot, to in moves(count, base):
        moved = pltpu.roll(groups[slot], LANES + lane - to, 1)
        groups[group] = jnp.where(between(lane, n), moved, groups[group])
    return jnp.concatenate(groups, axis=0)


def remote(src, dst, send, recv, device):
    return pltpu.make_async_remote_copy(
        src_ref=src,
        dst_ref=dst,
        send_sem=send,
        recv_sem=recv,
        device_id=device,
        device_id_type=pl.DeviceIdType.MESH,
    )


def kernel(
    field,
    depart,
    weight,
    legendre,
    damping,
    fwd_high,
    fwd_low,
    inv_high,
    inv_low,
    out,
    ext,
    hs,
    hr,
    wbuf,
    win,
    adv,
    sent,
    r1,
    s2,
    r2,
    zc,
    fh,
    fl,
    ih,
    il,
    s3,
    r3,
    eo,
    lf,
    lb,
    legf,
    legh,
    legl,
    pbuf,
    cbuf,
    sbuf,
    rbuf,
    tbuf,
    gbuf,
    syn,
    s4,
    s4p,
    r4,
    yc,
    s5,
    r5,
    o6,
    r6,
    w_sem,
    leg_sem,
    tab_sem,
    halo_s,
    halo_r,
    e1_s,
    e1_r,
    e2_s,
    e2_r,
    e3_s,
    e3_r,
    c1_s,
    c1_r,
    c2_s,
    c2_r,
    gz_s,
    gz_r,
    gp_s,
    gp_r,
    e4_s,
    e4_r,
    e5_s,
    e5_r,
    e6_s,
    e6_r,
):
    band = lax.axis_index("band")
    sec = lax.axis_index("sector")
    y, x = sec // 4, sec % 4
    z, core = band // 2, band % 2
    odd = x % 2 == 1

    def w_copy(h, t):
        return pltpu.make_async_copy(weight.at[h, t], wbuf.at[h, t], w_sem.at[h, t])

    @pl.loop(0, TILES)
    def _(t):
        for h in range(2):
            w_copy(h, t).start()

    loads = [
        pltpu.make_async_copy(src.at[x], dst, tab_sem.at[i])
        for i, (src, dst) in enumerate(
            [(fwd_high, fh), (fwd_low, fl), (inv_high, ih), (inv_low, il)]
        )
    ]
    loads[0].start()
    loads[1].start()

    def leg_copy(q):
        rows = pl.ds(q * SHARE, SHARE)
        return pltpu.make_async_copy(legendre.at[rows], legf.at[rows], leg_sem.at[q])

    barrier = pltpu.get_barrier_semaphore()

    def greet(device):
        pl.semaphore_signal(barrier, inc=1, device_id=device, device_id_type=pl.DeviceIdType.MESH)

    for k in range(1, 16):
        greet((band, (sec + k) % 16))
    for k in range(1, 4):
        greet((((z + k) % 4) * 2 + core, sec))
    greet((z * 2 + 1 - core, sec))

    for h in range(2):
        for v in range(2):
            ext[h, v, 64:224, 0:LAT] = field[h, v]
            for i, start in enumerate((64, 192, 96, 160, 128)):
                hs[i, h * 2 + v] = packed(ext[h, v, start : start + TILE, :], 3)

    pl.semaphore_wait(barrier, 19)

    def halo(i):
        to = (sec + 15 - 14 * (i % 2)) % 16
        return remote(hs.at[i], hr.at[i], halo_s.at[i], halo_r.at[i], (band, to))

    for i in range(TILES):
        halo(i).start()
    adv[...] = jnp.zeros_like(adv)

    @pl.when(jnp.logical_not(odd))
    def _():
        r2[1] = jnp.zeros_like(r2[1])

    @pl.loop(0, 8)
    def _(q):
        leg_copy(q).start(priority=1)


    def e1(t, k):
        to = (y + k) % 4
        return remote(
            sent.at[to, t], r1.at[y, t], e1_s.at[t, k], e1_r.at[t, y], (band, to * 4 + x)
        )

    def e1_arrives(t, k):
        source = (y + k) % 4
        remote(
            sent.at[source, t],
            r1.at[source, t],
            e1_s.at[t, k],
            e1_r.at[t, source],
            (band, source * 4 + x),
        ).wait_recv()

    def e2(t, k, part):
        to = (x + k) % 4
        src = s2.at[3, t] if part else s2.at[to - 2 * (to // 3), t]
        return remote(
            src,
            r2.at[part, x, t],
            e2_s.at[part, t, k],
            e2_r.at[part, t, x],
            (band, y * 4 + to),
        )

    def e2_arrives(t, k, part):
        source = (x + k) % 4
        remote(
            s2.at[0, t],
            r2.at[part, source, t],
            e2_s.at[part, t, k],
            e2_r.at[part, t, source],
            (band, y * 4 + source),
        ).wait_recv()

    def tile_of(i):
        return 2 + (1 - 2 * (i % 2)) * ((i + 1) // 2)

    def advect(i):
        t = tile_of(i)
        halo(i).wait_recv()
        start = (1 - i % 2) * (224 + 16 * i) + (i % 2) * (48 - 16 * i)
        rows = pl.ds(pl.multiple_of(start, TILE), TILE)
        for h in range(2):
            for v in range(2):
                ext[h, v, rows, :] = unpacked(hr[i, h * 2 + v], 4)
        for h in range(2):
            w_copy(h, t).wait()
            dep = depart[t, h : h + 1, :]
            for v in range(2):
                window = ext[h, v, pl.ds(pl.multiple_of(t * TILE, TILE), 64), 0:LAT]
                for offset in range(-1, 3):
                    start = pl.multiple_of((t + offset + 2) * TILE, TILE)
                    candidate = ext[h, v, pl.ds(start, 64), 0:LAT]
                    window = jnp.where(dep == offset, candidate, window)
                win[v] = window
            total = [jnp.zeros((TILE, LAT), F32) for _ in range(2)]
            for j in range(64):
                w = wbuf[h, t, j].astype(F32)
                for v in range(2):
                    total[v] = total[v] + win[v, j : j + 1, :] * w
            for v in range(2):
                adv[h * 2 + v, :, 0:LAT] = total[v]
                sent[h * 2 + v, t] = packed(adv[h * 2 + v], 3)
        for k in range(1, 4):
            e1(t, k).start()
        r1[y, t] = sent[y, t]

    def radix(i):
        t = tile_of(i)
        for k in range(1, 4):
            e1_arrives(t, k)
        a, b, c, d = r1[0, t], r1[1, t], r1[2, t], r1[3, t]
        s2[0, t] = (a + c) + (b + d)
        s2[1, t] = a - c
        s2[2, t] = (a + c) - (b + d)
        s2[3, t] = d - b
        for k in range(1, 4):
            e2(t, k, 0).start()

            @pl.when((x + k) % 2 == 1)
            def _():
                e2(t, k, 1).start()

        r2[0, x, t] = s2[x - 2 * (x // 3), t]

        @pl.when(odd)
        def _():
            r2[1, x, t] = s2[3, t]

    pl.loop(0, TILES)(advect)
    pl.loop(0, TILES)(radix)

    @pl.loop(0, TILES)
    def _(t):
        for k in range(1, 4):
            e2_arrives(t, k, 0)

            @pl.when(odd)
            def _():
                e2_arrives(t, k, 1)

    @pl.loop(0, 8)
    def _(i):
        part, source = i // 4, i % 4
        for t in range(TILES):
            high, low = split(unpacked(r2[part, source, t], 4))
            start = pl.multiple_of(i * 160 + t * TILE, TILE)
            zc[pl.ds(start, TILE), 0:LANES] = high
            zc[pl.ds(start, TILE), LANES : 2 * LANES] = low

    loads[0].wait()
    loads[1].wait()

    def e3(d):
        return remote(s3.at[d], r3.at[sec], e3_s.at[d], e3_r.at[sec], (band, d))

    @pl.loop(0, 4)
    def _(g):
        group = (g + sec // 4) % 4
        rows = pl.ds(pl.multiple_of(group * 160, 160), 160)
        both = dot(fh[rows, :], zc[...])
        value = both[:, 0:LANES] + both[:, LANES:] + dot(fl[rows, :], zc[:, 0:LANES])
        for q in range(4):
            d = group * 4 + q
            s3[d] = packed(value[q * BLOCK : (q + 1) * BLOCK], 4)

            @pl.when(d != sec)
            def _():
                e3(d).start()

            @pl.when(d == sec)
            def _():
                r3[d] = s3[d]

    loads[2].start()
    loads[3].start()

    @pl.loop(0, 8)
    def _(q):
        leg_copy(q).wait()

        @pl.loop(0, SHARE * TILES)
        def _(i):
            p = q * SHARE + i // 5
            rows = pl.ds(pl.multiple_of((i % 5) * 16, 16), 16)
            high, low = split(legf[p, rows, :])
            legh[p, rows, :] = high
            legl[p, rows, :] = low

    @pl.loop(1, 16)
    def _(k):
        source = (sec + k) % 16
        remote(
            s3.at[source], r3.at[source], e3_s.at[source], e3_r.at[source], (band, source)
        ).wait_recv()

    for v in range(2):
        for c in range(4):
            north, south = r3[v * 4 + c], r3[8 + v * 4 + c]
            eo[0, v, c] = unpacked(north + south, 5)
            eo[1, v, c] = unpacked(north - south, 5)
    for p in range(BLOCK):
        j, c = p // 4, p % 4
        for s in range(2):
            for v in range(2):
                row = s * 8 + v * 2
                lf[p, row : row + 2, :] = eo[s, v, c, 2 * j : 2 * j + 2, :]
                lf[p, row + 4 : row + 6, :] = eo[s, v, 3 - c, 20 + 2 * j : 22 + 2 * j, :]

    @pl.loop(0, BLOCK)
    def _(p):
        high, low = split(lf[p])
        lb[p, 0:16, :] = high
        lb[p, 16:32, :] = low

    column = lax.broadcasted_iota(jnp.int32, (8, ROWS), 1)

    def masks(p):
        limit = WAVES - (sec * BLOCK + p)
        leading = column < limit
        lag = jnp.where(leading, column, column - limit)
        return leading, (lag & 1) == 1

    def analyse(share):
        results = []
        for i in range(SHARE):
            p = share * SHARE + i
            lhs = lb[p, :, 0:LAT]
            both = dot(lhs, legh[p])
            total = both[0:16] + both[16:32] + dot(lhs[0:16], legl[p])
            leading, odd_rows = masks(p)
            chosen = jnp.where(odd_rows, total[8:16], total[0:8])
            results.append(jnp.where(leading[0:4], chosen[0:4], chosen[4:8]))
        return results

    partner = (z * 2 + 1 - core, sec)
    ahead, behind, across = (z + 1) % 4, (z + 3) % 4, (z + 2) % 4
    up, down = (ahead * 2 + core, sec), (behind * 2 + core, sec)

    def c1(k):
        return remote(pbuf.at[k], cbuf.at[k], c1_s.at[k], c1_r.at[k], partner)

    def share_at(k, which):
        return ((z + 2 + 3 * k + 3 * (k // 2) + 2 * (k // 3)) % 4) * 2 + which

    first, last = pl.ds(0, 3), pl.ds(3, 2)
    half_up = remote(sbuf.at[0, first], rbuf.at[first], c2_s.at[0], c2_r.at[0], up)
    half_down = remote(sbuf.at[0, last], rbuf.at[last], c2_s.at[1], c2_r.at[1], down)
    early_up = remote(sbuf.at[1, last], tbuf.at[0, last], c2_s.at[2], c2_r.at[2], up)
    early_down = remote(sbuf.at[2, first], tbuf.at[1, first], c2_s.at[3], c2_r.at[3], down)
    late_up = remote(sbuf.at[1, first], tbuf.at[0, first], c2_s.at[4], c2_r.at[4], up)
    late_down = remote(sbuf.at[2, last], tbuf.at[1, last], c2_s.at[5], c2_r.at[5], down)

    @pl.loop(0, 8)
    def _(n):
        late = n // 4
        mine = (1 - late) * (n // 2) + late * (n % 2)
        k = (1 - late) * (n % 2) + late * (n // 2)
        values = analyse(share_at(k, core + (1 - mine) * (1 - 2 * core)))

        @pl.when(mine == 0)
        def _():
            for i, value in enumerate(values):
                pbuf[k, i, :, 0:ROWS] = value
            c1(k).start()

        @pl.when(mine == 1)
        def _():
            for i, value in enumerate(values):
                sbuf[k, i, :, 0:ROWS] = value
            c1(k).wait_recv()
            for i in range(SHARE):
                sbuf[k, i] = sbuf[k, i] + cbuf[k, i]

        @pl.when(n == 2)
        def _():
            half_up.start()
            half_down.start()

        @pl.when(n == 3)
        def _():
            early_up.start()

        @pl.when(n == 5)
        def _():
            early_down.start()

        @pl.when(n == 6)
        def _():
            half_up.wait_recv()
            for i in range(3):
                sbuf[1, i] = sbuf[1, i] + rbuf[i]
            late_up.start()
            half_down.wait_recv()
            for i in range(3, SHARE):
                sbuf[2, i] = sbuf[2, i] + rbuf[i]
            late_down.start()

    for copy in (early_up, early_down, late_up, late_down):
        copy.wait_recv()
    first_level = lax.broadcasted_iota(jnp.int32, (4, ROWS), 0) < 2
    level = jnp.where(first_level, damping[0], damping[1])

    @pl.loop(0, SHARE)
    def _(i):
        p = sec * BLOCK + band * SHARE + i
        column4 = column[0:4]
        degree = jnp.where(column4 < WAVES - p, p + column4, column4 - 1)
        ratio = (degree * (degree + 1)).astype(F32) / float(WAVES * WAVES)
        total = (tbuf[0, i] + tbuf[1, i]) + sbuf[3, i]
        gbuf[band, i, :, 0:ROWS] = total[:, 0:ROWS] / (1.0 + level * ratio)

    def gathered(share, rows, sem, to, send, recv):
        ref = gbuf.at[share, rows]
        return remote(ref, ref, send.at[sem], recv.at[sem], to)

    every = pl.ds(0, SHARE)

    def gz(sem, share, rows, to):
        return gathered(share, rows, sem, to, gz_s, gz_r)

    def gp(sem, share, rows):
        return gathered(share, rows, sem, partner, gp_s, gp_r)

    other = 1 - core
    sends = [
        gz(0, band, first, up),
        gz(1, band, last, down),
        gz(2, behind * 2 + core, first, up),
        gz(3, ahead * 2 + core, last, down),
        gz(4, band, last, up),
        gz(5, band, first, down),
        gp(0, band, every),
        gp(1, behind * 2 + core, every),
        gp(2, ahead * 2 + core, every),
        gp(3, across * 2 + core, first),
        gp(4, across * 2 + core, last),
    ]
    arrivals = [
        gz(0, behind * 2 + core, first, up),
        gz(1, ahead * 2 + core, last, down),
        gz(2, across * 2 + core, first, up),
        gz(3, across * 2 + core, last, down),
        gz(4, behind * 2 + core, last, up),
        gz(5, ahead * 2 + core, first, down),
        gp(0, z * 2 + other, every),
        gp(1, behind * 2 + other, every),
        gp(2, ahead * 2 + other, every),
        gp(3, across * 2 + other, first),
        gp(4, across * 2 + other, last),
    ]
    for k in (0, 1, 4, 5, 6):
        sends[k].start()
    upper = lax.broadcasted_iota(jnp.int32, (8, ROWS), 0) >= 4

    def synthesise(share):
        for i in range(SHARE):
            p = share * SHARE + i
            spec = gbuf[share, i, :, 0:ROWS]
            leading, odd_rows = masks(p)
            north = jnp.concatenate([spec, spec], axis=0)
            north = jnp.where(leading != upper, north, 0.0)
            south = jnp.where(odd_rows, -north, north)
            high, low = split(jnp.concatenate([north, south], axis=0))
            both = dot_t(jnp.concatenate([high, low], axis=0), legh[p])
            syn[p, :, 0:LAT] = both[0:16] + both[16:32] + dot_t(high, legl[p])

    def step_share(k):
        late, turn = (k + 6) // 8, (k + 1) % 3
        chip = (z + late * (3 + 2 * turn + 3 * (turn // 2))) % 4
        swap = (k + 3) // 8 + (1 - late) * k
        return chip * 2 + core + swap * (1 - 2 * core)

    @pl.loop(0, 8)
    def _(k):
        @pl.when(k == 1)
        def _():
            arrivals[6].wait_recv()

        @pl.when(k == 2)
        def _():
            for n in (0, 1):
                arrivals[n].wait_recv()
                sends[n + 2].start()
            for n in (4, 5):
                arrivals[n].wait_recv()
                sends[n + 3].start()

        @pl.when(k == 4)
        def _():
            for n in (2, 3):
                arrivals[n].wait_recv()
                sends[n + 7].start()

        @pl.when(k == 5)
        def _():
            arrivals[7].wait_recv()

        @pl.when(k == 6)
        def _():
            arrivals[8].wait_recv()

        @pl.when(k == 7)
        def _():
            arrivals[9].wait_recv()
            arrivals[10].wait_recv()

        synthesise(step_share(k))

    for p in range(BLOCK):
        j, c = p // 4, p % 4
        for h in range(2):
            for v in range(2):
                row = h * 8 + v * 2
                block = (h * 2 + v) * 4
                s4[block + c, 2 * j : 2 * j + 2, :] = syn[p, row : row + 2, :]
                s4[block + 3 - c, 20 + 2 * j : 22 + 2 * j, :] = syn[p, row + 4 : row + 6, :]

    def e4(k):
        to = (sec + k) % 16
        return remote(s4p.at[to], r4.at[sec], e4_s.at[k], e4_r.at[sec], (band, to))

    @pl.loop(1, 16)
    def _(k):
        to = (sec + k) % 16
        s4p[to] = packed(s4[to], 4)
        e4(k).start()

    r4[sec] = packed(s4[sec], 4)
    loads[2].wait()
    loads[3].wait()

    @pl.loop(1, 16)
    def _(k):
        source = (sec + k) % 16
        remote(
            s4p.at[source], r4.at[source], e4_s.at[k], e4_r.at[source], (band, source)
        ).wait_recv()

    @pl.loop(0, 8)
    def _(i):
        pair = jnp.concatenate([unpacked(r4[2 * i], 5), unpacked(r4[2 * i + 1], 5)], axis=0)
        high, low = split(pair)
        start = pl.multiple_of(i * 80, 80)
        yc[pl.ds(start, 80), 0:LANES] = high
        yc[pl.ds(start, 80), LANES : 2 * LANES] = low

    def e5(k, part, half):
        to = (x + k) % 4
        return remote(
            s5.at[part, to, half],
            r5.at[part, x, half],
            e5_s.at[part, half, k],
            e5_r.at[part, half, x],
            (band, y * 4 + to),
        )

    def e5_arrives(k, part, half):
        source = (x + k) % 4
        remote(
            s5.at[part, source, half],
            r5.at[part, source, half],
            e5_s.at[part, half, k],
            e5_r.at[part, half, source],
            (band, y * 4 + source),
        ).wait_recv()

    @pl.loop(0, 8)
    def _(g):
        half, k = g // 4, (g + 1) % 4
        to = (x + k) % 4

        def part_of(part):
            rows = pl.ds(pl.multiple_of((to * 2 + part) * 160 + half * 80, 80), 80)
            both = dot(ih[rows, :], yc[...])
            value = both[:, 0:LANES] + both[:, LANES:] + dot(il[rows, :], yc[:, 0:LANES])
            s5[part, to, half] = packed(value, 7)

            @pl.when(k != 0)
            def _():
                e5(k, part, half).start()

            @pl.when(k == 0)
            def _():
                r5[part, to, half] = s5[part, to, half]

        part_of(0)

        @pl.when(odd)
        def _():
            part_of(1)

    def e6(half, k):
        to = (y + k) % 4
        return remote(
            o6.at[to, half], r6.at[y, half], e6_s.at[half, k], e6_r.at[half, y], (band, to * 4 + x)
        )

    @pl.loop(0, 2)
    def _(half):
        for k in range(1, 4):
            e5_arrives(k, 0, half)

            @pl.when((x + k) % 2 == 1)
            def _():
                e5_arrives(k, 1, half)

        a, c = r5[0, 0, half], r5[0, 2, half]
        b = r5[0, 1, half] + r5[0, 3, half]
        d = r5[1, 3, half] - r5[1, 1, half]
        o6[0, half] = (a + c) + b
        o6[1, half] = (a - c) + d
        o6[2, half] = (a + c) - b
        o6[3, half] = (a - c) - d
        for k in range(1, 4):
            e6(half, k).start()
        out[y, half] = unpacked(o6[y, half], 10)

    @pl.loop(0, 2)
    def _(half):
        for k in range(1, 4):
            source = (y + k) % 4
            remote(
                o6.at[source, half],
                r6.at[source, half],
                e6_s.at[half, k],
                e6_r.at[half, source],
                (band, source * 4 + x),
            ).wait_recv()
            out[source, half] = unpacked(r6[source, half], 10)

    for i in range(TILES):
        halo(i).wait_send()

    @pl.loop(0, TILES)
    def _(t):
        for k in range(1, 4):
            e1(t, k).wait_send()
            e2(t, k, 0).wait_send()

            @pl.when((x + k) % 2 == 1)
            def _():
                e2(t, k, 1).wait_send()

    @pl.loop(1, 16)
    def _(k):
        e3((sec + k) % 16).wait_send()
        e4(k).wait_send()

    for k in range(4):
        c1(k).wait_send()
    for copy in (half_up, half_down, early_up, early_down, late_up, late_down, *sends):
        copy.wait_send()
    for k in range(1, 4):
        for half in range(2):
            e5(k, 0, half).wait_send()

            @pl.when(odd)
            def _():
                e5(k, 1, half).wait_send()

            e6(half, k).wait_send()


def local(field, depart, interp_weight, legendre, damping):
    forward, inverse = tables()
    constants = [jnp.asarray(t) for t in (*halves(forward), *halves(inverse))]
    vmem = pl.BlockSpec(memory_space=pltpu.VMEM)
    hbm = pl.BlockSpec(memory_space=pl.ANY)
    scratch = [
        pltpu.VMEM((2, 2, 320, LANES), F32),
        pltpu.VMEM((5, 4, PACK, LANES), F32),
        pltpu.VMEM((5, 4, PACK, LANES), F32),
        pltpu.VMEM((2, 5, 64, TILE, LAT), BF16),
        pltpu.VMEM((2, 64, LAT), F32),
        pltpu.VMEM((4, TILE, LANES), F32),
        pltpu.VMEM((4, 5, PACK, LANES), F32),
        pltpu.VMEM((4, 5, PACK, LANES), F32),
        pltpu.VMEM((4, 5, PACK, LANES), F32),
        pltpu.VMEM((2, 4, 5, PACK, LANES), F32),
        pltpu.VMEM((1280, 2 * LANES), BF16),
        pltpu.VMEM((640, 1280), BF16),
        pltpu.VMEM((640, 1280), BF16),
        pltpu.VMEM((1280, 640), BF16),
        pltpu.VMEM((1280, 640), BF16),
        pltpu.VMEM((16, 32, LANES), F32),
        pltpu.VMEM((16, 32, LANES), F32),
        pltpu.VMEM((2, 2, 4, BLOCK, LANES), F32),
        pltpu.VMEM((BLOCK, 16, LANES), F32),
        pltpu.VMEM((BLOCK, 32, LANES), BF16),
        pltpu.VMEM((BLOCK, LAT, ROWS), F32),
        pltpu.VMEM((BLOCK, LAT, ROWS), BF16),
        pltpu.VMEM((BLOCK, LAT, ROWS), BF16),
        pltpu.VMEM((4, SHARE, 4, WIDE), F32),
        pltpu.VMEM((4, SHARE, 4, WIDE), F32),
        pltpu.VMEM((4, SHARE, 4, WIDE), F32),
        pltpu.VMEM((SHARE, 4, WIDE), F32),
        pltpu.VMEM((2, SHARE, 4, WIDE), F32),
        pltpu.VMEM((8, SHARE, 4, WIDE), F32),
        pltpu.VMEM((BLOCK, 16, LANES), F32),
        pltpu.VMEM((16, BLOCK, LANES), F32),
        pltpu.VMEM((16, 32, LANES), F32),
        pltpu.VMEM((16, 32, LANES), F32),
        pltpu.VMEM((640, 2 * LANES), BF16),
        pltpu.VMEM((2, 4, 2, 56, LANES), F32),
        pltpu.VMEM((2, 4, 2, 56, LANES), F32),
        pltpu.VMEM((4, 2, 56, LANES), F32),
        pltpu.VMEM((4, 2, 56, LANES), F32),
    ]
    dma = pltpu.SemaphoreType.DMA
    scratch += [
        dma((2, 5)),
        dma((8,)),
        dma((4,)),
        dma((5,)),
        dma((5,)),
        dma((5, 4)),
        dma((5, 4)),
        dma((2, 5, 4)),
        dma((2, 5, 4)),
        dma((16,)),
        dma((16,)),
        dma((4,)),
        dma((4,)),
        dma((6,)),
        dma((6,)),
        dma((6,)),
        dma((6,)),
        dma((5,)),
        dma((5,)),
        dma((16,)),
        dma((16,)),
        dma((2, 2, 4)),
        dma((2, 2, 4)),
        dma((2, 4)),
        dma((2, 4)),
    ]
    grid = pl.pallas_call(
        kernel,
        out_shape=jax.ShapeDtypeStruct((4, 2, 80, LANES), F32),
        in_specs=[vmem, vmem, hbm, hbm, pl.BlockSpec(memory_space=pltpu.SMEM)] + [hbm] * 4,
        out_specs=vmem,
        scratch_shapes=scratch,
        compiler_params=pltpu.CompilerParams(
            collective_id=0, has_side_effects=True, vmem_limit_bytes=62 * 1024 * 1024
        ),
    )(
        jnp.transpose(field, (0, 2, 3, 1)),
        jnp.transpose(depart, (2, 0, 1)),
        jnp.transpose(interp_weight, (0, 2, 3, 4, 1)),
        legendre,
        damping,
        *constants,
    )
    grid = grid.reshape(2, 2, 160, LANES)[..., 0:LAT]
    return jnp.transpose(grid, (0, 3, 1, 2))


def solution(mesh):
    placed = (
        P(None, "band", None, "sector"),
        P(None, "band", "sector"),
        P(None, "band", "sector", None, None),
        P("sector", "band", None),
        P(),
    )
    return jax.shard_map(
        local, mesh=mesh, in_specs=placed, out_specs=P(None, "band", None, "sector"), check_vma=False
    )
```

```python
import math

import jax
import jax.numpy as jnp
import ml_dtypes
import numpy as np
from jax import lax
from jax.experimental import pallas as pl
from jax.experimental.pallas import tpu as pltpu
from jax.sharding import PartitionSpec as P

F32 = jnp.float32
BF16 = jnp.bfloat16
LON = 2560
WAVES = 1280
ROWS = WAVES + 1
WIDE = WAVES + 128
TILE = 32
LANES = 128
LAT = 80
BLOCK = 40
SHARE = 5
TILES = 5
PACK = 24


def halves(table):
    high = table.astype(ml_dtypes.bfloat16)
    low = (table - high.astype(np.float64)).astype(ml_dtypes.bfloat16)
    return high, low


def tables():
    cls = np.arange(4)[:, None, None]
    d = np.arange(16)[None, :, None]
    j = np.arange(10)[None, None, :]
    lower = BLOCK * d + 4 * j + cls
    upper = WAVES - 4 - BLOCK * d - 4 * j + cls
    m = np.stack([lower, upper], axis=2)
    xi = np.arange(640)
    angle = 2.0 * math.pi / LON * ((m[..., None] * xi) % LON)
    cos, sin = np.cos(angle), np.sin(angle)
    sign = np.where(np.arange(4) == 3, -1.0, 1.0)[:, None, None, None, None]
    real = np.concatenate([cos, sin * sign], axis=-1)
    imag = np.concatenate([-sin, cos * sign], axis=-1)
    forward = np.stack([real, imag], axis=4).reshape(4, 640, 1280) / LON
    scale = np.where(m == 0, 1.0, 2.0)[..., None]
    cos, sin = cos * scale, sin * scale
    real = np.stack([cos, -sin], axis=4).reshape(4, 640, 640)
    imag = np.stack([sin, cos], axis=4).reshape(4, 640, 640)
    both = np.stack([real, imag], axis=1)
    both = both.reshape(4, 2, 640, 4, 2, 80).transpose(0, 4, 1, 3, 5, 2)
    inverse = both.reshape(4, 1280, 640)
    return forward, inverse


def split(value):
    high = value.astype(BF16)
    low = (value - high.astype(F32)).astype(BF16)
    return high, low


def dot(a, b):
    return jnp.dot(a, b, preferred_element_type=F32)


def dot_t(a, b):
    return lax.dot_general(a, b, (((1,), (1,)), ((), ())), preferred_element_type=F32)


def moves(count, base):
    found, slot, used = [], 0, 0
    for group in range(base, count):
        lane = 0
        while lane < LAT:
            n = min(LAT - lane, LANES - LAT - used)
            found.append((group, lane, n, slot, LAT + used))
            lane, used = lane + n, used + n
            if used == LANES - LAT:
                slot, used = slot + 1, 0
    return found


def between(start, n):
    lane = lax.broadcasted_iota(jnp.int32, (8, LANES), 1)
    return (lane >= start) & (lane < start + n)


def packed(value, base):
    groups = [value[8 * g : 8 * g + 8] for g in range(value.shape[0] // 8)]
    kept = groups[:base]
    for group, lane, n, slot, to in moves(len(groups), base):
        moved = pltpu.roll(groups[group], to - lane, 1)
        kept[slot] = jnp.where(between(to, n), moved, kept[slot])
    return jnp.concatenate(kept, axis=0)


def unpacked(value, count):
    base = value.shape[0] // 8
    groups = [value[8 * g : 8 * g + 8] for g in range(base)]
    groups += [jnp.zeros((8, LANES), F32)] * (count - base)
    for group, lane, n, slot, to in moves(count, base):
        moved = pltpu.roll(groups[slot], LANES + lane - to, 1)
        groups[group] = jnp.where(between(lane, n), moved, groups[group])
    return jnp.concatenate(groups, axis=0)


def remote(src, dst, send, recv, device):
    return pltpu.make_async_remote_copy(
        src_ref=src,
        dst_ref=dst,
        send_sem=send,
        recv_sem=recv,
        device_id=device,
        device_id_type=pl.DeviceIdType.MESH,
    )


def kernel(
    field,
    depart,
    weight,
    legendre,
    damping,
    fwd_high,
    fwd_low,
    inv_high,
    inv_low,
    out,
    ext,
    hs,
    hr,
    wbuf,
    win,
    adv,
    sent,
    r1,
    s2,
    r2,
    zc,
    fh,
    fl,
    ih,
    il,
    s3,
    r3,
    eo,
    lf,
    lb,
    legf,
    legh,
    legl,
    pbuf,
    cbuf,
    sbuf,
    rbuf,
    tbuf,
    gbuf,
    syn,
    s4,
    s4p,
    r4,
    yc,
    s5,
    r5,
    o6,
    r6,
    w_sem,
    leg_sem,
    tab_sem,
    halo_s,
    halo_r,
    e1_s,
    e1_r,
    e2_s,
    e2_r,
    e3_s,
    e3_r,
    c1_s,
    c1_r,
    c2_s,
    c2_r,
    gz_s,
    gz_r,
    gp_s,
    gp_r,
    e4_s,
    e4_r,
    e5_s,
    e5_r,
    e6_s,
    e6_r,
):
    band = lax.axis_index("band")
    sec = lax.axis_index("sector")
    y, x = sec // 4, sec % 4
    z, core = band // 2, band % 2
    odd = x % 2 == 1

    def w_copy(h, t):
        return pltpu.make_async_copy(weight.at[h, t], wbuf.at[h, t], w_sem.at[h, t])

    @pl.loop(0, TILES)
    def _(t):
        for h in range(2):
            w_copy(h, t).start()

    loads = [
        pltpu.make_async_copy(src.at[x], dst, tab_sem.at[i])
        for i, (src, dst) in enumerate(
            [(fwd_high, fh), (fwd_low, fl), (inv_high, ih), (inv_low, il)]
        )
    ]
    loads[0].start()
    loads[1].start()

    def leg_copy(q):
        rows = pl.ds(q * SHARE, SHARE)
        return pltpu.make_async_copy(legendre.at[rows], legf.at[rows], leg_sem.at[q])

    barrier = pltpu.get_barrier_semaphore()

    def greet(device):
        pl.semaphore_signal(barrier, inc=1, device_id=device, device_id_type=pl.DeviceIdType.MESH)

    for k in range(1, 16):
        greet((band, (sec + k) % 16))
    for k in range(1, 4):
        greet((((z + k) % 4) * 2 + core, sec))
    greet((z * 2 + 1 - core, sec))

    for h in range(2):
        for v in range(2):
            ext[h, v, 64:224, 0:LAT] = field[h, v]
            for i, start in enumerate((64, 192, 96, 160, 128)):
                hs[i, h * 2 + v] = packed(ext[h, v, start : start + TILE, :], 3)

    pl.semaphore_wait(barrier, 19)

    def halo(i):
        to = (sec + 15 - 14 * (i % 2)) % 16
        return remote(hs.at[i], hr.at[i], halo_s.at[i], halo_r.at[i], (band, to))

    for i in range(TILES):
        halo(i).start()
    adv[...] = jnp.zeros_like(adv)

    @pl.when(jnp.logical_not(odd))
    def _():
        r2[1] = jnp.zeros_like(r2[1])

    @pl.loop(0, 8)
    def _(q):
        leg_copy(q).start(priority=1)


    def e1(t, k):
        to = (y + k) % 4
        return remote(
            sent.at[to, t], r1.at[y, t], e1_s.at[t, k], e1_r.at[t, y], (band, to * 4 + x)
        )

    def e1_arrives(t, k):
        source = (y + k) % 4
        remote(
            sent.at[source, t],
            r1.at[source, t],
            e1_s.at[t, k],
            e1_r.at[t, source],
            (band, source * 4 + x),
        ).wait_recv()

    def e2(t, k, part):
        to = (x + k) % 4
        src = s2.at[3, t] if part else s2.at[to - 2 * (to // 3), t]
        return remote(
            src,
            r2.at[part, x, t],
            e2_s.at[part, t, k],
            e2_r.at[part, t, x],
            (band, y * 4 + to),
        )

    def e2_arrives(t, k, part):
        source = (x + k) % 4
        remote(
            s2.at[0, t],
            r2.at[part, source, t],
            e2_s.at[part, t, k],
            e2_r.at[part, t, source],
            (band, y * 4 + source),
        ).wait_recv()

    def tile_of(i):
        return 2 + (1 - 2 * (i % 2)) * ((i + 1) // 2)

    def advect(i):
        t = tile_of(i)
        halo(i).wait_recv()
        start = (1 - i % 2) * (224 + 16 * i) + (i % 2) * (48 - 16 * i)
        rows = pl.ds(pl.multiple_of(start, TILE), TILE)
        for h in range(2):
            for v in range(2):
                ext[h, v, rows, :] = unpacked(hr[i, h * 2 + v], 4)
        for h in range(2):
            w_copy(h, t).wait()
            dep = depart[t, h : h + 1, :]
            for v in range(2):
                window = ext[h, v, pl.ds(pl.multiple_of(t * TILE, TILE), 64), 0:LAT]
                for offset in range(-1, 3):
                    start = pl.multiple_of((t + offset + 2) * TILE, TILE)
                    candidate = ext[h, v, pl.ds(start, 64), 0:LAT]
                    window = jnp.where(dep == offset, candidate, window)
                win[v] = window
            total = [jnp.zeros((TILE, LAT), F32) for _ in range(2)]
            for j in range(64):
                w = wbuf[h, t, j].astype(F32)
                for v in range(2):
                    total[v] = total[v] + win[v, j : j + 1, :] * w
            for v in range(2):
                adv[h * 2 + v, :, 0:LAT] = total[v]
                sent[h * 2 + v, t] = packed(adv[h * 2 + v], 3)
        for k in range(1, 4):
            e1(t, k).start()
        r1[y, t] = sent[y, t]

    def radix(i):
        t = tile_of(i)
        for k in range(1, 4):
            e1_arrives(t, k)
        a, b, c, d = r1[0, t], r1[1, t], r1[2, t], r1[3, t]
        s2[0, t] = (a + c) + (b + d)
        s2[1, t] = a - c
        s2[2, t] = (a + c) - (b + d)
        s2[3, t] = d - b
        for k in range(1, 4):
            e2(t, k, 0).start()

            @pl.when((x + k) % 2 == 1)
            def _():
                e2(t, k, 1).start()

        r2[0, x, t] = s2[x - 2 * (x // 3), t]

        @pl.when(odd)
        def _():
            r2[1, x, t] = s2[3, t]

    pl.loop(0, TILES)(advect)
    pl.loop(0, TILES)(radix)

    @pl.loop(0, TILES)
    def _(i):
        t = tile_of(i)
        for k in range(1, 4):
            e2_arrives(t, k, 0)

            @pl.when(odd)
            def _():
                e2_arrives(t, k, 1)

        for part in range(2):
            for source in range(4):
                high, low = split(unpacked(r2[part, source, t], 4))
                start = pl.multiple_of((part * 4 + source) * 160 + t * TILE, TILE)
                zc[pl.ds(start, TILE), 0:LANES] = high
                zc[pl.ds(start, TILE), LANES : 2 * LANES] = low

    loads[0].wait()
    loads[1].wait()

    def e3(d):
        return remote(s3.at[d], r3.at[sec], e3_s.at[d], e3_r.at[sec], (band, d))

    @pl.loop(0, 2)
    def _(g):
        group = (g + sec // 8) % 2
        rows = pl.ds(pl.multiple_of(group * 320, 320), 320)
        both = dot(fh[rows, :], zc[...])
        value = both[:, 0:LANES] + both[:, LANES:] + dot(fl[rows, :], zc[:, 0:LANES])
        for q in range(8):
            d = group * 8 + q
            s3[d] = packed(value[q * BLOCK : (q + 1) * BLOCK], 4)

            @pl.when(d != sec)
            def _():
                e3(d).start()

            @pl.when(d == sec)
            def _():
                r3[d] = s3[d]

    loads[2].start()
    loads[3].start()

    @pl.loop(0, 8)
    def _(q):
        leg_copy(q).wait()

        @pl.loop(0, SHARE * TILES)
        def _(i):
            p = q * SHARE + i // 5
            rows = pl.ds(pl.multiple_of((i % 5) * 16, 16), 16)
            high, low = split(legf[p, rows, :])
            legh[p, rows, :] = high
            legl[p, rows, :] = low

    @pl.loop(1, 16)
    def _(k):
        source = (sec + k) % 16
        remote(
            s3.at[source], r3.at[source], e3_s.at[source], e3_r.at[source], (band, source)
        ).wait_recv()

    for v in range(2):
        for c in range(4):
            north, south = r3[v * 4 + c], r3[8 + v * 4 + c]
            eo[0, v, c] = unpacked(north + south, 5)
            eo[1, v, c] = unpacked(north - south, 5)
    for p in range(BLOCK):
        j, c = p // 4, p % 4
        for s in range(2):
            for v in range(2):
                row = s * 8 + v * 2
                lf[p, row : row + 2, :] = eo[s, v, c, 2 * j : 2 * j + 2, :]
                lf[p, row + 4 : row + 6, :] = eo[s, v, 3 - c, 20 + 2 * j : 22 + 2 * j, :]

    @pl.loop(0, BLOCK)
    def _(p):
        high, low = split(lf[p])
        lb[p, 0:16, :] = high
        lb[p, 16:32, :] = low

    column = lax.broadcasted_iota(jnp.int32, (8, ROWS), 1)

    def masks(p):
        limit = WAVES - (sec * BLOCK + p)
        leading = column < limit
        lag = jnp.where(leading, column, column - limit)
        return leading, (lag & 1) == 1

    def analyse(share):
        results = []
        for i in range(SHARE):
            p = share * SHARE + i
            lhs = lb[p, :, 0:LAT]
            both = dot(lhs, legh[p])
            total = both[0:16] + both[16:32] + dot(lhs[0:16], legl[p])
            leading, odd_rows = masks(p)
            chosen = jnp.where(odd_rows, total[8:16], total[0:8])
            results.append(jnp.where(leading[0:4], chosen[0:4], chosen[4:8]))
        return results

    partner = (z * 2 + 1 - core, sec)
    ahead, behind, across = (z + 1) % 4, (z + 3) % 4, (z + 2) % 4
    up, down = (ahead * 2 + core, sec), (behind * 2 + core, sec)

    def c1(k):
        return remote(pbuf.at[k], cbuf.at[k], c1_s.at[k], c1_r.at[k], partner)

    def share_at(k, which):
        return ((z + 2 + 3 * k + 3 * (k // 2) + 2 * (k // 3)) % 4) * 2 + which

    first, last = pl.ds(0, 3), pl.ds(3, 2)
    half_up = remote(sbuf.at[0, first], rbuf.at[first], c2_s.at[0], c2_r.at[0], up)
    half_down = remote(sbuf.at[0, last], rbuf.at[last], c2_s.at[1], c2_r.at[1], down)
    early_up = remote(sbuf.at[1, last], tbuf.at[0, last], c2_s.at[2], c2_r.at[2], up)
    early_down = remote(sbuf.at[2, first], tbuf.at[1, first], c2_s.at[3], c2_r.at[3], down)
    late_up = remote(sbuf.at[1, first], tbuf.at[0, first], c2_s.at[4], c2_r.at[4], up)
    late_down = remote(sbuf.at[2, last], tbuf.at[1, last], c2_s.at[5], c2_r.at[5], down)

    @pl.loop(0, 8)
    def _(n):
        late = n // 4
        mine = (1 - late) * (n // 2) + late * (n % 2)
        k = (1 - late) * (n % 2) + late * (n // 2)
        values = analyse(share_at(k, core + (1 - mine) * (1 - 2 * core)))

        @pl.when(mine == 0)
        def _():
            for i, value in enumerate(values):
                pbuf[k, i, :, 0:ROWS] = value
            c1(k).start()

        @pl.when(mine == 1)
        def _():
            for i, value in enumerate(values):
                sbuf[k, i, :, 0:ROWS] = value
            c1(k).wait_recv()
            for i in range(SHARE):
                sbuf[k, i] = sbuf[k, i] + cbuf[k, i]

        @pl.when(n == 2)
        def _():
            half_up.start()
            half_down.start()

        @pl.when(n == 3)
        def _():
            early_up.start()

        @pl.when(n == 5)
        def _():
            early_down.start()

        @pl.when(n == 6)
        def _():
            half_up.wait_recv()
            for i in range(3):
                sbuf[1, i] = sbuf[1, i] + rbuf[i]
            late_up.start()
            half_down.wait_recv()
            for i in range(3, SHARE):
                sbuf[2, i] = sbuf[2, i] + rbuf[i]
            late_down.start()

    for copy in (early_up, early_down, late_up, late_down):
        copy.wait_recv()
    first_level = lax.broadcasted_iota(jnp.int32, (4, ROWS), 0) < 2
    level = jnp.where(first_level, damping[0], damping[1])

    @pl.loop(0, SHARE)
    def _(i):
        p = sec * BLOCK + band * SHARE + i
        column4 = column[0:4]
        degree = jnp.where(column4 < WAVES - p, p + column4, column4 - 1)
        ratio = (degree * (degree + 1)).astype(F32) / float(WAVES * WAVES)
        total = (tbuf[0, i] + tbuf[1, i]) + sbuf[3, i]
        gbuf[band, i, :, 0:ROWS] = total[:, 0:ROWS] / (1.0 + level * ratio)

    def gathered(share, rows, sem, to, send, recv):
        ref = gbuf.at[share, rows]
        return remote(ref, ref, send.at[sem], recv.at[sem], to)

    every = pl.ds(0, SHARE)

    def gz(sem, share, rows, to):
        return gathered(share, rows, sem, to, gz_s, gz_r)

    def gp(sem, share, rows):
        return gathered(share, rows, sem, partner, gp_s, gp_r)

    other = 1 - core
    sends = [
        gz(0, band, first, up),
        gz(1, band, last, down),
        gz(2, behind * 2 + core, first, up),
        gz(3, ahead * 2 + core, last, down),
        gz(4, band, last, up),
        gz(5, band, first, down),
        gp(0, band, every),
        gp(1, behind * 2 + core, every),
        gp(2, ahead * 2 + core, every),
        gp(3, across * 2 + core, first),
        gp(4, across * 2 + core, last),
    ]
    arrivals = [
        gz(0, behind * 2 + core, first, up),
        gz(1, ahead * 2 + core, last, down),
        gz(2, across * 2 + core, first, up),
        gz(3, across * 2 + core, last, down),
        gz(4, behind * 2 + core, last, up),
        gz(5, ahead * 2 + core, first, down),
        gp(0, z * 2 + other, every),
        gp(1, behind * 2 + other, every),
        gp(2, ahead * 2 + other, every),
        gp(3, across * 2 + other, first),
        gp(4, across * 2 + other, last),
    ]
    for k in (0, 1, 4, 5, 6):
        sends[k].start()
    upper = lax.broadcasted_iota(jnp.int32, (8, ROWS), 0) >= 4

    def synthesise(share):
        for i in range(SHARE):
            p = share * SHARE + i
            spec = gbuf[share, i, :, 0:ROWS]
            leading, odd_rows = masks(p)
            north = jnp.concatenate([spec, spec], axis=0)
            north = jnp.where(leading != upper, north, 0.0)
            south = jnp.where(odd_rows, -north, north)
            high, low = split(jnp.concatenate([north, south], axis=0))
            both = dot_t(jnp.concatenate([high, low], axis=0), legh[p])
            syn[p, :, 0:LAT] = both[0:16] + both[16:32] + dot_t(high, legl[p])

    def step_share(k):
        late, turn = (k + 6) // 8, (k + 1) % 3
        chip = (z + late * (3 + 2 * turn + 3 * (turn // 2))) % 4
        swap = (k + 3) // 8 + (1 - late) * k
        return chip * 2 + core + swap * (1 - 2 * core)

    @pl.loop(0, 8)
    def _(k):
        @pl.when(k == 1)
        def _():
            arrivals[6].wait_recv()

        @pl.when(k == 2)
        def _():
            for n in (0, 1):
                arrivals[n].wait_recv()
                sends[n + 2].start()
            for n in (4, 5):
                arrivals[n].wait_recv()
                sends[n + 3].start()

        @pl.when(k == 4)
        def _():
            for n in (2, 3):
                arrivals[n].wait_recv()
                sends[n + 7].start()

        @pl.when(k == 5)
        def _():
            arrivals[7].wait_recv()

        @pl.when(k == 6)
        def _():
            arrivals[8].wait_recv()

        @pl.when(k == 7)
        def _():
            arrivals[9].wait_recv()
            arrivals[10].wait_recv()

        synthesise(step_share(k))

    for p in range(BLOCK):
        j, c = p // 4, p % 4
        for h in range(2):
            for v in range(2):
                row = h * 8 + v * 2
                block = (h * 2 + v) * 4
                s4[block + c, 2 * j : 2 * j + 2, :] = syn[p, row : row + 2, :]
                s4[block + 3 - c, 20 + 2 * j : 22 + 2 * j, :] = syn[p, row + 4 : row + 6, :]

    def e4(k):
        to = (sec + k) % 16
        return remote(s4p.at[to], r4.at[sec], e4_s.at[k], e4_r.at[sec], (band, to))

    @pl.loop(1, 16)
    def _(k):
        to = (sec + k) % 16
        s4p[to] = packed(s4[to], 4)
        e4(k).start()

    r4[sec] = packed(s4[sec], 4)
    loads[2].wait()
    loads[3].wait()

    @pl.loop(0, 8)
    def _(n):
        i = (sec // 2 + n) % 8
        for source in (2 * i, 2 * i + 1):

            @pl.when(source != sec)
            def _():
                remote(
                    s4p.at[source], r4.at[source], e4_s.at[0], e4_r.at[source], (band, source)
                ).wait_recv()

        pair = jnp.concatenate([unpacked(r4[2 * i], 5), unpacked(r4[2 * i + 1], 5)], axis=0)
        high, low = split(pair)
        start = pl.multiple_of(i * 80, 80)
        yc[pl.ds(start, 80), 0:LANES] = high
        yc[pl.ds(start, 80), LANES : 2 * LANES] = low

    def e5(k, part, half):
        to = (x + k) % 4
        return remote(
            s5.at[part, to, half],
            r5.at[part, x, half],
            e5_s.at[part, half, k],
            e5_r.at[part, half, x],
            (band, y * 4 + to),
        )

    def e5_arrives(k, part, half):
        source = (x + k) % 4
        remote(
            s5.at[part, source, half],
            r5.at[part, source, half],
            e5_s.at[part, half, k],
            e5_r.at[part, half, source],
            (band, y * 4 + source),
        ).wait_recv()

    @pl.loop(0, 2)
    def _(half):
        def part_of(part):
            rows = pl.ds(pl.multiple_of(half * 640 + part * 320, 320), 320)
            both = dot(ih[rows, :], yc[...])
            value = both[:, 0:LANES] + both[:, LANES:] + dot(il[rows, :], yc[:, 0:LANES])
            for to in range(4):
                s5[part, to, half] = packed(value[to * 80 : (to + 1) * 80], 7)

                @pl.when(to != x)
                def _():
                    e5((to - x + 4) % 4, part, half).start()

                @pl.when(to == x)
                def _():
                    r5[part, to, half] = s5[part, to, half]

        part_of(0)

        @pl.when(odd)
        def _():
            part_of(1)

    def e6(half, k):
        to = (y + k) % 4
        return remote(
            o6.at[to, half], r6.at[y, half], e6_s.at[half, k], e6_r.at[half, y], (band, to * 4 + x)
        )

    @pl.loop(0, 2)
    def _(half):
        for k in range(1, 4):
            e5_arrives(k, 0, half)

            @pl.when((x + k) % 2 == 1)
            def _():
                e5_arrives(k, 1, half)

        a, c = r5[0, 0, half], r5[0, 2, half]
        b = r5[0, 1, half] + r5[0, 3, half]
        d = r5[1, 3, half] - r5[1, 1, half]
        o6[0, half] = (a + c) + b
        o6[1, half] = (a - c) + d
        o6[2, half] = (a + c) - b
        o6[3, half] = (a - c) - d
        for k in range(1, 4):
            e6(half, k).start()
        out[y, half] = unpacked(o6[y, half], 10)

    @pl.loop(0, 2)
    def _(half):
        for k in range(1, 4):
            source = (y + k) % 4
            remote(
                o6.at[source, half],
                r6.at[source, half],
                e6_s.at[half, k],
                e6_r.at[half, source],
                (band, source * 4 + x),
            ).wait_recv()
            out[source, half] = unpacked(r6[source, half], 10)

    for i in range(TILES):
        halo(i).wait_send()

    @pl.loop(0, TILES)
    def _(t):
        for k in range(1, 4):
            e1(t, k).wait_send()
            e2(t, k, 0).wait_send()

            @pl.when((x + k) % 2 == 1)
            def _():
                e2(t, k, 1).wait_send()

    @pl.loop(1, 16)
    def _(k):
        e3((sec + k) % 16).wait_send()
        e4(k).wait_send()

    for k in range(4):
        c1(k).wait_send()
    for copy in (half_up, half_down, early_up, early_down, late_up, late_down, *sends):
        copy.wait_send()
    for k in range(1, 4):
        for half in range(2):
            e5(k, 0, half).wait_send()

            @pl.when(odd)
            def _():
                e5(k, 1, half).wait_send()

            e6(half, k).wait_send()


def local(field, depart, interp_weight, legendre, damping):
    forward, inverse = tables()
    constants = [jnp.asarray(t) for t in (*halves(forward), *halves(inverse))]
    vmem = pl.BlockSpec(memory_space=pltpu.VMEM)
    hbm = pl.BlockSpec(memory_space=pl.ANY)
    scratch = [
        pltpu.VMEM((2, 2, 320, LANES), F32),
        pltpu.VMEM((5, 4, PACK, LANES), F32),
        pltpu.VMEM((5, 4, PACK, LANES), F32),
        pltpu.VMEM((2, 5, 64, TILE, LAT), BF16),
        pltpu.VMEM((2, 64, LAT), F32),
        pltpu.VMEM((4, TILE, LANES), F32),
        pltpu.VMEM((4, 5, PACK, LANES), F32),
        pltpu.VMEM((4, 5, PACK, LANES), F32),
        pltpu.VMEM((4, 5, PACK, LANES), F32),
        pltpu.VMEM((2, 4, 5, PACK, LANES), F32),
        pltpu.VMEM((1280, 2 * LANES), BF16),
        pltpu.VMEM((640, 1280), BF16),
        pltpu.VMEM((640, 1280), BF16),
        pltpu.VMEM((1280, 640), BF16),
        pltpu.VMEM((1280, 640), BF16),
        pltpu.VMEM((16, 32, LANES), F32),
        pltpu.VMEM((16, 32, LANES), F32),
        pltpu.VMEM((2, 2, 4, BLOCK, LANES), F32),
        pltpu.VMEM((BLOCK, 16, LANES), F32),
        pltpu.VMEM((BLOCK, 32, LANES), BF16),
        pltpu.VMEM((BLOCK, LAT, ROWS), F32),
        pltpu.VMEM((BLOCK, LAT, ROWS), BF16),
        pltpu.VMEM((BLOCK, LAT, ROWS), BF16),
        pltpu.VMEM((4, SHARE, 4, WIDE), F32),
        pltpu.VMEM((4, SHARE, 4, WIDE), F32),
        pltpu.VMEM((4, SHARE, 4, WIDE), F32),
        pltpu.VMEM((SHARE, 4, WIDE), F32),
        pltpu.VMEM((2, SHARE, 4, WIDE), F32),
        pltpu.VMEM((8, SHARE, 4, WIDE), F32),
        pltpu.VMEM((BLOCK, 16, LANES), F32),
        pltpu.VMEM((16, BLOCK, LANES), F32),
        pltpu.VMEM((16, 32, LANES), F32),
        pltpu.VMEM((16, 32, LANES), F32),
        pltpu.VMEM((640, 2 * LANES), BF16),
        pltpu.VMEM((2, 4, 2, 56, LANES), F32),
        pltpu.VMEM((2, 4, 2, 56, LANES), F32),
        pltpu.VMEM((4, 2, 56, LANES), F32),
        pltpu.VMEM((4, 2, 56, LANES), F32),
    ]
    dma = pltpu.SemaphoreType.DMA
    scratch += [
        dma((2, 5)),
        dma((8,)),
        dma((4,)),
        dma((5,)),
        dma((5,)),
        dma((5, 4)),
        dma((5, 4)),
        dma((2, 5, 4)),
        dma((2, 5, 4)),
        dma((16,)),
        dma((16,)),
        dma((4,)),
        dma((4,)),
        dma((6,)),
        dma((6,)),
        dma((6,)),
        dma((6,)),
        dma((5,)),
        dma((5,)),
        dma((16,)),
        dma((16,)),
        dma((2, 2, 4)),
        dma((2, 2, 4)),
        dma((2, 4)),
        dma((2, 4)),
    ]
    grid = pl.pallas_call(
        kernel,
        out_shape=jax.ShapeDtypeStruct((4, 2, 80, LANES), F32),
        in_specs=[vmem, vmem, hbm, hbm, pl.BlockSpec(memory_space=pltpu.SMEM)] + [hbm] * 4,
        out_specs=vmem,
        scratch_shapes=scratch,
        compiler_params=pltpu.CompilerParams(
            collective_id=0, has_side_effects=True, vmem_limit_bytes=62 * 1024 * 1024
        ),
    )(
        jnp.transpose(field, (0, 2, 3, 1)),
        jnp.transpose(depart, (2, 0, 1)),
        jnp.transpose(interp_weight, (0, 2, 3, 4, 1)),
        legendre,
        damping,
        *constants,
    )
    grid = grid.reshape(2, 2, 160, LANES)[..., 0:LAT]
    return jnp.transpose(grid, (0, 3, 1, 2))


def solution(mesh):
    placed = (
        P(None, "band", None, "sector"),
        P(None, "band", "sector"),
        P(None, "band", "sector", None, None),
        P("sector", "band", None),
        P(),
    )
    return jax.shard_map(
        local, mesh=mesh, in_specs=placed, out_specs=P(None, "band", None, "sector"), check_vma=False
    )
```

```python
import math

import jax
import jax.numpy as jnp
import ml_dtypes
import numpy as np
from jax import lax
from jax.experimental import pallas as pl
from jax.experimental.pallas import tpu as pltpu
from jax.sharding import PartitionSpec as P

F32 = jnp.float32
BF16 = jnp.bfloat16
LON = 2560
WAVES = 1280
ROWS = WAVES + 1
WIDE = WAVES + 128
TILE = 32
LANES = 128
LAT = 80
BLOCK = 40
SHARE = 5
TILES = 5
PACK = 24


def halves(table):
    high = table.astype(ml_dtypes.bfloat16)
    low = (table - high.astype(np.float64)).astype(ml_dtypes.bfloat16)
    return high, low


def tables():
    cls = np.arange(4)[:, None, None]
    d = np.arange(16)[None, :, None]
    j = np.arange(10)[None, None, :]
    lower = BLOCK * d + 4 * j + cls
    upper = WAVES - 4 - BLOCK * d - 4 * j + cls
    m = np.stack([lower, upper], axis=2)
    xi = np.arange(640)
    angle = 2.0 * math.pi / LON * ((m[..., None] * xi) % LON)
    cos, sin = np.cos(angle), np.sin(angle)
    sign = np.where(np.arange(4) == 3, -1.0, 1.0)[:, None, None, None, None]
    real = np.concatenate([cos, sin * sign], axis=-1)
    imag = np.concatenate([-sin, cos * sign], axis=-1)
    forward = np.stack([real, imag], axis=4).reshape(4, 640, 1280) / LON
    scale = np.where(m == 0, 1.0, 2.0)[..., None]
    cos, sin = cos * scale, sin * scale
    real = np.stack([cos, -sin], axis=4).reshape(4, 640, 640)
    imag = np.stack([sin, cos], axis=4).reshape(4, 640, 640)
    both = np.stack([real, imag], axis=1)
    both = both.reshape(4, 2, 640, 4, 2, 80).transpose(0, 4, 1, 3, 5, 2)
    inverse = both.reshape(4, 1280, 640)
    return forward, inverse


def split(value):
    high = value.astype(BF16)
    low = (value - high.astype(F32)).astype(BF16)
    return high, low


def dot(a, b):
    return jnp.dot(a, b, preferred_element_type=F32)


def dot_t(a, b):
    return lax.dot_general(a, b, (((1,), (1,)), ((), ())), preferred_element_type=F32)


def moves(count, base):
    found, slot, used = [], 0, 0
    for group in range(base, count):
        lane = 0
        while lane < LAT:
            n = min(LAT - lane, LANES - LAT - used)
            found.append((group, lane, n, slot, LAT + used))
            lane, used = lane + n, used + n
            if used == LANES - LAT:
                slot, used = slot + 1, 0
    return found


def between(start, n):
    lane = lax.broadcasted_iota(jnp.int32, (8, LANES), 1)
    return (lane >= start) & (lane < start + n)


def packed(value, base):
    groups = [value[8 * g : 8 * g + 8] for g in range(value.shape[0] // 8)]
    kept = groups[:base]
    for group, lane, n, slot, to in moves(len(groups), base):
        moved = pltpu.roll(groups[group], to - lane, 1)
        kept[slot] = jnp.where(between(to, n), moved, kept[slot])
    return jnp.concatenate(kept, axis=0)


def unpacked(value, count):
    base = value.shape[0] // 8
    groups = [value[8 * g : 8 * g + 8] for g in range(base)]
    groups += [jnp.zeros((8, LANES), F32)] * (count - base)
    for group, lane, n, slot, to in moves(count, base):
        moved = pltpu.roll(groups[slot], LANES + lane - to, 1)
        groups[group] = jnp.where(between(lane, n), moved, groups[group])
    return jnp.concatenate(groups, axis=0)


def remote(src, dst, send, recv, device):
    return pltpu.make_async_remote_copy(
        src_ref=src,
        dst_ref=dst,
        send_sem=send,
        recv_sem=recv,
        device_id=device,
        device_id_type=pl.DeviceIdType.MESH,
    )


def kernel(
    field,
    depart,
    weight,
    legendre,
    damping,
    fwd_high,
    fwd_low,
    inv_high,
    inv_low,
    out,
    ext,
    hs,
    hr,
    wbuf,
    win,
    adv,
    sent,
    r1,
    s2,
    r2,
    zc,
    fh,
    fl,
    ih,
    il,
    s3,
    r3,
    eo,
    lf,
    lb,
    legf,
    legh,
    legl,
    pbuf,
    cbuf,
    sbuf,
    rbuf,
    tbuf,
    gbuf,
    syn,
    s4,
    s4p,
    r4,
    yc,
    s5,
    r5,
    o6,
    r6,
    w_sem,
    leg_sem,
    tab_sem,
    halo_s,
    halo_r,
    e1_s,
    e1_r,
    e2_s,
    e2_r,
    e3_s,
    e3_r,
    c1_s,
    c1_r,
    c2_s,
    c2_r,
    gz_s,
    gz_r,
    gp_s,
    gp_r,
    e4_s,
    e4_r,
    e5_s,
    e5_r,
    e6_s,
    e6_r,
):
    band = lax.axis_index("band")
    sec = lax.axis_index("sector")
    y, x = sec // 4, sec % 4
    z, core = band // 2, band % 2
    odd = x % 2 == 1

    def w_copy(h, t):
        return pltpu.make_async_copy(weight.at[h, t], wbuf.at[h, t], w_sem.at[h, t])

    @pl.loop(0, TILES)
    def _(t):
        for h in range(2):
            w_copy(h, t).start()

    loads = [
        pltpu.make_async_copy(src.at[x], dst, tab_sem.at[i])
        for i, (src, dst) in enumerate(
            [(fwd_high, fh), (fwd_low, fl), (inv_high, ih), (inv_low, il)]
        )
    ]
    loads[0].start()
    loads[1].start()

    def leg_copy(q):
        rows = pl.ds(q * SHARE, SHARE)
        return pltpu.make_async_copy(legendre.at[rows], legf.at[rows], leg_sem.at[q])

    barrier = pltpu.get_barrier_semaphore()

    def greet(device):
        pl.semaphore_signal(barrier, inc=1, device_id=device, device_id_type=pl.DeviceIdType.MESH)

    for k in range(1, 16):
        greet((band, (sec + k) % 16))
    for k in range(1, 4):
        greet((((z + k) % 4) * 2 + core, sec))
    greet((z * 2 + 1 - core, sec))

    for h in range(2):
        for v in range(2):
            ext[h, v, 64:224, 0:LAT] = field[h, v]
            for i, start in enumerate((64, 192, 96, 160, 128)):
                hs[i, h * 2 + v] = packed(ext[h, v, start : start + TILE, :], 3)

    pl.semaphore_wait(barrier, 19)

    def halo(i):
        to = (sec + 15 - 14 * (i % 2)) % 16
        return remote(hs.at[i], hr.at[i], halo_s.at[i], halo_r.at[i], (band, to))

    for i in range(TILES):
        halo(i).start()
    adv[...] = jnp.zeros_like(adv)

    @pl.when(jnp.logical_not(odd))
    def _():
        r2[1] = jnp.zeros_like(r2[1])

    @pl.loop(0, 8)
    def _(q):
        leg_copy(q).start(priority=1)


    def e1(t, k):
        to = (y + k) % 4
        return remote(
            sent.at[to, t], r1.at[y, t], e1_s.at[t, k], e1_r.at[t, y], (band, to * 4 + x)
        )

    def e1_arrives(t, k):
        source = (y + k) % 4
        remote(
            sent.at[source, t],
            r1.at[source, t],
            e1_s.at[t, k],
            e1_r.at[t, source],
            (band, source * 4 + x),
        ).wait_recv()

    def e2(t, k, part):
        to = (x + k) % 4
        src = s2.at[3, t] if part else s2.at[to - 2 * (to // 3), t]
        return remote(
            src,
            r2.at[part, x, t],
            e2_s.at[part, t, k],
            e2_r.at[part, t, x],
            (band, y * 4 + to),
        )

    def e2_arrives(t, k, part):
        source = (x + k) % 4
        remote(
            s2.at[0, t],
            r2.at[part, source, t],
            e2_s.at[part, t, k],
            e2_r.at[part, t, source],
            (band, y * 4 + source),
        ).wait_recv()

    def tile_of(i):
        return 2 + (1 - 2 * (i % 2)) * ((i + 1) // 2)

    def advect(i):
        t = tile_of(i)
        halo(i).wait_recv()
        start = (1 - i % 2) * (224 + 16 * i) + (i % 2) * (48 - 16 * i)
        rows = pl.ds(pl.multiple_of(start, TILE), TILE)
        for h in range(2):
            for v in range(2):
                ext[h, v, rows, :] = unpacked(hr[i, h * 2 + v], 4)
        for h in range(2):
            w_copy(h, t).wait()
            dep = depart[t, h : h + 1, :]
            for v in range(2):
                window = ext[h, v, pl.ds(pl.multiple_of(t * TILE, TILE), 64), 0:LAT]
                for offset in range(-1, 3):
                    start = pl.multiple_of((t + offset + 2) * TILE, TILE)
                    candidate = ext[h, v, pl.ds(start, 64), 0:LAT]
                    window = jnp.where(dep == offset, candidate, window)
                win[v] = window
            total = [jnp.zeros((TILE, LAT), F32) for _ in range(2)]
            for j in range(64):
                w = wbuf[h, t, j].astype(F32)
                for v in range(2):
                    total[v] = total[v] + win[v, j : j + 1, :] * w
            for v in range(2):
                adv[h * 2 + v, :, 0:LAT] = total[v]
                sent[h * 2 + v, t] = packed(adv[h * 2 + v], 3)
        for k in range(1, 4):
            e1(t, k).start()
        r1[y, t] = sent[y, t]

    def radix(i):
        t = tile_of(i)
        for k in range(1, 4):
            e1_arrives(t, k)
        a, b, c, d = r1[0, t], r1[1, t], r1[2, t], r1[3, t]
        s2[0, t] = (a + c) + (b + d)
        s2[1, t] = a - c
        s2[2, t] = (a + c) - (b + d)
        s2[3, t] = d - b
        for k in range(1, 4):
            e2(t, k, 0).start()

            @pl.when((x + k) % 2 == 1)
            def _():
                e2(t, k, 1).start()

        r2[0, x, t] = s2[x - 2 * (x // 3), t]

        @pl.when(odd)
        def _():
            r2[1, x, t] = s2[3, t]

    pl.loop(0, TILES)(advect)
    pl.loop(0, TILES)(radix)

    @pl.loop(0, TILES)
    def _(i):
        t = tile_of(i)
        for k in range(1, 4):
            e2_arrives(t, k, 0)

            @pl.when(odd)
            def _():
                e2_arrives(t, k, 1)

        for part in range(2):
            for source in range(4):
                high, low = split(unpacked(r2[part, source, t], 4))
                start = pl.multiple_of((part * 4 + source) * 160 + t * TILE, TILE)
                zc[pl.ds(start, TILE), 0:LANES] = high
                zc[pl.ds(start, TILE), LANES : 2 * LANES] = low

    loads[0].wait()
    loads[1].wait()

    def e3(d):
        return remote(s3.at[d], r3.at[sec], e3_s.at[d], e3_r.at[sec], (band, d))

    @pl.loop(0, 2)
    def _(g):
        group = (g + sec // 8) % 2
        rows = pl.ds(pl.multiple_of(group * 320, 320), 320)
        both = dot(fh[rows, :], zc[...])
        value = both[:, 0:LANES] + both[:, LANES:] + dot(fl[rows, :], zc[:, 0:LANES])
        for q in range(8):
            d = group * 8 + q
            s3[d] = packed(value[q * BLOCK : (q + 1) * BLOCK], 4)

            @pl.when(d != sec)
            def _():
                e3(d).start()

            @pl.when(d == sec)
            def _():
                r3[d] = s3[d]

    loads[2].start()
    loads[3].start()

    @pl.loop(0, 8)
    def _(q):
        leg_copy(q).wait()

        @pl.loop(0, SHARE * TILES)
        def _(i):
            p = q * SHARE + i // 5
            rows = pl.ds(pl.multiple_of((i % 5) * 16, 16), 16)
            high, low = split(legf[p, rows, :])
            legh[p, rows, :] = high
            legl[p, rows, :] = low

    @pl.loop(1, 16)
    def _(k):
        source = (sec + k) % 16
        remote(
            s3.at[source], r3.at[source], e3_s.at[source], e3_r.at[source], (band, source)
        ).wait_recv()

    for v in range(2):
        for c in range(4):
            north, south = r3[v * 4 + c], r3[8 + v * 4 + c]
            eo[0, v, c] = unpacked(north + south, 5)
            eo[1, v, c] = unpacked(north - south, 5)
    for p in range(BLOCK):
        j, c = p // 4, p % 4
        for s in range(2):
            for v in range(2):
                row = s * 8 + v * 2
                lf[p, row : row + 2, :] = eo[s, v, c, 2 * j : 2 * j + 2, :]
                lf[p, row + 4 : row + 6, :] = eo[s, v, 3 - c, 20 + 2 * j : 22 + 2 * j, :]

    @pl.loop(0, BLOCK)
    def _(p):
        high, low = split(lf[p])
        lb[p, 0:16, :] = high
        lb[p, 16:32, :] = low

    column = lax.broadcasted_iota(jnp.int32, (8, ROWS), 1)

    def masks(p):
        limit = WAVES - (sec * BLOCK + p)
        leading = column < limit
        lag = jnp.where(leading, column, column - limit)
        return leading, (lag & 1) == 1

    def analyse(share):
        results = []
        for i in range(SHARE):
            p = share * SHARE + i
            lhs = lb[p, :, 0:LAT]
            both = dot(lhs, legh[p])
            total = both[0:16] + both[16:32] + dot(lhs[0:16], legl[p])
            leading, odd_rows = masks(p)
            chosen = jnp.where(odd_rows, total[8:16], total[0:8])
            results.append(jnp.where(leading[0:4], chosen[0:4], chosen[4:8]))
        return results

    partner = (z * 2 + 1 - core, sec)
    ahead, behind, across = (z + 1) % 4, (z + 3) % 4, (z + 2) % 4
    up, down = (ahead * 2 + core, sec), (behind * 2 + core, sec)

    def c1(k):
        return remote(pbuf.at[k], cbuf.at[k], c1_s.at[k], c1_r.at[k], partner)

    def share_at(k, which):
        return ((z + 2 + 3 * k + 3 * (k // 2) + 2 * (k // 3)) % 4) * 2 + which

    first, last = pl.ds(0, 3), pl.ds(3, 2)
    half_up = remote(sbuf.at[0, first], rbuf.at[first], c2_s.at[0], c2_r.at[0], up)
    half_down = remote(sbuf.at[0, last], rbuf.at[last], c2_s.at[1], c2_r.at[1], down)
    early_up = remote(sbuf.at[1, last], tbuf.at[0, last], c2_s.at[2], c2_r.at[2], up)
    early_down = remote(sbuf.at[2, first], tbuf.at[1, first], c2_s.at[3], c2_r.at[3], down)
    late_up = remote(sbuf.at[1, first], tbuf.at[0, first], c2_s.at[4], c2_r.at[4], up)
    late_down = remote(sbuf.at[2, last], tbuf.at[1, last], c2_s.at[5], c2_r.at[5], down)

    @pl.loop(0, 8)
    def _(n):
        late = n // 4
        mine = (1 - late) * (n // 2) + late * (n % 2)
        k = (1 - late) * (n % 2) + late * (n // 2)
        values = analyse(share_at(k, core + (1 - mine) * (1 - 2 * core)))

        @pl.when(mine == 0)
        def _():
            for i, value in enumerate(values):
                pbuf[k, i, :, 0:ROWS] = value
            c1(k).start()

        @pl.when(mine == 1)
        def _():
            for i, value in enumerate(values):
                sbuf[k, i, :, 0:ROWS] = value
            c1(k).wait_recv()
            for i in range(SHARE):
                sbuf[k, i] = sbuf[k, i] + cbuf[k, i]

        @pl.when(n == 2)
        def _():
            half_up.start()
            half_down.start()

        @pl.when(n == 3)
        def _():
            early_up.start()

        @pl.when(n == 5)
        def _():
            early_down.start()

        @pl.when(n == 6)
        def _():
            half_up.wait_recv()
            for i in range(3):
                sbuf[1, i] = sbuf[1, i] + rbuf[i]
            late_up.start()
            half_down.wait_recv()
            for i in range(3, SHARE):
                sbuf[2, i] = sbuf[2, i] + rbuf[i]
            late_down.start()

    for copy in (early_up, early_down, late_up, late_down):
        copy.wait_recv()
    first_level = lax.broadcasted_iota(jnp.int32, (4, ROWS), 0) < 2
    level = jnp.where(first_level, damping[0], damping[1])

    @pl.loop(0, SHARE)
    def _(i):
        p = sec * BLOCK + band * SHARE + i
        column4 = column[0:4]
        degree = jnp.where(column4 < WAVES - p, p + column4, column4 - 1)
        ratio = (degree * (degree + 1)).astype(F32) / float(WAVES * WAVES)
        total = (tbuf[0, i] + tbuf[1, i]) + sbuf[3, i]
        gbuf[band, i, :, 0:ROWS] = total[:, 0:ROWS] / (1.0 + level * ratio)

    def gathered(share, rows, sem, to, send, recv):
        ref = gbuf.at[share, rows]
        return remote(ref, ref, send.at[sem], recv.at[sem], to)

    every = pl.ds(0, SHARE)

    def gz(sem, share, rows, to):
        return gathered(share, rows, sem, to, gz_s, gz_r)

    def gp(sem, share, rows):
        return gathered(share, rows, sem, partner, gp_s, gp_r)

    other = 1 - core
    sends = [
        gz(0, band, first, up),
        gz(1, band, last, down),
        gz(2, behind * 2 + core, first, up),
        gz(3, ahead * 2 + core, last, down),
        gz(4, band, last, up),
        gz(5, band, first, down),
        gp(0, band, every),
        gp(1, behind * 2 + core, every),
        gp(2, ahead * 2 + core, every),
        gp(3, across * 2 + core, first),
        gp(4, across * 2 + core, last),
    ]
    arrivals = [
        gz(0, behind * 2 + core, first, up),
        gz(1, ahead * 2 + core, last, down),
        gz(2, across * 2 + core, first, up),
        gz(3, across * 2 + core, last, down),
        gz(4, behind * 2 + core, last, up),
        gz(5, ahead * 2 + core, first, down),
        gp(0, z * 2 + other, every),
        gp(1, behind * 2 + other, every),
        gp(2, ahead * 2 + other, every),
        gp(3, across * 2 + other, first),
        gp(4, across * 2 + other, last),
    ]
    for k in (0, 1, 4, 5, 6):
        sends[k].start()
    upper = lax.broadcasted_iota(jnp.int32, (8, ROWS), 0) >= 4

    def synthesise(share):
        for i in range(SHARE):
            p = share * SHARE + i
            spec = gbuf[share, i, :, 0:ROWS]
            leading, odd_rows = masks(p)
            north = jnp.concatenate([spec, spec], axis=0)
            north = jnp.where(leading != upper, north, 0.0)
            south = jnp.where(odd_rows, -north, north)
            high, low = split(jnp.concatenate([north, south], axis=0))
            both = dot_t(jnp.concatenate([high, low], axis=0), legh[p])
            syn[p, :, 0:LAT] = both[0:16] + both[16:32] + dot_t(high, legl[p])

    def step_share(k):
        late, turn = (k + 6) // 8, (k + 1) % 3
        chip = (z + late * (3 + 2 * turn + 3 * (turn // 2))) % 4
        swap = (k + 3) // 8 + (1 - late) * k
        return chip * 2 + core + swap * (1 - 2 * core)

    @pl.loop(0, 8)
    def _(k):
        @pl.when(k == 1)
        def _():
            arrivals[6].wait_recv()

        @pl.when(k == 2)
        def _():
            for n in (0, 1):
                arrivals[n].wait_recv()
                sends[n + 2].start()
            for n in (4, 5):
                arrivals[n].wait_recv()
                sends[n + 3].start()

        @pl.when(k == 4)
        def _():
            for n in (2, 3):
                arrivals[n].wait_recv()
                sends[n + 7].start()

        @pl.when(k == 5)
        def _():
            arrivals[7].wait_recv()

        @pl.when(k == 6)
        def _():
            arrivals[8].wait_recv()

        @pl.when(k == 7)
        def _():
            arrivals[9].wait_recv()
            arrivals[10].wait_recv()

        synthesise(step_share(k))

    for p in range(BLOCK):
        j, c = p // 4, p % 4
        for h in range(2):
            for v in range(2):
                row = h * 8 + v * 2
                block = (h * 2 + v) * 4
                s4[block + c, 2 * j : 2 * j + 2, :] = syn[p, row : row + 2, :]
                s4[block + 3 - c, 20 + 2 * j : 22 + 2 * j, :] = syn[p, row + 4 : row + 6, :]

    def e4(k):
        to = (sec + k) % 16
        return remote(s4p.at[to], r4.at[sec], e4_s.at[k], e4_r.at[sec], (band, to))

    @pl.loop(1, 16)
    def _(k):
        to = (sec + k) % 16
        s4p[to] = packed(s4[to], 4)
        e4(k).start()

    r4[sec] = packed(s4[sec], 4)
    loads[2].wait()
    loads[3].wait()

    @pl.loop(0, 8)
    def _(n):
        i = (sec // 2 + n) % 8
        for source in (2 * i, 2 * i + 1):

            @pl.when(source != sec)
            def _():
                remote(
                    s4p.at[source], r4.at[source], e4_s.at[0], e4_r.at[source], (band, source)
                ).wait_recv()

        pair = jnp.concatenate([unpacked(r4[2 * i], 5), unpacked(r4[2 * i + 1], 5)], axis=0)
        high, low = split(pair)
        start = pl.multiple_of(i * 80, 80)
        yc[pl.ds(start, 80), 0:LANES] = high
        yc[pl.ds(start, 80), LANES : 2 * LANES] = low

    def e5(k, part, half):
        to = (x + k) % 4
        return remote(
            s5.at[part, to, half],
            r5.at[part, x, half],
            e5_s.at[part, half, k],
            e5_r.at[part, half, x],
            (band, y * 4 + to),
        )

    def e5_arrives(k, part, half):
        source = (x + k) % 4
        remote(
            s5.at[part, source, half],
            r5.at[part, source, half],
            e5_s.at[part, half, k],
            e5_r.at[part, half, source],
            (band, y * 4 + source),
        ).wait_recv()

    @pl.loop(0, 2)
    def _(half):
        def part_of(part):
            rows = pl.ds(pl.multiple_of(half * 640 + part * 320, 320), 320)
            both = dot(ih[rows, :], yc[...])
            value = both[:, 0:LANES] + both[:, LANES:] + dot(il[rows, :], yc[:, 0:LANES])
            for to in range(4):
                s5[part, to, half] = packed(value[to * 80 : (to + 1) * 80], 7)

                @pl.when(to != x)
                def _():
                    e5((to - x + 4) % 4, part, half).start()

                @pl.when(to == x)
                def _():
                    r5[part, to, half] = s5[part, to, half]

        part_of(0)

        @pl.when(odd)
        def _():
            part_of(1)

    def e6(half, k):
        to = (y + k) % 4
        return remote(
            o6.at[to, half], r6.at[y, half], e6_s.at[half, k], e6_r.at[half, y], (band, to * 4 + x)
        )

    @pl.loop(0, 2)
    def _(half):
        for k in range(1, 4):
            e5_arrives(k, 0, half)

            @pl.when((x + k) % 2 == 1)
            def _():
                e5_arrives(k, 1, half)

        a, c = r5[0, 0, half], r5[0, 2, half]
        b = r5[0, 1, half] + r5[0, 3, half]
        d = r5[1, 3, half] - r5[1, 1, half]
        o6[0, half] = (a + c) + b
        o6[1, half] = (a - c) + d
        o6[2, half] = (a + c) - b
        o6[3, half] = (a - c) - d
        for k in range(1, 4):
            e6(half, k).start()
        r6[y, half] = o6[y, half]

    @pl.loop(0, 2)
    def _(half):
        for k in range(1, 4):
            source = (y + k) % 4
            remote(
                o6.at[source, half],
                r6.at[source, half],
                e6_s.at[half, k],
                e6_r.at[half, source],
                (band, source * 4 + x),
            ).wait_recv()

    for block in range(4):
        rows = [unpacked(r6[block, half], 10) for half in range(2)]
        out[block] = jnp.transpose(jnp.concatenate(rows, axis=0))[0:LAT]

    for i in range(TILES):
        halo(i).wait_send()

    @pl.loop(0, TILES)
    def _(t):
        for k in range(1, 4):
            e1(t, k).wait_send()
            e2(t, k, 0).wait_send()

            @pl.when((x + k) % 2 == 1)
            def _():
                e2(t, k, 1).wait_send()

    @pl.loop(1, 16)
    def _(k):
        e3((sec + k) % 16).wait_send()
        e4(k).wait_send()

    for k in range(4):
        c1(k).wait_send()
    for copy in (half_up, half_down, early_up, early_down, late_up, late_down, *sends):
        copy.wait_send()
    for k in range(1, 4):
        for half in range(2):
            e5(k, 0, half).wait_send()

            @pl.when(odd)
            def _():
                e5(k, 1, half).wait_send()

            e6(half, k).wait_send()


def local(field, depart, interp_weight, legendre, damping):
    forward, inverse = tables()
    constants = [jnp.asarray(t) for t in (*halves(forward), *halves(inverse))]
    vmem = pl.BlockSpec(memory_space=pltpu.VMEM)
    hbm = pl.BlockSpec(memory_space=pl.ANY)
    scratch = [
        pltpu.VMEM((2, 2, 320, LANES), F32),
        pltpu.VMEM((5, 4, PACK, LANES), F32),
        pltpu.VMEM((5, 4, PACK, LANES), F32),
        pltpu.VMEM((2, 5, 64, TILE, LAT), BF16),
        pltpu.VMEM((2, 64, LAT), F32),
        pltpu.VMEM((4, TILE, LANES), F32),
        pltpu.VMEM((4, 5, PACK, LANES), F32),
        pltpu.VMEM((4, 5, PACK, LANES), F32),
        pltpu.VMEM((4, 5, PACK, LANES), F32),
        pltpu.VMEM((2, 4, 5, PACK, LANES), F32),
        pltpu.VMEM((1280, 2 * LANES), BF16),
        pltpu.VMEM((640, 1280), BF16),
        pltpu.VMEM((640, 1280), BF16),
        pltpu.VMEM((1280, 640), BF16),
        pltpu.VMEM((1280, 640), BF16),
        pltpu.VMEM((16, 32, LANES), F32),
        pltpu.VMEM((16, 32, LANES), F32),
        pltpu.VMEM((2, 2, 4, BLOCK, LANES), F32),
        pltpu.VMEM((BLOCK, 16, LANES), F32),
        pltpu.VMEM((BLOCK, 32, LANES), BF16),
        pltpu.VMEM((BLOCK, LAT, ROWS), F32),
        pltpu.VMEM((BLOCK, LAT, ROWS), BF16),
        pltpu.VMEM((BLOCK, LAT, ROWS), BF16),
        pltpu.VMEM((4, SHARE, 4, WIDE), F32),
        pltpu.VMEM((4, SHARE, 4, WIDE), F32),
        pltpu.VMEM((4, SHARE, 4, WIDE), F32),
        pltpu.VMEM((SHARE, 4, WIDE), F32),
        pltpu.VMEM((2, SHARE, 4, WIDE), F32),
        pltpu.VMEM((8, SHARE, 4, WIDE), F32),
        pltpu.VMEM((BLOCK, 16, LANES), F32),
        pltpu.VMEM((16, BLOCK, LANES), F32),
        pltpu.VMEM((16, 32, LANES), F32),
        pltpu.VMEM((16, 32, LANES), F32),
        pltpu.VMEM((640, 2 * LANES), BF16),
        pltpu.VMEM((2, 4, 2, 56, LANES), F32),
        pltpu.VMEM((2, 4, 2, 56, LANES), F32),
        pltpu.VMEM((4, 2, 56, LANES), F32),
        pltpu.VMEM((4, 2, 56, LANES), F32),
    ]
    dma = pltpu.SemaphoreType.DMA
    scratch += [
        dma((2, 5)),
        dma((8,)),
        dma((4,)),
        dma((5,)),
        dma((5,)),
        dma((5, 4)),
        dma((5, 4)),
        dma((2, 5, 4)),
        dma((2, 5, 4)),
        dma((16,)),
        dma((16,)),
        dma((4,)),
        dma((4,)),
        dma((6,)),
        dma((6,)),
        dma((6,)),
        dma((6,)),
        dma((5,)),
        dma((5,)),
        dma((16,)),
        dma((16,)),
        dma((2, 2, 4)),
        dma((2, 2, 4)),
        dma((2, 4)),
        dma((2, 4)),
    ]
    grid = pl.pallas_call(
        kernel,
        out_shape=jax.ShapeDtypeStruct((4, LAT, 160), F32),
        in_specs=[vmem, vmem, hbm, hbm, pl.BlockSpec(memory_space=pltpu.SMEM)] + [hbm] * 4,
        out_specs=vmem,
        scratch_shapes=scratch,
        compiler_params=pltpu.CompilerParams(
            collective_id=0, has_side_effects=True, vmem_limit_bytes=62 * 1024 * 1024
        ),
    )(
        jnp.transpose(field, (0, 2, 3, 1)),
        jnp.transpose(depart, (2, 0, 1)),
        jnp.transpose(interp_weight, (0, 2, 3, 4, 1)),
        legendre,
        damping,
        *constants,
    )
    return jnp.transpose(grid.reshape(2, 2, LAT, 160), (0, 2, 1, 3))


def solution(mesh):
    placed = (
        P(None, "band", None, "sector"),
        P(None, "band", "sector"),
        P(None, "band", "sector", None, None),
        P("sector", "band", None),
        P(),
    )
    return jax.shard_map(
        local, mesh=mesh, in_specs=placed, out_specs=P(None, "band", None, "sector"), check_vma=False
    )
```

```python
import math

import jax
import jax.numpy as jnp
import ml_dtypes
import numpy as np
from jax import lax
from jax.experimental import pallas as pl
from jax.experimental.pallas import tpu as pltpu
from jax.sharding import PartitionSpec as P

F32 = jnp.float32
BF16 = jnp.bfloat16
LON = 2560
WAVES = 1280
ROWS = WAVES + 1
WIDE = WAVES + 128
TILE = 32
LANES = 128
LAT = 80
BLOCK = 40
SHARE = 5
TILES = 5
PACK = 24


def halves(table):
    high = table.astype(ml_dtypes.bfloat16)
    low = (table - high.astype(np.float64)).astype(ml_dtypes.bfloat16)
    return high, low


def tables():
    cls = np.arange(4)[:, None, None]
    d = np.arange(16)[None, :, None]
    j = np.arange(10)[None, None, :]
    lower = BLOCK * d + 4 * j + cls
    upper = WAVES - 4 - BLOCK * d - 4 * j + cls
    m = np.stack([lower, upper], axis=2)
    xi = np.arange(640)
    angle = 2.0 * math.pi / LON * ((m[..., None] * xi) % LON)
    cos, sin = np.cos(angle), np.sin(angle)
    sign = np.where(np.arange(4) == 3, -1.0, 1.0)[:, None, None, None, None]
    real = np.concatenate([cos, sin * sign], axis=-1)
    imag = np.concatenate([-sin, cos * sign], axis=-1)
    forward = np.stack([real, imag], axis=4).reshape(4, 640, 1280) / LON
    scale = np.where(m == 0, 1.0, 2.0)[..., None]
    cos, sin = cos * scale, sin * scale
    real = np.stack([cos, -sin], axis=4).reshape(4, 640, 640)
    imag = np.stack([sin, cos], axis=4).reshape(4, 640, 640)
    both = np.stack([real, imag], axis=1)
    both = both.reshape(4, 2, 640, 4, 2, 80).transpose(0, 4, 1, 3, 5, 2)
    inverse = both.reshape(4, 1280, 640)
    return forward, inverse


def split(value):
    high = value.astype(BF16)
    low = (value - high.astype(F32)).astype(BF16)
    return high, low


def dot(a, b):
    return jnp.dot(a, b, preferred_element_type=F32)


def dot_t(a, b):
    return lax.dot_general(a, b, (((1,), (1,)), ((), ())), preferred_element_type=F32)


def moves(count, base):
    found, slot, used = [], 0, 0
    for group in range(base, count):
        lane = 0
        while lane < LAT:
            n = min(LAT - lane, LANES - LAT - used)
            found.append((group, lane, n, slot, LAT + used))
            lane, used = lane + n, used + n
            if used == LANES - LAT:
                slot, used = slot + 1, 0
    return found


def between(start, n):
    lane = lax.broadcasted_iota(jnp.int32, (8, LANES), 1)
    return (lane >= start) & (lane < start + n)


def packed(value, base):
    groups = [value[8 * g : 8 * g + 8] for g in range(value.shape[0] // 8)]
    kept = groups[:base]
    for group, lane, n, slot, to in moves(len(groups), base):
        moved = pltpu.roll(groups[group], to - lane, 1)
        kept[slot] = jnp.where(between(to, n), moved, kept[slot])
    return jnp.concatenate(kept, axis=0)


def unpacked(value, count):
    base = value.shape[0] // 8
    groups = [value[8 * g : 8 * g + 8] for g in range(base)]
    groups += [jnp.zeros((8, LANES), F32)] * (count - base)
    for group, lane, n, slot, to in moves(count, base):
        moved = pltpu.roll(groups[slot], LANES + lane - to, 1)
        groups[group] = jnp.where(between(lane, n), moved, groups[group])
    return jnp.concatenate(groups, axis=0)


def remote(src, dst, send, recv, device):
    return pltpu.make_async_remote_copy(
        src_ref=src,
        dst_ref=dst,
        send_sem=send,
        recv_sem=recv,
        device_id=device,
        device_id_type=pl.DeviceIdType.MESH,
    )


def kernel(
    field,
    depart,
    weight,
    legendre,
    damping,
    fwd_high,
    fwd_low,
    inv_high,
    inv_low,
    out,
    ext,
    hs,
    hr,
    wbuf,
    win,
    adv,
    sent,
    r1,
    s2,
    r2,
    zc,
    fh,
    fl,
    ih,
    il,
    s3,
    r3,
    eo,
    lf,
    lb,
    legf,
    legh,
    legl,
    pbuf,
    cbuf,
    sbuf,
    rbuf,
    tbuf,
    gbuf,
    syn,
    s4,
    s4p,
    r4,
    yc,
    s5,
    r5,
    o6,
    r6,
    w_sem,
    leg_sem,
    tab_sem,
    halo_s,
    halo_r,
    e1_s,
    e1_r,
    e2_s,
    e2_r,
    e3_s,
    e3_r,
    c1_s,
    c1_r,
    c2_s,
    c2_r,
    gz_s,
    gz_r,
    gp_s,
    gp_r,
    e4_s,
    e4_r,
    e5_s,
    e5_r,
    e6_s,
    e6_r,
):
    band = lax.axis_index("band")
    sec = lax.axis_index("sector")
    y, x = sec // 4, sec % 4
    z, core = band // 2, band % 2
    odd = x % 2 == 1

    def w_copy(h, t):
        return pltpu.make_async_copy(weight.at[h, t], wbuf.at[h, t], w_sem.at[h, t])

    @pl.loop(0, TILES)
    def _(t):
        for h in range(2):
            w_copy(h, t).start()

    loads = [
        pltpu.make_async_copy(src.at[x], dst, tab_sem.at[i])
        for i, (src, dst) in enumerate(
            [(fwd_high, fh), (fwd_low, fl), (inv_high, ih), (inv_low, il)]
        )
    ]
    loads[0].start()
    loads[1].start()

    def leg_copy(q):
        rows = pl.ds(q * SHARE, SHARE)
        return pltpu.make_async_copy(legendre.at[rows], legf.at[rows], leg_sem.at[q])

    barrier = pltpu.get_barrier_semaphore()

    def greet(device):
        pl.semaphore_signal(barrier, inc=1, device_id=device, device_id_type=pl.DeviceIdType.MESH)

    for k in range(1, 16):
        greet((band, (sec + k) % 16))
    for k in range(1, 4):
        greet((((z + k) % 4) * 2 + core, sec))
    greet((z * 2 + 1 - core, sec))

    for h in range(2):
        for v in range(2):
            ext[h, v, 64:224, 0:LAT] = field[h, v]
            for i, start in enumerate((64, 192, 96, 160, 128)):
                hs[i, h * 2 + v] = packed(ext[h, v, start : start + TILE, :], 3)

    pl.semaphore_wait(barrier, 19)

    def halo(i):
        to = (sec + 15 - 14 * (i % 2)) % 16
        return remote(hs.at[i], hr.at[i], halo_s.at[i], halo_r.at[i], (band, to))

    for i in range(TILES):
        halo(i).start()
    adv[...] = jnp.zeros_like(adv)

    @pl.when(jnp.logical_not(odd))
    def _():
        r2[1] = jnp.zeros_like(r2[1])

    @pl.loop(0, 8)
    def _(q):
        leg_copy(q).start(priority=1)


    def e1(t, k):
        to = (y + k) % 4
        return remote(
            sent.at[to, t], r1.at[y, t], e1_s.at[t, k], e1_r.at[t, y], (band, to * 4 + x)
        )

    def e1_arrives(t, k):
        source = (y + k) % 4
        remote(
            sent.at[source, t],
            r1.at[source, t],
            e1_s.at[t, k],
            e1_r.at[t, source],
            (band, source * 4 + x),
        ).wait_recv()

    def e2(t, k, part):
        to = (x + k) % 4
        src = s2.at[3, t] if part else s2.at[to - 2 * (to // 3), t]
        return remote(
            src,
            r2.at[part, x, t],
            e2_s.at[part, t, k],
            e2_r.at[part, t, x],
            (band, y * 4 + to),
        )

    def e2_arrives(t, k, part):
        source = (x + k) % 4
        remote(
            s2.at[0, t],
            r2.at[part, source, t],
            e2_s.at[part, t, k],
            e2_r.at[part, t, source],
            (band, y * 4 + source),
        ).wait_recv()

    def tile_of(i):
        return 2 + (1 - 2 * (i % 2)) * ((i + 1) // 2)

    def advect(i):
        t = tile_of(i)
        halo(i).wait_recv()
        start = (1 - i % 2) * (224 + 16 * i) + (i % 2) * (48 - 16 * i)
        rows = pl.ds(pl.multiple_of(start, TILE), TILE)
        for h in range(2):
            for v in range(2):
                ext[h, v, rows, :] = unpacked(hr[i, h * 2 + v], 4)
        for h in range(2):
            w_copy(h, t).wait()
            dep = depart[t, h : h + 1, :]
            for v in range(2):
                window = ext[h, v, pl.ds(pl.multiple_of(t * TILE, TILE), 64), 0:LAT]
                for offset in range(-1, 3):
                    start = pl.multiple_of((t + offset + 2) * TILE, TILE)
                    candidate = ext[h, v, pl.ds(start, 64), 0:LAT]
                    window = jnp.where(dep == offset, candidate, window)
                win[v] = window
            total = [jnp.zeros((TILE, LAT), F32) for _ in range(2)]
            for j in range(64):
                w = wbuf[h, t, j].astype(F32)
                for v in range(2):
                    total[v] = total[v] + win[v, j : j + 1, :] * w
            for v in range(2):
                adv[h * 2 + v, :, 0:LAT] = total[v]
                sent[h * 2 + v, t] = packed(adv[h * 2 + v], 3)
        for k in range(1, 4):
            e1(t, k).start()
        r1[y, t] = sent[y, t]

    def radix(i):
        t = tile_of(i)
        for k in range(1, 4):
            e1_arrives(t, k)
        a, b, c, d = r1[0, t], r1[1, t], r1[2, t], r1[3, t]
        s2[0, t] = (a + c) + (b + d)
        s2[1, t] = a - c
        s2[2, t] = (a + c) - (b + d)
        s2[3, t] = d - b
        for k in range(1, 4):
            e2(t, k, 0).start()

            @pl.when((x + k) % 2 == 1)
            def _():
                e2(t, k, 1).start()

        r2[0, x, t] = s2[x - 2 * (x // 3), t]

        @pl.when(odd)
        def _():
            r2[1, x, t] = s2[3, t]

    pl.loop(0, TILES)(advect)
    pl.loop(0, TILES)(radix)

    @pl.loop(0, TILES)
    def _(i):
        t = tile_of(i)
        for k in range(1, 4):
            e2_arrives(t, k, 0)

            @pl.when(odd)
            def _():
                e2_arrives(t, k, 1)

        for part in range(2):
            for source in range(4):
                high, low = split(unpacked(r2[part, source, t], 4))
                start = pl.multiple_of((part * 4 + source) * 160 + t * TILE, TILE)
                zc[pl.ds(start, TILE), 0:LANES] = high
                zc[pl.ds(start, TILE), LANES : 2 * LANES] = low

    loads[0].wait()
    loads[1].wait()

    def e3(d):
        return remote(s3.at[d], r3.at[sec], e3_s.at[d], e3_r.at[sec], (band, d))

    @pl.loop(0, 2)
    def _(g):
        group = (g + sec // 8) % 2
        rows = pl.ds(pl.multiple_of(group * 320, 320), 320)
        both = dot(fh[rows, :], zc[...])
        value = both[:, 0:LANES] + both[:, LANES:] + dot(fl[rows, :], zc[:, 0:LANES])
        for q in range(8):
            d = group * 8 + q
            s3[d] = packed(value[q * BLOCK : (q + 1) * BLOCK], 4)

            @pl.when(d != sec)
            def _():
                e3(d).start()

            @pl.when(d == sec)
            def _():
                r3[d] = s3[d]

    loads[2].start()
    loads[3].start()

    @pl.loop(0, 8)
    def _(q):
        leg_copy(q).wait()

        @pl.loop(0, SHARE * TILES)
        def _(i):
            p = q * SHARE + i // 5
            rows = pl.ds(pl.multiple_of((i % 5) * 16, 16), 16)
            high, low = split(legf[p, rows, :])
            legh[p, rows, :] = high
            legl[p, rows, :] = low

    @pl.loop(1, 16)
    def _(k):
        source = (sec + k) % 16
        remote(
            s3.at[source], r3.at[source], e3_s.at[source], e3_r.at[source], (band, source)
        ).wait_recv()

    for v in range(2):
        for c in range(4):
            north, south = r3[v * 4 + c], r3[8 + v * 4 + c]
            eo[0, v, c] = unpacked(north + south, 5)
            eo[1, v, c] = unpacked(north - south, 5)
    for p in range(BLOCK):
        j, c = p // 4, p % 4
        for s in range(2):
            for v in range(2):
                row = s * 8 + v * 2
                lf[p, row : row + 2, :] = eo[s, v, c, 2 * j : 2 * j + 2, :]
                lf[p, row + 4 : row + 6, :] = eo[s, v, 3 - c, 20 + 2 * j : 22 + 2 * j, :]

    @pl.loop(0, BLOCK)
    def _(p):
        high, low = split(lf[p])
        lb[p, 0:16, :] = high
        lb[p, 16:32, :] = low

    column = lax.broadcasted_iota(jnp.int32, (8, ROWS), 1)

    def masks(p):
        limit = WAVES - (sec * BLOCK + p)
        leading = column < limit
        lag = jnp.where(leading, column, column - limit)
        return leading, (lag & 1) == 1

    def analyse(share):
        results = []
        for i in range(SHARE):
            p = share * SHARE + i
            lhs = lb[p, :, 0:LAT]
            both = dot(lhs, legh[p])
            total = both[0:16] + both[16:32] + dot(lhs[0:16], legl[p])
            leading, odd_rows = masks(p)
            chosen = jnp.where(odd_rows, total[8:16], total[0:8])
            results.append(jnp.where(leading[0:4], chosen[0:4], chosen[4:8]))
        return results

    partner = (z * 2 + 1 - core, sec)
    ahead, behind, across = (z + 1) % 4, (z + 3) % 4, (z + 2) % 4
    up, down = (ahead * 2 + core, sec), (behind * 2 + core, sec)

    def c1(k):
        return remote(pbuf.at[k], cbuf.at[k], c1_s.at[k], c1_r.at[k], partner)

    def share_at(k, which):
        return ((z + 2 + 3 * k + 3 * (k // 2) + 2 * (k // 3)) % 4) * 2 + which

    first, last = pl.ds(0, 3), pl.ds(3, 2)
    half_up = remote(sbuf.at[0, first], rbuf.at[first], c2_s.at[0], c2_r.at[0], up)
    half_down = remote(sbuf.at[0, last], rbuf.at[last], c2_s.at[1], c2_r.at[1], down)
    early_up = remote(sbuf.at[1, last], tbuf.at[0, last], c2_s.at[2], c2_r.at[2], up)
    early_down = remote(sbuf.at[2, first], tbuf.at[1, first], c2_s.at[3], c2_r.at[3], down)
    late_up = remote(sbuf.at[1, first], tbuf.at[0, first], c2_s.at[4], c2_r.at[4], up)
    late_down = remote(sbuf.at[2, last], tbuf.at[1, last], c2_s.at[5], c2_r.at[5], down)

    @pl.loop(0, 8)
    def _(n):
        late = n // 4
        mine = (1 - late) * (n // 2) + late * (n % 2)
        k = (1 - late) * (n % 2) + late * (n // 2)
        values = analyse(share_at(k, core + (1 - mine) * (1 - 2 * core)))

        @pl.when(mine == 0)
        def _():
            for i, value in enumerate(values):
                pbuf[k, i, :, 0:ROWS] = value
            c1(k).start()

        @pl.when(mine == 1)
        def _():
            for i, value in enumerate(values):
                sbuf[k, i, :, 0:ROWS] = value
            c1(k).wait_recv()
            for i in range(SHARE):
                sbuf[k, i] = sbuf[k, i] + cbuf[k, i]

        @pl.when(n == 2)
        def _():
            half_up.start()
            half_down.start()

        @pl.when(n == 3)
        def _():
            early_up.start()

        @pl.when(n == 5)
        def _():
            early_down.start()

        @pl.when(n == 6)
        def _():
            half_up.wait_recv()
            for i in range(3):
                sbuf[1, i] = sbuf[1, i] + rbuf[i]
            late_up.start()
            half_down.wait_recv()
            for i in range(3, SHARE):
                sbuf[2, i] = sbuf[2, i] + rbuf[i]
            late_down.start()

    for copy in (early_up, early_down, late_up, late_down):
        copy.wait_recv()
    first_level = lax.broadcasted_iota(jnp.int32, (4, ROWS), 0) < 2
    level = jnp.where(first_level, damping[0], damping[1])

    @pl.loop(0, SHARE)
    def _(i):
        p = sec * BLOCK + band * SHARE + i
        column4 = column[0:4]
        degree = jnp.where(column4 < WAVES - p, p + column4, column4 - 1)
        ratio = (degree * (degree + 1)).astype(F32) / float(WAVES * WAVES)
        total = (tbuf[0, i] + tbuf[1, i]) + sbuf[3, i]
        gbuf[band, i, :, 0:ROWS] = total[:, 0:ROWS] / (1.0 + level * ratio)

    def gathered(share, rows, sem, to, send, recv):
        ref = gbuf.at[share, rows]
        return remote(ref, ref, send.at[sem], recv.at[sem], to)

    every = pl.ds(0, SHARE)

    def gz(sem, share, rows, to):
        return gathered(share, rows, sem, to, gz_s, gz_r)

    def gp(sem, share, rows):
        return gathered(share, rows, sem, partner, gp_s, gp_r)

    other = 1 - core
    sends = [
        gz(0, band, first, up),
        gz(1, band, last, down),
        gz(2, behind * 2 + core, first, up),
        gz(3, ahead * 2 + core, last, down),
        gz(4, band, last, up),
        gz(5, band, first, down),
        gp(0, band, every),
        gp(1, behind * 2 + core, every),
        gp(2, ahead * 2 + core, every),
        gp(3, across * 2 + core, first),
        gp(4, across * 2 + core, last),
    ]
    arrivals = [
        gz(0, behind * 2 + core, first, up),
        gz(1, ahead * 2 + core, last, down),
        gz(2, across * 2 + core, first, up),
        gz(3, across * 2 + core, last, down),
        gz(4, behind * 2 + core, last, up),
        gz(5, ahead * 2 + core, first, down),
        gp(0, z * 2 + other, every),
        gp(1, behind * 2 + other, every),
        gp(2, ahead * 2 + other, every),
        gp(3, across * 2 + other, first),
        gp(4, across * 2 + other, last),
    ]
    for k in (0, 1, 4, 5, 6):
        sends[k].start()
    upper = lax.broadcasted_iota(jnp.int32, (8, ROWS), 0) >= 4

    def synthesise(share):
        for i in range(SHARE):
            p = share * SHARE + i
            spec = gbuf[share, i, :, 0:ROWS]
            leading, odd_rows = masks(p)
            north = jnp.concatenate([spec, spec], axis=0)
            north = jnp.where(leading != upper, north, 0.0)
            south = jnp.where(odd_rows, -north, north)
            high, low = split(jnp.concatenate([north, south], axis=0))
            both = dot_t(jnp.concatenate([high, low], axis=0), legh[p])
            syn[p, :, 0:LAT] = both[0:16] + both[16:32] + dot_t(high, legl[p])

    def step_share(k):
        late, turn = (k + 6) // 8, (k + 1) % 3
        chip = (z + late * (3 + 2 * turn + 3 * (turn // 2))) % 4
        swap = (k + 3) // 8 + (1 - late) * k
        return chip * 2 + core + swap * (1 - 2 * core)

    @pl.loop(0, 8)
    def _(k):
        @pl.when(k == 1)
        def _():
            arrivals[6].wait_recv()

        @pl.when(k == 2)
        def _():
            for n in (0, 1):
                arrivals[n].wait_recv()
                sends[n + 2].start()
            arrivals[4].wait_recv()
            sends[7].start()

        @pl.when(k == 3)
        def _():
            arrivals[5].wait_recv()
            sends[8].start()

        @pl.when(k == 4)
        def _():
            for n in (2, 3):
                arrivals[n].wait_recv()
                sends[n + 7].start()

        @pl.when(k == 5)
        def _():
            arrivals[7].wait_recv()

        @pl.when(k == 6)
        def _():
            arrivals[8].wait_recv()

        @pl.when(k == 7)
        def _():
            arrivals[9].wait_recv()
            arrivals[10].wait_recv()

        synthesise(step_share(k))

    for p in range(BLOCK):
        j, c = p // 4, p % 4
        for h in range(2):
            for v in range(2):
                row = h * 8 + v * 2
                block = (h * 2 + v) * 4
                s4[block + c, 2 * j : 2 * j + 2, :] = syn[p, row : row + 2, :]
                s4[block + 3 - c, 20 + 2 * j : 22 + 2 * j, :] = syn[p, row + 4 : row + 6, :]

    def e4(k):
        to = (sec + k) % 16
        return remote(s4p.at[to], r4.at[sec], e4_s.at[k], e4_r.at[sec], (band, to))

    @pl.loop(1, 16)
    def _(k):
        to = (sec + k) % 16
        s4p[to] = packed(s4[to], 4)
        e4(k).start()

    r4[sec] = packed(s4[sec], 4)
    loads[2].wait()
    loads[3].wait()

    @pl.loop(0, 8)
    def _(n):
        i = (sec // 2 + n) % 8
        for source in (2 * i, 2 * i + 1):

            @pl.when(source != sec)
            def _():
                remote(
                    s4p.at[source], r4.at[source], e4_s.at[0], e4_r.at[source], (band, source)
                ).wait_recv()

        pair = jnp.concatenate([unpacked(r4[2 * i], 5), unpacked(r4[2 * i + 1], 5)], axis=0)
        high, low = split(pair)
        start = pl.multiple_of(i * 80, 80)
        yc[pl.ds(start, 80), 0:LANES] = high
        yc[pl.ds(start, 80), LANES : 2 * LANES] = low

    def e5(k, part, half):
        to = (x + k) % 4
        return remote(
            s5.at[part, to, half],
            r5.at[part, x, half],
            e5_s.at[part, half, k],
            e5_r.at[part, half, x],
            (band, y * 4 + to),
        )

    def e5_arrives(k, part, half):
        source = (x + k) % 4
        remote(
            s5.at[part, source, half],
            r5.at[part, source, half],
            e5_s.at[part, half, k],
            e5_r.at[part, half, source],
            (band, y * 4 + source),
        ).wait_recv()

    @pl.loop(0, 2)
    def _(half):
        def part_of(part):
            rows = pl.ds(pl.multiple_of(half * 640 + part * 320, 320), 320)
            both = dot(ih[rows, :], yc[...])
            value = both[:, 0:LANES] + both[:, LANES:] + dot(il[rows, :], yc[:, 0:LANES])
            for to in range(4):
                s5[part, to, half] = packed(value[to * 80 : (to + 1) * 80], 7)

                @pl.when(to != x)
                def _():
                    e5((to - x + 4) % 4, part, half).start()

                @pl.when(to == x)
                def _():
                    r5[part, to, half] = s5[part, to, half]

        part_of(0)

        @pl.when(odd)
        def _():
            part_of(1)

    def e6(half, k):
        to = (y + k) % 4
        return remote(
            o6.at[to, half], r6.at[y, half], e6_s.at[half, k], e6_r.at[half, y], (band, to * 4 + x)
        )

    @pl.loop(0, 2)
    def _(half):
        for k in range(1, 4):
            e5_arrives(k, 0, half)

            @pl.when((x + k) % 2 == 1)
            def _():
                e5_arrives(k, 1, half)

        a, c = r5[0, 0, half], r5[0, 2, half]
        b = r5[0, 1, half] + r5[0, 3, half]
        d = r5[1, 3, half] - r5[1, 1, half]
        o6[0, half] = (a + c) + b
        o6[1, half] = (a - c) + d
        o6[2, half] = (a + c) - b
        o6[3, half] = (a - c) - d
        for k in range(1, 4):
            e6(half, k).start()
        out[y, half] = unpacked(o6[y, half], 10)

    @pl.loop(0, 2)
    def _(half):
        for k in range(1, 4):
            source = (y + k) % 4
            remote(
                o6.at[source, half],
                r6.at[source, half],
                e6_s.at[half, k],
                e6_r.at[half, source],
                (band, source * 4 + x),
            ).wait_recv()
            out[source, half] = unpacked(r6[source, half], 10)

    for i in range(TILES):
        halo(i).wait_send()

    @pl.loop(0, TILES)
    def _(t):
        for k in range(1, 4):
            e1(t, k).wait_send()
            e2(t, k, 0).wait_send()

            @pl.when((x + k) % 2 == 1)
            def _():
                e2(t, k, 1).wait_send()

    @pl.loop(1, 16)
    def _(k):
        e3((sec + k) % 16).wait_send()
        e4(k).wait_send()

    for k in range(4):
        c1(k).wait_send()
    for copy in (half_up, half_down, early_up, early_down, late_up, late_down, *sends):
        copy.wait_send()
    for k in range(1, 4):
        for half in range(2):
            e5(k, 0, half).wait_send()

            @pl.when(odd)
            def _():
                e5(k, 1, half).wait_send()

            e6(half, k).wait_send()


def local(field, depart, interp_weight, legendre, damping):
    forward, inverse = tables()
    constants = [jnp.asarray(t) for t in (*halves(forward), *halves(inverse))]
    vmem = pl.BlockSpec(memory_space=pltpu.VMEM)
    hbm = pl.BlockSpec(memory_space=pl.ANY)
    scratch = [
        pltpu.VMEM((2, 2, 320, LANES), F32),
        pltpu.VMEM((5, 4, PACK, LANES), F32),
        pltpu.VMEM((5, 4, PACK, LANES), F32),
        pltpu.VMEM((2, 5, 64, TILE, LAT), BF16),
        pltpu.VMEM((2, 64, LAT), F32),
        pltpu.VMEM((4, TILE, LANES), F32),
        pltpu.VMEM((4, 5, PACK, LANES), F32),
        pltpu.VMEM((4, 5, PACK, LANES), F32),
        pltpu.VMEM((4, 5, PACK, LANES), F32),
        pltpu.VMEM((2, 4, 5, PACK, LANES), F32),
        pltpu.VMEM((1280, 2 * LANES), BF16),
        pltpu.VMEM((640, 1280), BF16),
        pltpu.VMEM((640, 1280), BF16),
        pltpu.VMEM((1280, 640), BF16),
        pltpu.VMEM((1280, 640), BF16),
        pltpu.VMEM((16, 32, LANES), F32),
        pltpu.VMEM((16, 32, LANES), F32),
        pltpu.VMEM((2, 2, 4, BLOCK, LANES), F32),
        pltpu.VMEM((BLOCK, 16, LANES), F32),
        pltpu.VMEM((BLOCK, 32, LANES), BF16),
        pltpu.VMEM((BLOCK, LAT, ROWS), F32),
        pltpu.VMEM((BLOCK, LAT, ROWS), BF16),
        pltpu.VMEM((BLOCK, LAT, ROWS), BF16),
        pltpu.VMEM((4, SHARE, 4, WIDE), F32),
        pltpu.VMEM((4, SHARE, 4, WIDE), F32),
        pltpu.VMEM((4, SHARE, 4, WIDE), F32),
        pltpu.VMEM((SHARE, 4, WIDE), F32),
        pltpu.VMEM((2, SHARE, 4, WIDE), F32),
        pltpu.VMEM((8, SHARE, 4, WIDE), F32),
        pltpu.VMEM((BLOCK, 16, LANES), F32),
        pltpu.VMEM((16, BLOCK, LANES), F32),
        pltpu.VMEM((16, 32, LANES), F32),
        pltpu.VMEM((16, 32, LANES), F32),
        pltpu.VMEM((640, 2 * LANES), BF16),
        pltpu.VMEM((2, 4, 2, 56, LANES), F32),
        pltpu.VMEM((2, 4, 2, 56, LANES), F32),
        pltpu.VMEM((4, 2, 56, LANES), F32),
        pltpu.VMEM((4, 2, 56, LANES), F32),
    ]
    dma = pltpu.SemaphoreType.DMA
    scratch += [
        dma((2, 5)),
        dma((8,)),
        dma((4,)),
        dma((5,)),
        dma((5,)),
        dma((5, 4)),
        dma((5, 4)),
        dma((2, 5, 4)),
        dma((2, 5, 4)),
        dma((16,)),
        dma((16,)),
        dma((4,)),
        dma((4,)),
        dma((6,)),
        dma((6,)),
        dma((6,)),
        dma((6,)),
        dma((5,)),
        dma((5,)),
        dma((16,)),
        dma((16,)),
        dma((2, 2, 4)),
        dma((2, 2, 4)),
        dma((2, 4)),
        dma((2, 4)),
    ]
    grid = pl.pallas_call(
        kernel,
        out_shape=jax.ShapeDtypeStruct((4, 2, 80, LANES), F32),
        in_specs=[vmem, vmem, hbm, hbm, pl.BlockSpec(memory_space=pltpu.SMEM)] + [hbm] * 4,
        out_specs=vmem,
        scratch_shapes=scratch,
        compiler_params=pltpu.CompilerParams(
            collective_id=0, has_side_effects=True, vmem_limit_bytes=62 * 1024 * 1024
        ),
    )(
        jnp.transpose(field, (0, 2, 3, 1)),
        jnp.transpose(depart, (2, 0, 1)),
        jnp.transpose(interp_weight, (0, 2, 3, 4, 1)),
        legendre,
        damping,
        *constants,
    )
    grid = grid.reshape(2, 2, 160, LANES)[..., 0:LAT]
    return jnp.transpose(grid, (0, 3, 1, 2))


def solution(mesh):
    placed = (
        P(None, "band", None, "sector"),
        P(None, "band", "sector"),
        P(None, "band", "sector", None, None),
        P("sector", "band", None),
        P(),
    )
    return jax.shard_map(
        local, mesh=mesh, in_specs=placed, out_specs=P(None, "band", None, "sector"), check_vma=False
    )
```
